32 devices in a mesh: dp: 8 (over y, x, core), tensor: 4 (over z).
Axes of the slice: x: 2, y: 2, z: 4, core: 2. Of those that a mesh axis runs over, the one named last changes fastest.
Arguments:
- tokens: bfloat16 [8192, 2048], P('dp'), may hold values from -6 to 6
- project_weight: float32 [2048, 6144], P('dp', 'tensor'), may hold values from -0.125 to 0.125
- project_bias: float32 [8, 768], P('tensor', 'dp'), may hold values from -1.2 to 1.2
- dense_weight: float32 [2048, 2048], P('tensor', 'dp'), may hold values from -2 to 2
- dense_bias: float32 [2048], P('dp'), may hold values from -1.2 to 1.2
- expand_weight: float32 [2048, 8192], P('dp', 'tensor'), may hold values from -0.125 to 0.125
- expand_bias: float32 [8, 1024], P('tensor', 'dp'), may hold values from -1.2 to 1.2
- shrink_weight: float32 [8192, 2048], P('tensor', 'dp'), may hold values from -0.0625 to 0.0625
- shrink_bias: float32 [2048], P('dp'), may hold values from -1.2 to 1.2
- first_gain: float32 [2048], P('dp'), may hold values from 0.5 to 1.5
- first_shift: float32 [2048], P('dp'), may hold values from -1.2 to 1.2
- second_gain: float32 [2048], P('dp'), may hold values from 0.5 to 1.5
- second_shift: float32 [2048], P('dp'), may hold values from -1.2 to 1.2
- lengths: int32 [24], replicated, may hold values from 0 to 1024, as said below
- prefix: int32 [24], replicated, may hold values from 102 to 512
- upstream: bfloat16 [8192, 2048], P('dp'), may hold values from -6 to 6
Outputs:
- output: bfloat16 [8192, 2048], P('dp')
- tokens_grad: bfloat16 [8192, 2048], P('dp')
- project_weight_grad: float32 [2048, 6144], P('dp', 'tensor')
- project_bias_grad: float32 [8, 768], P('tensor', 'dp')
- dense_weight_grad: float32 [2048, 2048], P('tensor', 'dp')
- dense_bias_grad: float32 [2048], P('dp')
- expand_weight_grad: float32 [2048, 8192], P('dp', 'tensor')
- expand_bias_grad: float32 [8, 1024], P('tensor', 'dp')
- shrink_weight_grad: float32 [8192, 2048], P('tensor', 'dp')
- shrink_bias_grad: float32 [2048], P('dp')
- first_gain_grad: float32 [2048], P('dp')
- first_shift_grad: float32 [2048], P('dp')
- second_gain_grad: float32 [2048], P('dp')
- second_shift_grad: float32 [2048], P('dp')
The draws below stay inside these ranges and needn't reach their ends.
Inputs may be any that keep to these rules, and one draw needn't show every extreme that they name: `lengths`: sequences lie end to end in order and fill all 8192 rows; some slots are empty (length 0); the longest has exactly 1024 tokens; every boundary between blocks of 1024 rows lies inside a sequence.
All inputs are finite; a program needn't handle non-finite values.
Results may differ from the reference program's by a relative error of at most 0.025.
Values may be sent and summed in bfloat16 or wider, within the bound.
No kernel may reach another device: no remote copies, remote signals or barrier semaphores. Data moves between devices by JAX's collectives and lax.ppermute only.
A program may use at most 256 MiB of HBM per device.

```python
import math
import jax
import jax.numpy as jnp
from jax import lax

D = 2048
HEADS = 8
HD = 256
FF = 8192
ROT = 64
TOK_DEV = 1024
SEQ_MAX = 1024
TOKENS = 8192
N_DP = 8


def packing(key):
    shards = TOKENS // TOK_DEV
    slots = TOK_DEV // SEQ_MAX + 1
    key_below, key_above, key_choose, key_fill, key_cross = jax.random.split(key, 5)
    below_rows = jax.random.randint(key_below, (shards,), SEQ_MAX // 8, SEQ_MAX // 4 + 1)
    above_rows = jax.random.randint(key_above, (shards,), SEQ_MAX // 2, SEQ_MAX - SEQ_MAX // 4 + 1)
    chosen = jax.random.randint(key_choose, (), 0, shards - 1)
    shard_ids = jnp.arange(shards, dtype=jnp.int32)
    picked = shard_ids == chosen
    below_rows = jnp.where(picked, SEQ_MAX // 4, below_rows)
    above_rows = jnp.where(picked, SEQ_MAX - SEQ_MAX // 4, above_rows)
    final = shard_ids == shards - 1
    below_rows = jnp.where(final, 0, below_rows).astype(jnp.int32)
    above_rows = jnp.where(final, 0, above_rows).astype(jnp.int32)
    entering = jnp.concatenate([jnp.zeros((1,), jnp.int32), above_rows[:-1]])
    free_rows = TOK_DEV - entering - below_rows
    pieces = jnp.maximum((free_rows + SEQ_MAX - 1) // SEQ_MAX, 1)
    slot_ids = jnp.arange(slots, dtype=jnp.int32)[None, :]
    fill = free_rows[:, None] * (slot_ids + 1) // pieces[:, None] - free_rows[:, None] * slot_ids // pieces[:, None]
    fill = jnp.where(slot_ids < pieces[:, None], fill, 0).astype(jnp.int32)
    crossing = (below_rows + above_rows).astype(jnp.int32)
    lengths = jnp.concatenate([fill, crossing[:, None]], axis=1).reshape(-1)
    fill_prefix = jax.random.randint(key_fill, (shards, slots), SEQ_MAX // 10, SEQ_MAX // 2 + 1)
    cross_prefix = jax.random.randint(key_cross, (shards,), below_rows + SEQ_MAX // 8, SEQ_MAX // 2 + 1)
    cross_prefix = jnp.where(picked, SEQ_MAX // 2, cross_prefix)
    prefix = jnp.concatenate([fill_prefix, cross_prefix[:, None]], axis=1).reshape(-1)
    return (lengths.astype(jnp.int32), prefix.astype(jnp.int32))


def draw_lengths(key, part):
    return packing(key)[0]


def draw_prefix(key, part):
    return packing(key)[1]


def with_spikes(drawn, key, source, target, parts, factor):
    def block_of(position):
        return (jnp.arange(drawn.shape[position]) // (drawn.shape[position] // parts)).reshape((-1,) + (1,) * (drawn.ndim - 1 - position))

    near = jax.random.permutation(key, parts)[block_of(target)]
    second = (block_of(target) + parts // 2) % parts
    return jnp.where((block_of(source) == near) | (block_of(source) == second), factor * drawn, drawn)


def level_of(key, dims, cuts, smallest, high):
    def one(axis_at, shards_of):
        draws = jax.random.uniform(jax.random.fold_in(jax.random.fold_in(key, 6), axis_at), (shards_of,), jnp.float32, smallest / len(cuts), high / len(cuts))
        return jnp.repeat(jnp.exp(draws), dims[axis_at] // shards_of).reshape((-1,) + (1,) * (len(dims) - axis_at - 1))

    level = one(*cuts[0])
    for cut in cuts[1:]:
        level = level * one(*cut)
    return level


def bell_draw(key, extent, deviation, bound, cuts=(), kind=jnp.bfloat16):
    values = deviation * jax.random.normal(key, extent, jnp.float32)
    if cuts:
        values = values * level_of(key, extent, cuts, -0.22, 0.18)
    return jnp.clip(values, -bound, bound).astype(kind)


def bell_draw_with(key, dims, width, limit, cuts, heavy, kind=jnp.bfloat16):
    values = width * jax.random.normal(key, dims, jnp.float32)
    if cuts:
        values = values * level_of(key, dims, cuts, -0.22, 0.18)
    return jnp.clip(with_spikes(values, jax.random.fold_in(key, 3), *heavy), -limit, limit).astype(kind)


def setup_inputs(seed: int = 0) -> dict:
    splits = jax.random.split(jax.random.key(seed), 17)
    return {
        "tokens": bell_draw(splits[0], (TOKENS, D), 1.0, 6.0, ((0, 8),)),
        "project_weight": bell_draw(splits[1], (D, 3 * D), D ** -0.5, 0.125, ((0, 8), (1, 4)), jnp.float32),
        "project_bias": bell_draw(splits[2], (HEADS, 3 * HD), 0.2, 1.2, ((0, 4), (1, 8)), jnp.float32),
        "dense_weight": bell_draw(splits[3], (D, D), (max(D // 256, 2)) ** -0.5, 2.0, ((0, 4), (1, 8)), jnp.float32),
        "dense_bias": bell_draw(splits[4], (D,), 0.2, 1.2, ((0, 8),), jnp.float32),
        "expand_weight": bell_draw(splits[5], (D, FF), D ** -0.5, 0.125, ((0, 8), (1, 4)), jnp.float32),
        "expand_bias": bell_draw(splits[6], (HEADS, FF // HEADS), 0.2, 1.2, ((0, 4), (1, 8)), jnp.float32),
        "shrink_weight": bell_draw(splits[7], (FF, D), FF ** -0.5, 0.0625, ((0, 4), (1, 8)), jnp.float32),
        "shrink_bias": bell_draw(splits[8], (D,), 0.2, 1.2, ((0, 8),), jnp.float32),
        "first_gain": jnp.clip(1.0 + 0.1 * jax.random.normal(splits[9], (D,), jnp.float32), 0.5, 1.5),
        "first_shift": bell_draw(splits[10], (D,), 0.2, 1.2, ((0, 8),), jnp.float32),
        "second_gain": jnp.clip(1.0 + 0.1 * jax.random.normal(splits[11], (D,), jnp.float32), 0.5, 1.5),
        "second_shift": bell_draw(splits[12], (D,), 0.2, 1.2, ((0, 8),), jnp.float32),
        "lengths": draw_lengths(jax.random.fold_in(splits[16], 71), 0),
        "prefix": draw_prefix(jax.random.fold_in(splits[16], 71), 0),
        "upstream": bell_draw_with(splits[15], (TOKENS, D), 1.0, 6.0, ((0, 8),), (0, 1, 8, 2.0)),
    }


@jax.custom_vjp
def low(v):
    return lax.optimization_barrier(v.astype(jnp.bfloat16)).astype(jnp.float32)

@jax.custom_vjp
def low_back(v):
    return v

def low_keep(v):
    return (low(v), None)

def low_pass(kept, grad):
    return (grad,)

def back_keep(v):
    return (v, None)

def back_low(kept, grad):
    return (low(grad),)
low.defvjp(low_keep, low_pass)
low_back.defvjp(back_keep, back_low)
EPSILON = 1e-05
MASKED = -1e+30
HIGHEST = lax.Precision.HIGHEST

def normalize(values, gain, shift):
    center = values - lax.optimization_barrier(jnp.mean(values, axis=1, keepdims=True))
    spread = lax.optimization_barrier(jnp.mean(center * center, axis=1, keepdims=True))
    return center * lax.rsqrt(spread + EPSILON) * gain + shift

def rotary(values, places):
    half_rot = ROT // 2
    exponents = jnp.arange(half_rot).astype(jnp.float32) * (2.0 / ROT)
    frequency = jnp.exp(exponents * -math.log(10000.0))
    angles = places[:, None] * frequency[None, :]
    cosine = jnp.cos(angles)[:, None, :]
    sines = jnp.sin(angles)[:, None, :]
    leading = values[:, :, :half_rot]
    trailing = values[:, :, half_rot:ROT]
    return jnp.concatenate([leading * cosine - trailing * sines, trailing * cosine + leading * sines, values[:, :, ROT:]], axis=2)

def locate(token_index, lengths, prefix, total_rows):
    seq_count = lengths.shape[0]
    starts = (jnp.cumsum(lengths) - lengths).astype(jnp.int32)
    inside = (token_index >= 0) & (token_index < total_rows)
    member = lax.optimization_barrier(jnp.sum((starts[None, :] <= token_index[:, None]).astype(jnp.int32), axis=1)).astype(jnp.int32) - 1
    member = jnp.where(inside, member, -1)
    onehot = jnp.arange(seq_count, dtype=jnp.int32)[None, :] == member[:, None]
    seq_begin = lax.optimization_barrier(jnp.sum(jnp.where(onehot, starts[None, :], 0), axis=1)).astype(jnp.int32)
    limits = lax.optimization_barrier(jnp.sum(jnp.where(onehot, jnp.minimum(prefix, lengths)[None, :], 0), axis=1)).astype(jnp.int32)
    return (member, token_index - seq_begin, limits)

def visible(query_index, key_index, lengths, prefix, total_rows):
    query_member, unused_place, query_limit = locate(query_index, lengths, prefix, total_rows)
    key_member, key_place, unused_limit = locate(key_index, lengths, prefix, total_rows)
    same_seq = (query_member[:, None] == key_member[None, :]) & (key_member[None, :] >= 0)
    earlier = key_index[None, :] <= query_index[:, None]
    opened = key_place[None, :] < query_limit[:, None]
    return same_seq & (earlier | opened)

def attend(queries, key_rows, value_rows, lengths, prefix):
    scale = HD ** (-0.5)
    padding = jnp.zeros((SEQ_MAX, HEADS, HD), jnp.float32)
    key_padded = jnp.concatenate([padding, key_rows, padding], axis=0)
    value_padded = jnp.concatenate([padding, value_rows, padding], axis=0)
    window = TOK_DEV + 2 * SEQ_MAX
    query_blocks = queries.reshape(N_DP, TOK_DEV, HEADS, HD)

    @jax.checkpoint
    def one_block(inputs):
        query_block, block_index = inputs
        block_start = (block_index * TOK_DEV).astype(jnp.int32)
        key_block = lax.dynamic_slice_in_dim(key_padded, block_start, window, 0)
        value_block = lax.dynamic_slice_in_dim(value_padded, block_start, window, 0)
        query_index = block_start + jnp.arange(TOK_DEV, dtype=jnp.int32)
        key_index = block_start - SEQ_MAX + jnp.arange(window, dtype=jnp.int32)
        allowed = visible(query_index, key_index, lengths, prefix, TOKENS)
        scores = low_back(jnp.einsum('qhd,khd->hqk', query_block, key_block, precision=HIGHEST) * scale)
        scores = jnp.where(allowed[None], scores, MASKED)
        largest = lax.optimization_barrier(jnp.max(scores, axis=2, keepdims=True))
        weights = jnp.exp(scores - largest)
        probs = weights / lax.optimization_barrier(jnp.sum(weights, axis=2, keepdims=True))
        return jnp.einsum('hqk,khd->qhd', low(probs), value_block, precision=HIGHEST)
    blocks = lax.map(one_block, (query_blocks, jnp.arange(N_DP, dtype=jnp.int32)))
    return blocks.reshape(TOKENS, HEADS * HD)

def layer(tokens, params, lengths, prefix):
    project_weight, project_bias, dense_weight, dense_bias, expand_weight, expand_bias, shrink_weight, shrink_bias, first_gain, first_shift, second_gain, second_shift = jax.tree.map(low, params)
    first_normed = low(normalize(tokens, first_gain, first_shift))
    second_normed = low(normalize(tokens, second_gain, second_shift))
    mixed_rows = low_back(jnp.dot(first_normed, project_weight, precision=HIGHEST) + project_bias.reshape(-1))
    mixed_rows = mixed_rows.reshape(TOKENS, HEADS, 3, HD)
    token_index = jnp.arange(TOKENS, dtype=jnp.int32)
    unused_member, places, unused_limit = locate(token_index, lengths, prefix, TOKENS)
    places = places.astype(jnp.float32)
    queries = low(rotary(mixed_rows[:, :, 0], places))
    key_rows = low(rotary(mixed_rows[:, :, 1], places))
    value_rows = low(mixed_rows[:, :, 2])
    attended = low(low_back(attend(queries, key_rows, value_rows, lengths, prefix)))
    hidden = low_back(jnp.dot(second_normed, expand_weight, precision=HIGHEST) + expand_bias.reshape(-1))
    active = low(jax.nn.gelu(hidden, approximate=False))
    branch = jnp.dot(attended, dense_weight, precision=HIGHEST) + jnp.dot(active, shrink_weight, precision=HIGHEST)
    return tokens + branch + dense_bias + shrink_bias

def reference(tokens, project_weight, project_bias, dense_weight, dense_bias, expand_weight, expand_bias, shrink_weight, shrink_bias, first_gain, first_shift, second_gain, second_shift, lengths, prefix, upstream):
    params = (project_weight, project_bias, dense_weight, dense_bias, expand_weight, expand_bias, shrink_weight, shrink_bias, first_gain, first_shift, second_gain, second_shift)

    def forward(inputs, weights):
        return layer(inputs, weights, lengths, prefix)
    result, pullback = jax.vjp(forward, tokens.astype(jnp.float32), params)
    tokens_grad, grads = pullback(upstream.astype(jnp.float32))
    return (result.astype(jnp.bfloat16), tokens_grad.astype(jnp.bfloat16), grads[0], grads[1], grads[2], grads[3], grads[4], grads[5], grads[6], grads[7], grads[8], grads[9], grads[10], grads[11])
```

```python
import functools
import math

import jax
import jax.numpy as jnp
from jax import lax
from jax.experimental import pallas as pl
from jax.experimental.pallas import tpu as pltpu
from jax.sharding import PartitionSpec as P

HD = 256
ROT = 64
SEQ_MAX = 1024
PREFIX_MAX = 512
BLOCK = 256
BLOCKS = 8
HALF = 4
EPSILON = 1e-05
MASKED = -1e30
bf16 = jnp.bfloat16
f32 = jnp.float32
NN = (((1,), (0,)), ((), ()))
NT = (((1,), (1,)), ((), ()))
TN = (((0,), (0,)), ((), ()))
VMEM_BYTES = 56 * 2**20


def mul(a, b, dims=NN):
    return lax.dot_general(a, b, dims, preferred_element_type=f32)


def params(**more):
    return pltpu.CompilerParams(vmem_limit_bytes=VMEM_BYTES, **more)


def cost(flops, moved, transcendentals=0):
    return pl.CostEstimate(flops=flops, bytes_accessed=moved, transcendentals=transcendentals)


def whole_spec(array):
    zeros = (0,) * array.ndim
    return pl.BlockSpec(array.shape, lambda *_: zeros)


def swap(value, bit):
    count = lax.axis_size("dp")
    return lax.ppermute(value, "dp", [(i, i ^ bit) for i in range(count)])


CORE, ALONG_X, ALONG_Y = 1, 2, 4


def is_cube():
    return lax.axis_size("dp") == BLOCKS


def natural_places():
    place = jnp.arange(BLOCKS, dtype=jnp.int32)
    if not is_cube():
        return place
    owner = ((place >> 2) & 1) * CORE + ((place >> 1) & 1) * ALONG_Y + (place & 1) * ALONG_X
    return owner ^ lax.axis_index("dp")


class Spread:
    def __init__(self, weight):
        self.weight = weight

    def first(self):
        if is_cube():
            self.from_x = swap(self.weight, ALONG_X)
            self.from_y = swap(self.weight, ALONG_Y)
            return self.from_x, self.from_y
        self.full = lax.all_gather(self.weight, "dp", axis=0, tiled=True)
        return (self.full,)

    def second(self, *seen):
        if is_cube():
            half = self.weight.shape[0] // 2
            self.over_x = swap(after(self.from_x[:half], seen), ALONG_Y)
            self.over_y = swap(after(self.from_y[half:], seen), ALONG_X)
            return self.over_x, self.over_y
        return (self.full,)

    def join(self, *seen):
        if is_cube():
            parts = [self.weight, self.from_x, self.from_y, self.over_x, self.over_y]
            mine = jnp.concatenate(after(parts, seen), axis=0)
            return mine, swap(mine, CORE)
        half = self.full.shape[0] // 2
        return self.full[:half], self.full[half:]


def gather_columns(weight):
    if is_cube():
        return lax.all_gather(weight, "dp", axis=0)
    full = lax.all_gather(weight, "dp", axis=1, tiled=True)
    return full.reshape(full.shape[0], BLOCKS, -1).transpose(1, 0, 2)


def after(value, seen):
    return lax.optimization_barrier((value, seen))[0]


def norm_kernel(places, tokens, upstream, gains, tok, one_a, one_b, two_a, two_b, up_a, up_b, mean, inverse, grad_bias):
    values = tokens[...].astype(f32)
    average = jnp.mean(values, axis=1, keepdims=True)
    center = values - average
    scale = lax.rsqrt(jnp.mean(center * center, axis=1, keepdims=True) + EPSILON)
    mean[...] = average
    inverse[...] = scale

    @pl.when(pl.program_id(0) == 0)
    def _():
        grad_bias[...] = jnp.zeros_like(grad_bias)

    for place in range(BLOCKS):
        from_ = pl.ds(pl.multiple_of(places[place] * BLOCK, BLOCK), BLOCK)
        to = pl.ds(place * BLOCK, BLOCK)
        inner = pl.ds(place % HALF * BLOCK, BLOCK)
        first, second, up = (one_a, two_a, up_a) if place < HALF else (one_b, two_b, up_b)
        low = tokens[:, from_]
        tok[:, to] = low
        normed = (low.astype(f32) - average) * scale
        first[:, inner] = (normed * gains[0:1, to] + gains[1:2, to]).astype(bf16)
        second[:, inner] = (normed * gains[2:3, to] + gains[3:4, to]).astype(bf16)
        grad = upstream[:, from_]
        up[:, inner] = grad
        grad_bias[0:1, to] += jnp.sum(grad.astype(f32), axis=0, keepdims=True)


def norm(places, tokens, upstream, gains, tile=256):
    rows, width = tokens.shape
    row = lambda w: pl.BlockSpec((tile, w), lambda i, *_: (i, 0))
    shape = lambda w, kind: jax.ShapeDtypeStruct((rows, w), kind)
    half = width // 2
    return pl.pallas_call(
        norm_kernel,
        grid_spec=pltpu.PrefetchScalarGridSpec(
            num_scalar_prefetch=1,
            grid=(rows // tile,),
            in_specs=[row(width), row(width), whole_spec(gains)],
            out_specs=[row(width)] + [row(half)] * 6 + [row(1), row(1), pl.BlockSpec((8, width), lambda *_: (0, 0))],
        ),
        out_shape=[shape(width, bf16)]
        + [shape(half, bf16)] * 6
        + [shape(1, f32), shape(1, f32), jax.ShapeDtypeStruct((8, width), f32)],
        compiler_params=params(),
        cost_estimate=cost(20 * rows * width, 20 * rows * width),
        name="norm",
    )(places, tokens, upstream, gains)


def turn(part, cos, sin, sign):
    lane = lax.broadcasted_iota(jnp.int32, part.shape, 1)
    partner = jnp.where(lane < ROT // 2, pltpu.roll(part, 128 - ROT // 2, 1), pltpu.roll(part, ROT // 2, 1))
    if sign > 0:
        return part * cos + partner * sin
    return part * cos - partner * sin


def project_kernel(one_a, one_b, w_a, w_b, bias, cos, sin, queries, pairs):
    for part in range(3):
        at = slice(part * HD, (part + 1) * HD)
        mixed = mul(one_a[...], w_a[:, at]) + mul(one_b[...], w_b[:, at]) + bias[:, at]
        if part < 2:
            ref, to = (queries, 0) if part == 0 else (pairs, 0)
            ref[:, to : to + 128] = turn(mixed[:, :128], cos[...], sin[...], 1).astype(bf16)
            ref[:, to + 128 : to + HD] = mixed[:, 128:].astype(bf16)
        else:
            pairs[:, HD:] = mixed.astype(bf16)


def project(one_a, one_b, w_a, w_b, bias, cos, sin):
    rows, half = one_a.shape
    heads = w_a.shape[1] // (3 * HD)
    weight = pl.BlockSpec((half, 3 * HD), lambda h: (0, h))
    return pl.pallas_call(
        project_kernel,
        grid=(heads,),
        in_specs=[
            whole_spec(one_a),
            whole_spec(one_b),
            weight,
            weight,
            pl.BlockSpec((1, 3 * HD), lambda h: (0, h)),
            whole_spec(cos),
            whole_spec(sin),
        ],
        out_specs=[pl.BlockSpec((rows, HD), lambda h: (0, h)), pl.BlockSpec((rows, 2 * HD), lambda h: (0, h))],
        out_shape=[
            jax.ShapeDtypeStruct((rows, heads * HD), bf16),
            jax.ShapeDtypeStruct((rows, heads * 2 * HD), bf16),
        ],
        compiler_params=params(),
        cost_estimate=cost(4 * rows * half * w_a.shape[1], 14_000_000),
        name="project",
    )(one_a, one_b, w_a, w_b, bias, cos, sin)


def expand_kernel(two_a, two_b, w_a, w_b, bias, active, slope):
    rows = two_a.shape[0]
    for start in range(0, rows, 512):
        at = slice(start, start + 512)
        hidden = mul(two_a[at], w_a[...]) + mul(two_b[at], w_b[...]) + bias[...]
        below = 0.5 + 0.5 * lax.erf(hidden * (0.5**0.5))
        density = jnp.exp(hidden * hidden * -0.5) * (1.0 / math.sqrt(2.0 * math.pi))
        active[at] = (hidden * below).astype(bf16)
        slope[at] = (below + hidden * density).astype(bf16)


def expand(two_a, two_b, w_a, w_b, bias, tile=512):
    rows, half = two_a.shape
    width = w_a.shape[1]
    column = lambda r: pl.BlockSpec((r, tile), lambda n: (0, n))
    return pl.pallas_call(
        expand_kernel,
        grid=(width // tile,),
        in_specs=[whole_spec(two_a), whole_spec(two_b), column(half), column(half), column(1)],
        out_specs=[column(rows), column(rows)],
        out_shape=[jax.ShapeDtypeStruct((rows, width), bf16)] * 2,
        compiler_params=params(),
        cost_estimate=cost(4 * rows * half * width, 22_000_000, 2 * rows * width),
        name="expand",
    )(two_a, two_b, w_a, w_b, bias)


def branch_kernel(attended, active, mine, theirs, out):
    depth = attended.shape[1]
    slabs = BLOCK // 128
    for number, weight in enumerate((mine, theirs)):
        full = (mul(attended[...], weight[:depth]) + mul(active[...], weight[depth:])).astype(bf16)
        for slab in range(slabs):
            out[number * slabs + slab] = full[:, slab * 128 : (slab + 1) * 128]


def branch_piece(attended, active, mine, theirs, tile=512):
    rows = attended.shape[0]
    depth = mine.shape[0]
    slabs = 2 * BLOCK // 128
    row = lambda a: pl.BlockSpec((tile, a.shape[1]), lambda i: (i, 0))
    return pl.pallas_call(
        branch_kernel,
        grid=(rows // tile,),
        in_specs=[row(attended), row(active), whole_spec(mine), whole_spec(theirs)],
        out_specs=pl.BlockSpec((slabs, tile, 128), lambda i: (0, i, 0)),
        out_shape=jax.ShapeDtypeStruct((slabs, rows, 128), bf16),
        compiler_params=params(),
        cost_estimate=cost(4 * rows * depth * BLOCK, 2 * (rows * depth + 2 * (rows + depth) * BLOCK)),
        name="branch",
    )(attended, active, mine, theirs)


def branch_place(places, attended, active, weight, place, tile=512):
    rows = attended.shape[0]
    depth = weight.shape[1]
    slabs = 2 * BLOCK // 128
    row = lambda a: pl.BlockSpec((tile, a.shape[1]), lambda i, *_: (i, 0))
    block = lambda p: pl.BlockSpec((None, depth, BLOCK), lambda i, w: (w[p], 0, 0))
    return pl.pallas_call(
        lambda _, *refs: branch_kernel(*refs),
        grid_spec=pltpu.PrefetchScalarGridSpec(
            num_scalar_prefetch=1,
            grid=(rows // tile,),
            in_specs=[row(attended), row(active), block(place), block(place + HALF)],
            out_specs=pl.BlockSpec((slabs, tile, 128), lambda i, *_: (0, i, 0)),
        ),
        out_shape=jax.ShapeDtypeStruct((slabs, rows, 128), bf16),
        compiler_params=params(),
        cost_estimate=cost(4 * rows * depth * BLOCK, 2 * (rows * depth + 2 * (rows + depth) * BLOCK)),
        name="branch",
    )(places, attended, active, weight, weight)


def back_kernel(places, up_a, up_b, blocks, slope, out, sums, joined):
    for place in range(BLOCKS):
        joined[:, place * BLOCK : (place + 1) * BLOCK] = blocks[places[place]]
    half = HALF * BLOCK
    total = jnp.zeros((1, out.shape[1]), f32)
    for start in range(0, out.shape[0], 512):
        at = slice(start, start + 512)
        grad = mul(up_a[at], joined[:, :half], NT) + mul(up_b[at], joined[:, half:], NT)
        if slope is not None:
            grad = grad * slope[at].astype(f32)
        grad = grad.astype(bf16)
        out[at] = grad
        if sums is not None:
            total = total + jnp.sum(grad.astype(f32), axis=0, keepdims=True)
    if sums is not None:
        sums[...] = total


def back(places, up_a, up_b, blocks, start, width, slope=None, tile=512):
    rows, half = up_a.shape
    weight = pl.BlockSpec((BLOCKS, tile, BLOCK), lambda n, *_: (0, n + start // tile, 0))
    column = lambda r: pl.BlockSpec((r, tile), lambda n, *_: (0, n))
    scaled = slope is not None

    def body(w, a, b, c, *rest):
        if scaled:
            s, out, sums, joined = rest
        else:
            (out, joined), s, sums = rest, None, None
        back_kernel(w, a, b, c, s, out, sums, joined)

    out = jax.ShapeDtypeStruct((rows, width), bf16)
    return pl.pallas_call(
        body,
        grid_spec=pltpu.PrefetchScalarGridSpec(
            num_scalar_prefetch=1,
            grid=(width // tile,),
            in_specs=[whole_spec(up_a), whole_spec(up_b), weight] + [column(rows)] * scaled,
            out_specs=[column(rows), column(1)] if scaled else column(rows),
            scratch_shapes=[pltpu.VMEM((tile, 2 * half), bf16)],
        ),
        out_shape=[out, jax.ShapeDtypeStruct((1, width), f32)] if scaled else out,
        compiler_params=params(),
        cost_estimate=cost(4 * rows * half * width, 4 * rows * half + 4 * half * width + 4 * rows * width),
        name="back",
    )(places, up_a, up_b, blocks, *([slope] if scaled else []))


def second_kernel(grad, w_a, w_b, out):
    step = pl.program_id(0)

    @pl.when(step < 2)
    def _():
        out[...] = mul(grad[...], w_a[...], NT).astype(bf16)

    @pl.when(step >= 2)
    def _():
        out[...] = mul(grad[...], w_b[...], NT).astype(bf16)


def second_back(grad, w_a, w_b):
    rows, width = grad.shape
    half = w_a.shape[0]
    tile = half // 2
    return pl.pallas_call(
        second_kernel,
        grid=(4,),
        in_specs=[
            whole_spec(grad),
            pl.BlockSpec((tile, width), lambda n: (jnp.minimum(n, 1), 0)),
            pl.BlockSpec((tile, width), lambda n: (jnp.maximum(n - 2, 0), 0)),
        ],
        out_specs=pl.BlockSpec((rows, tile), lambda n: (0, n)),
        out_shape=jax.ShapeDtypeStruct((rows, 2 * half), bf16),
        compiler_params=params(),
        cost_estimate=cost(4 * rows * half * width, 2 * rows * width + 4 * half * width + 4 * rows * half),
        name="second_back",
    )(grad, w_a, w_b)


def row_grad_kernel(where, left_a, left_b, right, *rest):
    out = rest[-1]
    for number, left in enumerate((left_a, left_b)):
        full = mul(left[...], right[...], TN)
        for place in range(HALF):
            out[where[number * HALF + place]] = full[place * BLOCK : (place + 1) * BLOCK].astype(bf16)


def row_grad(where, left_a, left_b, right, total, start=0, into=None, tile=512):
    rows, width = right.shape
    blocks = 2 * HALF
    extra = [] if into is None else [into]
    return pl.pallas_call(
        row_grad_kernel,
        grid_spec=pltpu.PrefetchScalarGridSpec(
            num_scalar_prefetch=1,
            grid=(width // tile,),
            in_specs=[whole_spec(left_a), whole_spec(left_b), pl.BlockSpec((rows, tile), lambda n, *_: (0, n))]
            + [pl.BlockSpec(memory_space=pl.ANY)] * len(extra),
            out_specs=pl.BlockSpec((blocks, BLOCK, tile), lambda n, *_: (0, 0, n + start // tile)),
        ),
        out_shape=jax.ShapeDtypeStruct((blocks, BLOCK, total), bf16),
        input_output_aliases={4: 0} if extra else {},
        compiler_params=params(),
        cost_estimate=cost(2 * rows * blocks * BLOCK * width, 2 * blocks * BLOCK * (rows + width) + 2 * rows * width),
        name="row_grad",
    )(where, left_a, left_b, right, *extra)


def column_grad_kernel(where, first, second, right_a, right_b, out):
    def store(left):
        for number, right in enumerate((right_a, right_b)):
            full = mul(left[...], right[...], TN)
            for place in range(HALF):
                out[where[number * HALF + place]] = full[:, place * BLOCK : (place + 1) * BLOCK].astype(bf16)

    ahead = first.shape[1] // out.shape[1]
    assert ahead == 1
    pl.when(pl.program_id(0) == 0)(lambda: store(first))
    pl.when(pl.program_id(0) > 0)(lambda: store(second))


def column_grad(where, first, second, right_a, right_b, tile=512):
    rows = first.shape[0]
    width = first.shape[1] + second.shape[1]
    blocks = 2 * HALF
    return pl.pallas_call(
        column_grad_kernel,
        grid_spec=pltpu.PrefetchScalarGridSpec(
            num_scalar_prefetch=1,
            grid=(width // tile,),
            in_specs=[
                pl.BlockSpec((rows, tile), lambda n, *_: (0, 0)),
                pl.BlockSpec((rows, tile), lambda n, *_: (0, jnp.maximum(n - 1, 0))),
                whole_spec(right_a),
                whole_spec(right_b),
            ],
            out_specs=pl.BlockSpec((blocks, tile, BLOCK), lambda n, *_: (0, n, 0)),
        ),
        out_shape=jax.ShapeDtypeStruct((blocks, width, BLOCK), bf16),
        compiler_params=params(),
        cost_estimate=cost(2 * rows * blocks * BLOCK * width, 2 * blocks * BLOCK * (rows + width) + 2 * rows * width),
        name="column_grad",
    )(where, first, second, right_a, right_b)


def attend_kernel(first, last, q, left, own, right, low, high, out, lse, keys, values_turned, *, wide):
    step = pl.program_id(1)
    tall = q.shape[0]

    @pl.when(step == 0)
    def _():
        at = 0
        for ref in (left, own, right):
            count = ref.shape[0]
            keys[at : at + count, :] = ref[:, :HD]
            for r in range(0, count, 512):
                values_turned[:, at + r : at + r + 512] = jnp.transpose(ref[r : r + 512, HD:])
            at += count

    scaled = q[...] * jnp.asarray(HD**-0.5, bf16)
    low_row = low[...]
    high_row = high[...]

    def block(j, carry):
        top, total, acc = carry
        rows = pl.ds(pl.multiple_of(j * wide, wide), wide)
        scores = mul(keys[rows, :], scaled, NT)
        key = j * wide + lax.broadcasted_iota(jnp.int32, (wide, tall), 0)
        scores = jnp.where((key >= low_row) & (key <= high_row), scores, MASKED)
        new = jnp.maximum(top, jnp.max(scores, axis=0, keepdims=True))
        weights = jnp.exp(scores - new)
        fade = jnp.exp(top - new)
        total = total * fade + jnp.sum(weights, axis=0, keepdims=True)
        acc = acc * fade + mul(values_turned[:, rows], weights.astype(bf16))
        return new, total, acc

    start = (jnp.full((1, tall), MASKED, f32), jnp.zeros((1, tall), f32), jnp.zeros((HD, tall), f32))
    top, total, acc = lax.fori_loop(first[step], last[step] + 1, block, start)
    out[...] = jnp.transpose(acc / total).astype(bf16)
    lse[0] = top + jnp.log(total)


def key_blocks(low, high, tall, wide):
    return jnp.min(low.reshape(-1, tall), axis=1) // wide, jnp.max(high.reshape(-1, tall), axis=1) // wide


def attend(q, left, own, right, low, high, tall=512, wide=512):
    rows, width = q.shape
    heads = width // HD
    extent = left.shape[0] + rows + right.shape[0]
    pair = lambda a: pl.BlockSpec((a.shape[0], 2 * HD), lambda h, i, *_: (0, h))
    row = pl.BlockSpec((1, tall), lambda h, i, *_: (0, i))
    mine = pl.BlockSpec((tall, HD), lambda h, i, *_: (i, h))
    return pl.pallas_call(
        functools.partial(attend_kernel, wide=wide),
        grid_spec=pltpu.PrefetchScalarGridSpec(
            num_scalar_prefetch=2,
            grid=(heads, rows // tall),
            in_specs=[mine, pair(left), pair(own), pair(right), row, row],
            out_specs=[mine, pl.BlockSpec((1, 1, tall), lambda h, i, *_: (h, 0, i))],
            scratch_shapes=[pltpu.VMEM((extent, HD), bf16), pltpu.VMEM((HD, extent), bf16)],
        ),
        out_shape=[jax.ShapeDtypeStruct((rows, width), bf16), jax.ShapeDtypeStruct((heads, 1, rows), f32)],
        compiler_params=params(),
        cost_estimate=cost(8_000_000_000, 10_000_000, 3_000_000),
        name="attend",
    )(*key_blocks(low, high, tall, wide), q, left, own, right, low.reshape(1, rows), high.reshape(1, rows))


def attend_back_kernel(
    first, last, q, left, own, right, low, high, lse, attended, grad, cos, sin,
    dq, dleft, down, dright, keys, values, keys_turned, dk, dv, *, wide,
):
    step = pl.program_id(1)
    tall = q.shape[0]

    @pl.when(step == 0)
    def _():
        at = 0
        for ref in (left, own, right):
            count = ref.shape[0]
            keys[at : at + count, :] = ref[:, :HD]
            values[at : at + count, :] = ref[:, HD:]
            for r in range(0, count, 512):
                keys_turned[:, at + r : at + r + 512] = jnp.transpose(ref[r : r + 512, :HD])
            at += count
        dk[...] = jnp.zeros_like(dk)
        dv[...] = jnp.zeros_like(dv)

    scaled = q[...] * jnp.asarray(HD**-0.5, bf16)
    low_row = low[...]
    high_row = high[...]
    log_total = lse[0]
    given = grad[...]
    delta = jnp.sum(jnp.transpose(given.astype(f32) * attended[...].astype(f32)), axis=0, keepdims=True)

    def block(j, acc):
        rows = pl.ds(pl.multiple_of(j * wide, wide), wide)
        scores = mul(keys[rows, :], scaled, NT)
        grad_probs = mul(values[rows, :], given, NT)
        key = j * wide + lax.broadcasted_iota(jnp.int32, (wide, tall), 0)
        probs = jnp.exp(jnp.where((key >= low_row) & (key <= high_row), scores - log_total, MASKED))
        grad_scores = (probs * (grad_probs - delta)).astype(bf16)
        dv[rows, :] += mul(probs.astype(bf16), given)
        dk[rows, :] += mul(grad_scores, scaled)
        return acc + mul(keys_turned[:, rows], grad_scores)

    acc = lax.fori_loop(first[step], last[step] + 1, block, jnp.zeros((HD, tall), f32))
    full = jnp.transpose(acc) * (HD**-0.5)
    dq[:, :128] = turn(full[:, :128], cos[...], sin[...], -1).astype(bf16)
    dq[:, 128:] = full[:, 128:].astype(bf16)

    @pl.when(step == pl.num_programs(1) - 1)
    def _():
        at = 0
        for ref in (dleft, down, dright):
            count = ref.shape[0]
            ref[:, :HD] = dk[at : at + count, :].astype(ref.dtype)
            ref[:, HD:] = dv[at : at + count, :].astype(ref.dtype)
            at += count


def attend_back(q, left, own, right, low, high, lse, attended, grad, cos, sin, tall=512, wide=512):
    rows, width = q.shape
    heads = width // HD
    extent = left.shape[0] + rows + right.shape[0]
    pair = lambda a: pl.BlockSpec((a.shape[0], 2 * HD), lambda h, i, *_: (0, h))
    row = pl.BlockSpec((1, tall), lambda h, i, *_: (0, i))
    mine = pl.BlockSpec((tall, HD), lambda h, i, *_: (i, h))
    table = pl.BlockSpec((tall, 128), lambda h, i, *_: (i, 0))
    return pl.pallas_call(
        functools.partial(attend_back_kernel, wide=wide),
        grid_spec=pltpu.PrefetchScalarGridSpec(
            num_scalar_prefetch=2,
            grid=(heads, rows // tall),
            in_specs=[
                mine, pair(left), pair(own), pair(right), row, row,
                pl.BlockSpec((1, 1, tall), lambda h, i, *_: (h, 0, i)), mine, mine, table, table,
            ],
            out_specs=[mine, pair(left), pair(own), pair(right)],
            scratch_shapes=[
                pltpu.VMEM((extent, HD), bf16),
                pltpu.VMEM((extent, HD), bf16),
                pltpu.VMEM((HD, extent), bf16),
                pltpu.VMEM((extent, HD), f32),
                pltpu.VMEM((extent, HD), f32),
            ],
        ),
        out_shape=[
            jax.ShapeDtypeStruct((rows, width), bf16),
            jax.ShapeDtypeStruct(left.shape, bf16),
            jax.ShapeDtypeStruct(own.shape, f32),
            jax.ShapeDtypeStruct(right.shape, bf16),
        ],
        compiler_params=params(),
        cost_estimate=cost(16_000_000_000, 20_000_000, 3_000_000),
        name="attend_back",
    )(*key_blocks(low, high, tall, wide), q, left, own, right, low.reshape(1, rows), high.reshape(1, rows), lse, attended, grad, cos, sin)


def mixed_kernel(dq, own, later, earlier, cos, sin, out, sums):
    rows = dq.shape[0]
    near = earlier.shape[0]
    out[:, :HD] = dq[...]
    pairs = own[...] + later[...].astype(f32)
    top = pairs[:near] + earlier[...].astype(f32)
    for at, part in ((slice(0, near), top), (slice(near, rows), pairs[near:])):
        out[at, HD : HD + 128] = turn(part[:, :128], cos[at], sin[at], -1).astype(bf16)
        out[at, HD + 128 :] = part[:, 128:].astype(bf16)
    sums[...] = jnp.sum(out[...].astype(f32), axis=0, keepdims=True)


def mix(dq, own, later, earlier, cos, sin):
    rows, width = dq.shape
    heads = width // HD
    pair = lambda a: pl.BlockSpec((a.shape[0], 2 * HD), lambda h: (0, h))
    return pl.pallas_call(
        mixed_kernel,
        grid=(heads,),
        in_specs=[
            pl.BlockSpec((rows, HD), lambda h: (0, h)), pair(own), pair(later), pair(earlier),
            whole_spec(cos), whole_spec(sin),
        ],
        out_specs=[pl.BlockSpec((rows, 3 * HD), lambda h: (0, h)), pl.BlockSpec((1, 3 * HD), lambda h: (0, h))],
        out_shape=[
            jax.ShapeDtypeStruct((rows, 3 * width), bf16),
            jax.ShapeDtypeStruct((1, 3 * width), f32),
        ],
        compiler_params=params(),
        cost_estimate=cost(10_000_000, 14_000_000),
        name="mix",
    )(dq, own, later, earlier, cos, sin)


def input_kernel(mixed, w_a, w_b, second, tok, mean, inverse, gains, out_a, out_b, sums):
    step = pl.program_id(0)
    half = w_a.shape[0]
    grad_a = mul(mixed[...], w_a[...], NT)
    grad_b = mul(mixed[...], w_b[...], NT)
    scale = inverse[...]

    @pl.when(step == 0)
    def _():
        sums[...] = jnp.zeros_like(sums)

    pieces = []
    total = 0.0
    product = 0.0
    for number, grad in enumerate((grad_a, grad_b)):
        at = slice(number * half, (number + 1) * half)
        normed = (tok[:, at].astype(f32) - mean[...]) * scale
        other = second[:, at].astype(f32)
        both = grad * gains[0:1, at] + other * gains[2:3, at]
        sums[0:1, at] += jnp.sum(grad * normed, axis=0, keepdims=True)
        sums[1:2, at] += jnp.sum(grad, axis=0, keepdims=True)
        sums[2:3, at] += jnp.sum(other * normed, axis=0, keepdims=True)
        sums[3:4, at] += jnp.sum(other, axis=0, keepdims=True)
        total = total + jnp.sum(both, axis=1, keepdims=True)
        product = product + jnp.sum(both * normed, axis=1, keepdims=True)
        pieces.append((at, both, normed))
    total = total * (0.5 / half)
    product = product * (0.5 / half)
    for ref, chosen in ((out_a, step == 0), (out_b, step == 1)):

        @pl.when(chosen)
        def _(ref=ref):
            for at, both, normed in pieces:
                grad = (scale * (both - total - normed * product)).astype(bf16)
                for slab in range(half // 128):
                    ref[at.start // 128 + slab] = grad[:, slab * 128 : (slab + 1) * 128]


def input_back(mixed, w_a, w_b, second, tok, mean, inverse, gains, start, tile=256):
    width = tok.shape[1]
    depth = mixed.shape[1]
    row = lambda w: pl.BlockSpec((tile, w), lambda i: (i + start, 0))
    slabs = (width // 128, tile, 128)
    out = pl.BlockSpec(slabs, lambda i: (0, 0, 0))
    return pl.pallas_call(
        input_kernel,
        grid=(2,),
        in_specs=[
            row(depth), whole_spec(w_a), whole_spec(w_b), row(width), row(width), row(1), row(1), whole_spec(gains),
        ],
        out_specs=[out, out, pl.BlockSpec((8, width), lambda i: (0, 0))],
        out_shape=[jax.ShapeDtypeStruct(slabs, bf16)] * 2 + [jax.ShapeDtypeStruct((8, width), f32)],
        compiler_params=params(),
        cost_estimate=cost(4 * tile * depth * width, 14_000_000),
        name="input_back",
    )(mixed, w_a, w_b, second, tok, mean, inverse, gains)


def output_kernel(places, middle, tokens, bias, *refs):
    out = refs[-1]
    inside = middle[0] == 1
    for place in range(BLOCKS):
        settled, passed = refs[place % HALF], refs[HALF + place % HALF]
        for slab in range(BLOCK // 128):
            to = pl.ds(pl.multiple_of(places[place] * BLOCK + slab * 128, 128), 128)
            at = place // HALF * (BLOCK // 128) + slab
            total = jnp.where(inside, settled[at].astype(f32), passed[at].astype(f32))
            here = bias[0:1, place * BLOCK + slab * 128 : place * BLOCK + slab * 128 + 128]
            out[:, to] = (tokens[:, to].astype(f32) + total + here).astype(bf16)


def output_sum(places, middle, bias, settled, passed, tokens, tile=256):
    rows, width = tokens.shape
    row = lambda w: pl.BlockSpec((tile, w), lambda i, *_: (i, 0))
    slabs = pl.BlockSpec((width // 512, tile, 128), lambda i, *_: (0, i, 0))
    view = lambda a: a.reshape(width // 512, rows, 128)
    return pl.pallas_call(
        output_kernel,
        grid_spec=pltpu.PrefetchScalarGridSpec(
            num_scalar_prefetch=2,
            grid=(rows // tile,),
            in_specs=[row(width), whole_spec(bias)] + [slabs] * 8,
            out_specs=row(width),
        ),
        out_shape=jax.ShapeDtypeStruct((rows, width), bf16),
        compiler_params=params(),
        cost_estimate=cost(10_000_000, 17_000_000),
        name="output_sum",
    )(places, middle, tokens, bias, *map(view, settled), *map(view, passed))


def tokens_kernel(places, middle, upstream, settled, passed, *rest):
    out = rest[-1]
    inside = middle[0] == 1
    tile = out.shape[0]
    for slab in range(out.shape[1] // 128):
        per = BLOCK // 128
        at = slice(slab * tile, (slab + 1) * tile)
        to = pl.ds(pl.multiple_of(places[slab // per] * BLOCK + slab % per * 128, 128), 128)
        total = jnp.where(inside, settled[at].astype(f32), passed[at].astype(f32))
        out[:, to] = (upstream[:, to].astype(f32) + total).astype(bf16)


def tokens_sum(places, middle, upstream, settled, passed, number, earlier, tile=256):
    rows, width = upstream.shape
    row = pl.BlockSpec((tile, width), lambda i, *_: (number, 0))
    slabs = pl.BlockSpec((width // 128 * tile, 128), lambda i, *_: (0, 0))
    extra = [earlier]
    return pl.pallas_call(
        tokens_kernel,
        grid_spec=pltpu.PrefetchScalarGridSpec(
            num_scalar_prefetch=2,
            grid=(1,),
            in_specs=[row, slabs, slabs] + [pl.BlockSpec(memory_space=pl.ANY)] * len(extra),
            out_specs=row,
        ),
        out_shape=jax.ShapeDtypeStruct((rows, width), bf16),
        input_output_aliases={5: 0} if number else {},
        compiler_params=params(),
        cost_estimate=cost(2_000_000, 4_000_000),
        name="tokens_sum",
    )(places, middle, upstream, settled, passed, *extra)


class LineSum:
    def __init__(self, middle):
        self.middle = middle[0] == 1
        self.line = lax.axis_size("tensor") == 4
        self.pieces, self.joined, self.other, self.results = [], {}, {}, []

    def slot(self, piece, seen):
        number = len(self.pieces)
        shape = None if piece is None else piece.shape
        piece = None if piece is None else piece.reshape(-1, 128)
        self.pieces.append(piece)
        if not self.line:
            if piece is not None:
                total = lax.psum(piece, "tensor")
                self.results.append((total, total))
            return seen
        sent = []
        pairs, operand = [], None
        if piece is not None:
            operand = after(piece, seen)
            pairs += [(0, 1), (3, 2)]
        done = self.pieces[number - 2] if number >= 2 else None
        if done is not None:
            other = after(self.other[number - 2], (seen, self.inward))
            settled = (self.joined[number - 2] + other.astype(f32)).astype(bf16)
            if operand is None:
                operand = settled
            else:
                settled = jnp.pad(settled, ((0, operand.shape[0] - settled.shape[0]), (0, 0)))
                operand = jnp.where(self.middle, settled, operand)
            pairs += [(1, 0), (2, 3)]
        if number >= 1 and self.pieces[number - 1] is not None:
            inward = after(self.inward, seen).astype(f32)
            joined = (self.pieces[number - 1].astype(f32) + inward).astype(bf16)
            self.joined[number - 1] = joined.astype(f32)
            self.other[number - 1] = lax.ppermute(joined, "tensor", [(1, 2), (2, 1)])
            sent.append(joined)
        if operand is not None:
            self.inward = lax.ppermute(operand, "tensor", pairs)
            sent.append(operand)
        if done is not None:
            self.results.append((operand, self.inward))
        return tuple(sent)


def scatter_blocks(blocks, by_rows):
    if is_cube():
        return lax.psum_scatter(blocks, "dp", scatter_dimension=0, tiled=True)[0].astype(f32)
    if by_rows:
        full = blocks.reshape(-1, blocks.shape[2])
        return lax.psum_scatter(full, "dp", scatter_dimension=0, tiled=True).astype(f32)
    full = blocks.transpose(1, 0, 2).reshape(blocks.shape[1], -1)
    return lax.psum_scatter(full, "dp", scatter_dimension=1, tiled=True).astype(f32)


def ring(value, step):
    count = lax.axis_size("dp")
    pairs = [(i, i + step) for i in range(count) if 0 <= i + step < count]
    return lax.ppermute(value, "dp", pairs)


def locate(token_index, lengths, prefix):
    ends = jnp.cumsum(lengths)
    starts = ends - lengths
    inside = (token_index[:, None] >= starts[None, :]) & (token_index[:, None] < ends[None, :])
    begin = jnp.sum(jnp.where(inside, starts[None, :], 0), axis=1)
    limit = jnp.sum(jnp.where(inside, jnp.minimum(prefix, lengths)[None, :], 0), axis=1)
    return begin, limit


def rotary_tables(places):
    lane = jnp.arange(128, dtype=jnp.int32)
    exponents = (lane % (ROT // 2)).astype(f32) * (2.0 / ROT)
    angles = places.astype(f32)[:, None] * jnp.exp(exponents * -math.log(10000.0))[None, :]
    turned = (lane < ROT)[None, :]
    sign = jnp.where(lane < ROT // 2, -1.0, 1.0)[None, :]
    return jnp.where(turned, jnp.cos(angles), 1.0), jnp.where(turned, jnp.sin(angles) * sign, 0.0)


def on_device(
    tokens,
    project_weight,
    project_bias,
    dense_weight,
    dense_bias,
    expand_weight,
    expand_bias,
    shrink_weight,
    shrink_bias,
    first_gain,
    first_shift,
    second_gain,
    second_shift,
    lengths,
    prefix,
    upstream,
):
    rows, width = tokens.shape
    count = lax.axis_size("dp")
    me = lax.axis_index("dp")
    heads = project_bias.shape[0]
    places = natural_places()
    cube = is_cube()
    line = lax.axis_index("tensor")
    middle = ((line == 1) | (line == 2)).astype(jnp.int32).reshape(1)

    turned_width, hidden_width = dense_weight.shape[0], shrink_weight.shape[0]
    vectors = [first_gain, first_shift, second_gain, second_shift, dense_bias, shrink_bias]
    if cube:
        own = jnp.concatenate([v.reshape(-1).astype(bf16) for v in (*vectors, expand_bias, project_bias)])
        own = jnp.pad(own, (0, -own.size % 2048)).reshape(-1, 128)
        gathered = lax.all_gather(own, "dp", axis=0).reshape(count, -1)
        small = jnp.take(gathered, places, axis=0).astype(f32)
        wide = vectors[0].shape[0]
        rows_of = jnp.stack([small[:, k * wide : (k + 1) * wide].reshape(-1) for k in range(len(vectors))])
        at = len(vectors) * wide
        small = gathered.astype(f32)
        split = at + expand_bias.size
        full_expand_bias = small[:, at:split].reshape((count,) + expand_bias.shape).transpose(1, 0, 2).reshape(1, -1)
        full_project_bias = small[:, split : split + project_bias.size].reshape((count,) + project_bias.shape).transpose(1, 0, 2).reshape(1, -1)
    else:
        rows_of = lax.all_gather(jnp.stack(vectors).astype(bf16), "dp", axis=1, tiled=True).astype(f32)
        full_expand_bias = lax.all_gather(expand_bias.astype(bf16), "dp", axis=1, tiled=True).astype(f32).reshape(1, -1)
        full_project_bias = lax.all_gather(project_bias.astype(bf16), "dp", axis=1, tiled=True).astype(f32).reshape(1, -1)
    gains = jnp.concatenate([rows_of[:4], jnp.zeros((4, width), f32)], axis=0)
    bias_total = rows_of[4:5] + rows_of[5:6]

    def halved(vector, bit):
        keep = vector.shape[0] // 2
        return vector[:keep] + swap(vector[keep:], bit)

    def vector_parts(sums, grad_bias, expand_bias_sums, project_bias_sums):
        norms = sums[:4].reshape(4, BLOCKS, BLOCK).transpose(1, 0, 2).reshape(BLOCKS, -1)
        bias = grad_bias[0].reshape(BLOCKS, BLOCK)
        per_head = lambda v, like: v.reshape(heads, BLOCKS, like.shape[1]).transpose(1, 0, 2).reshape(BLOCKS, -1)
        heads_part = jnp.concatenate(
            [per_head(expand_bias_sums, expand_bias), per_head(project_bias_sums, project_bias)], axis=1
        )
        heads_part = jnp.take(heads_part, places, axis=0)
        return jnp.concatenate([norms, bias, heads_part], axis=1)

    token_index = me * rows + jnp.arange(rows, dtype=jnp.int32)
    begin, limit = locate(token_index, lengths, prefix)
    base = me * rows - SEQ_MAX
    low = begin - base
    high = jnp.maximum(token_index, begin + limit - 1) - base
    cos, sin = rotary_tables(token_index - begin)

    tok, one_a, one_b, two_a, two_b, up_a, up_b, mean, inverse, grad_bias = norm(places, tokens, upstream, gains)

    spread_expand = Spread(expand_weight.astype(bf16))
    spread_project = Spread(project_weight.astype(bf16))
    seen_expand = spread_expand.first()
    seen_project = spread_project.first()
    seen_expand_too = spread_expand.second(seen_expand, mean)
    seen_project_too = spread_project.second(seen_project, mean)
    down_weight = jnp.concatenate([dense_weight.astype(bf16), shrink_weight.astype(bf16)], axis=0)
    down_weight = after(down_weight, (mean, seen_expand, seen_project))
    project_a, project_b = spread_project.join(seen_project_too, down_weight)
    expand_a, expand_b = spread_expand.join(seen_expand_too, project_a)
    down_blocks = gather_columns(after(down_weight, (project_a, expand_a)))
    queries, pairs = project(after(one_a, expand_a), one_b, project_a, project_b, full_project_bias, cos, sin)
    left = ring(pairs, 1)
    right = ring(pairs[:PREFIX_MAX], -1)
    if cube:
        own_blocks = (down_weight, swap(after(down_weight, seen_expand_too), CORE))
    else:
        own_blocks = (down_blocks[0], down_blocks[HALF])
    active, slope = expand(after(two_a, (pairs, own_blocks)), two_b, expand_a, expand_b, full_expand_bias)
    attended, lse = attend(after(queries, active), left, pairs, right, low, high)

    line = LineSum(middle)
    pieces = [branch_piece(attended, active, *own_blocks)]
    seen = line.slot(pieces[0], ())
    column_blocks = column_grad(places, after(attended, (pieces[0], seen)), active, up_a, up_b)
    grad_attended = back(places, after(up_a, column_blocks), up_b, down_blocks, 0, turned_width)
    dq, dleft, down, dright = attend_back(
        queries, left, pairs, right, low, high, lse, attended, grad_attended, cos, sin
    )
    later = ring(dleft, -1)
    earlier = ring(dright, 1)
    last = dq
    for place in (1, 2, 3):
        pieces.append(branch_place(places, after(attended, last), active, down_blocks, place))
        last = pieces[-1]
        if place == 1:
            seen = line.slot(pieces[1], last)
            last = (last, seen, earlier)
    column_blocks, later, earlier, last = lax.optimization_barrier((column_blocks, later, earlier, last))
    grad_down = scatter_blocks(column_blocks, False)
    grad_hidden, expand_bias_sums = back(
        places, after(up_a, last), up_b, down_blocks, turned_width, hidden_width, slope
    )
    seen = line.slot(pieces[2], grad_hidden)
    grad_second = second_back(after(grad_hidden, seen), expand_a, expand_b)
    grad_mixed, project_bias_sums = mix(after(dq, grad_second), down, later, earlier, cos, sin)
    seen = line.slot(pieces[3], grad_mixed)
    *tails, sums = input_back(
        after(grad_mixed, seen), project_a, project_b, grad_second, tok, mean, inverse, gains, 0
    )
    seen = line.slot(tails[0], sums)
    *more, part = input_back(
        after(grad_mixed, (sums, seen)), project_a, project_b, grad_second, tok, mean, inverse, gains, 2
    )
    tails += more
    sums = sums + part
    seen = line.slot(tails[1], part)
    vector = part
    if cube:
        vector = after(vector_parts(sums, grad_bias, expand_bias_sums, project_bias_sums), seen)
        vector = halved(halved(halved(vector, CORE), ALONG_Y), ALONG_X)[0]
    widths = grad_hidden.shape[1], grad_mixed.shape[1]
    row_blocks = row_grad(places, two_a, two_b, after(grad_hidden, seen), sum(widths))
    row_blocks = row_grad(places, one_a, one_b, grad_mixed, sum(widths), widths[0], row_blocks)
    seen = line.slot(tails[2], row_blocks)
    row_blocks, grad_down, vector, seen = lax.optimization_barrier((row_blocks, grad_down, vector, seen))
    if cube:
        grad_rows = scatter_blocks(row_blocks, True)
        grad_expand, grad_project = grad_rows[:, : widths[0]], grad_rows[:, widths[0] :]
    else:
        grad_expand = scatter_blocks(row_blocks[:, :, : widths[0]], True)
        grad_project = scatter_blocks(row_blocks[:, :, widths[0] :], True)
    settled, passed = zip(*line.results[:4])
    output = output_sum(places, middle, after(bias_total, (row_blocks, seen)), settled, passed, tokens)
    tail = tails[3]
    if cube:
        norms = vector[: 4 * BLOCK].astype(bf16).reshape(-1, 128)
        tail = jnp.concatenate([tail.reshape(-1, 128), norms, jnp.zeros_like(norms)], axis=0)
    seen = line.slot(tail, output)
    tokens_grad = tokens_sum(places, middle, upstream, *line.results[4], 0, after(up_a, (output, seen)))
    seen = line.slot(None, tokens_grad)
    tokens_grad = tokens_sum(places, middle, upstream, *line.results[5], 1, after(tokens_grad, seen))
    line.slot(None, tokens_grad)
    for number in range(2, 4):
        tokens_grad = tokens_sum(places, middle, upstream, *line.results[4 + number], number, tokens_grad)
    grad_dense, grad_shrink = grad_down[:turned_width], grad_down[turned_width:]

    if cube:
        settled, passed = line.results[7]
        norms = jnp.where(middle[0] == 1, settled[-16:-8], passed[-16:-8]).astype(f32).reshape(4, BLOCK)
        at = 5 * BLOCK
        bias = vector[4 * BLOCK : at]
        expand_bias_grad = vector[at : at + expand_bias.size].reshape(expand_bias.shape)
        project_bias_grad = vector[at + expand_bias.size :].reshape(project_bias.shape)
    else:
        norms = lax.psum(lax.psum_scatter(sums[:4], "dp", scatter_dimension=1, tiled=True), "tensor")
        bias = lax.psum_scatter(grad_bias[0], "dp", scatter_dimension=0, tiled=True)
        split = lambda v: lax.psum_scatter(v.reshape(heads, -1), "dp", scatter_dimension=1, tiled=True)
        expand_bias_grad, project_bias_grad = split(expand_bias_sums), split(project_bias_sums)
    return (
        output,
        tokens_grad,
        grad_project,
        project_bias_grad,
        grad_dense,
        bias,
        grad_expand,
        expand_bias_grad,
        grad_shrink,
        bias,
        norms[0],
        norms[1],
        norms[2],
        norms[3],
    )


def solution(mesh):
    placed = (
        P("dp", None),
        P("dp", "tensor"),
        P("tensor", "dp"),
        P("tensor", "dp"),
        P("dp"),
        P("dp", "tensor"),
        P("tensor", "dp"),
        P("tensor", "dp"),
        P("dp"),
        P("dp"),
        P("dp"),
        P("dp"),
        P("dp"),
        P(),
        P(),
        P("dp", None),
    )
    return jax.shard_map(
        on_device,
        mesh=mesh,
        in_specs=placed,
        out_specs=(
            P("dp", None),
            P("dp", None),
            P("dp", "tensor"),
            P("tensor", "dp"),
            P("tensor", "dp"),
            P("dp"),
            P("dp", "tensor"),
            P("tensor", "dp"),
            P("tensor", "dp"),
            P("dp"),
            P("dp"),
            P("dp"),
            P("dp"),
            P("dp"),
        ),
        check_vma=False,
    )
```

```python
import functools
import math

import jax
import jax.numpy as jnp
from jax import lax
from jax.experimental import pallas as pl
from jax.experimental.pallas import tpu as pltpu
from jax.sharding import PartitionSpec as P

HD = 256
ROT = 64
SEQ_MAX = 1024
PREFIX_MAX = 512
BLOCK = 256
BLOCKS = 8
HALF = 4
EPSILON = 1e-05
MASKED = -1e30
bf16 = jnp.bfloat16
f32 = jnp.float32
NN = (((1,), (0,)), ((), ()))
NT = (((1,), (1,)), ((), ()))
TN = (((0,), (0,)), ((), ()))
VMEM_BYTES = 56 * 2**20


def mul(a, b, dims=NN):
    return lax.dot_general(a, b, dims, preferred_element_type=f32)


def params(**more):
    return pltpu.CompilerParams(vmem_limit_bytes=VMEM_BYTES, **more)


def cost(flops, moved, transcendentals=0):
    return pl.CostEstimate(flops=flops, bytes_accessed=moved, transcendentals=transcendentals)


def whole_spec(array):
    zeros = (0,) * array.ndim
    return pl.BlockSpec(array.shape, lambda *_: zeros)


def swap(value, bit):
    count = lax.axis_size("dp")
    return lax.ppermute(value, "dp", [(i, i ^ bit) for i in range(count)])


CORE, ALONG_X, ALONG_Y = 1, 2, 4


def is_cube():
    return lax.axis_size("dp") == BLOCKS


def natural_places():
    place = jnp.arange(BLOCKS, dtype=jnp.int32)
    if not is_cube():
        return place
    owner = ((place >> 2) & 1) * CORE + ((place >> 1) & 1) * ALONG_Y + (place & 1) * ALONG_X
    return owner ^ lax.axis_index("dp")


class Spread:
    def __init__(self, weight, by_rows):
        self.weight, self.by_rows = weight, by_rows

    def first(self):
        if is_cube():
            self.from_x = swap(self.weight, ALONG_X)
            self.from_y = swap(self.weight, ALONG_Y)
            return self.from_x, self.from_y
        self.full = lax.all_gather(self.weight, "dp", axis=0 if self.by_rows else 1, tiled=True)
        return (self.full,)

    def second(self, *seen):
        if is_cube():
            half = self.weight.shape[0] // 2
            self.over_x = swap(after(self.from_x[:half], seen), ALONG_Y)
            self.over_y = swap(after(self.from_y[half:], seen), ALONG_X)
            return self.over_x, self.over_y
        return (self.full,)

    def join(self, *seen):
        if is_cube():
            parts = [self.weight, self.from_x, self.from_y, self.over_x, self.over_y]
            mine = jnp.concatenate(after(parts, seen), axis=0)
            return mine, swap(mine, CORE)
        half = self.full.shape[0] // 2
        return self.full[:half], self.full[half:]

    def begin_parts(self, *seen):
        if is_cube():
            self.near = [swap(after(part, seen), CORE) for part in (self.weight, self.from_x, self.from_y)]

    def parts(self, *seen):
        if is_cube():
            far = [swap(after(part, seen), CORE) for part in (self.over_x, self.over_y)]
            return [self.weight, self.from_x, self.from_y, self.over_x, self.over_y], self.near + far
        half = self.full.shape[0] // 2
        return [self.full[:half]], [self.full[half:]]

    def pair(self, place, seen=()):
        if is_cube():
            if place == 3:
                mine = jnp.concatenate([self.over_x, self.over_y], axis=0)
            else:
                mine = self.weight if place == 0 else (self.from_x, self.from_y)[place - 1]
            return mine, swap(after(mine, seen), CORE)
        blocks = self.full.reshape(self.full.shape[0], BLOCKS, -1)
        return blocks[:, place], blocks[:, place + HALF]


def after(value, seen):
    return lax.optimization_barrier((value, seen))[0]


def norm_kernel(places, tokens, upstream, gains, tok, one_a, one_b, two_a, two_b, up_a, up_b, mean, inverse, grad_bias):
    values = tokens[...].astype(f32)
    average = jnp.mean(values, axis=1, keepdims=True)
    center = values - average
    scale = lax.rsqrt(jnp.mean(center * center, axis=1, keepdims=True) + EPSILON)
    mean[...] = average
    inverse[...] = scale

    @pl.when(pl.program_id(0) == 0)
    def _():
        grad_bias[...] = jnp.zeros_like(grad_bias)

    for place in range(BLOCKS):
        from_ = pl.ds(pl.multiple_of(places[place] * BLOCK, BLOCK), BLOCK)
        to = pl.ds(place * BLOCK, BLOCK)
        inner = pl.ds(place % HALF * BLOCK, BLOCK)
        first, second, up = (one_a, two_a, up_a) if place < HALF else (one_b, two_b, up_b)
        low = tokens[:, from_]
        tok[:, to] = low
        normed = (low.astype(f32) - average) * scale
        first[:, inner] = (normed * gains[0:1, to] + gains[1:2, to]).astype(bf16)
        second[:, inner] = (normed * gains[2:3, to] + gains[3:4, to]).astype(bf16)
        grad = upstream[:, from_]
        up[:, inner] = grad
        grad_bias[0:1, to] += jnp.sum(grad.astype(f32), axis=0, keepdims=True)


def norm(places, tokens, upstream, gains, tile=256):
    rows, width = tokens.shape
    row = lambda w: pl.BlockSpec((tile, w), lambda i, *_: (i, 0))
    shape = lambda w, kind: jax.ShapeDtypeStruct((rows, w), kind)
    half = width // 2
    return pl.pallas_call(
        norm_kernel,
        grid_spec=pltpu.PrefetchScalarGridSpec(
            num_scalar_prefetch=1,
            grid=(rows // tile,),
            in_specs=[row(width), row(width), whole_spec(gains)],
            out_specs=[row(width)] + [row(half)] * 6 + [row(1), row(1), pl.BlockSpec((8, width), lambda *_: (0, 0))],
        ),
        out_shape=[shape(width, bf16)]
        + [shape(half, bf16)] * 6
        + [shape(1, f32), shape(1, f32), jax.ShapeDtypeStruct((8, width), f32)],
        compiler_params=params(),
        cost_estimate=cost(20 * rows * width, 20 * rows * width),
        name="norm",
    )(places, tokens, upstream, gains)


def turn(part, cos, sin, sign):
    lane = lax.broadcasted_iota(jnp.int32, part.shape, 1)
    partner = jnp.where(lane < ROT // 2, pltpu.roll(part, 128 - ROT // 2, 1), pltpu.roll(part, ROT // 2, 1))
    if sign > 0:
        return part * cos + partner * sin
    return part * cos - partner * sin


def project_kernel(one_a, one_b, w_a, w_b, bias, cos, sin, queries, pairs):
    for part in range(3):
        at = slice(part * HD, (part + 1) * HD)
        mixed = mul(one_a[...], w_a[:, at]) + mul(one_b[...], w_b[:, at]) + bias[:, at]
        if part < 2:
            ref, to = (queries, 0) if part == 0 else (pairs, 0)
            ref[:, to : to + 128] = turn(mixed[:, :128], cos[...], sin[...], 1).astype(bf16)
            ref[:, to + 128 : to + HD] = mixed[:, 128:].astype(bf16)
        else:
            pairs[:, HD:] = mixed.astype(bf16)


def project(one_a, one_b, w_a, w_b, bias, cos, sin):
    rows, half = one_a.shape
    heads = w_a.shape[1] // (3 * HD)
    weight = pl.BlockSpec((half, 3 * HD), lambda h: (0, h))
    return pl.pallas_call(
        project_kernel,
        grid=(heads,),
        in_specs=[
            whole_spec(one_a),
            whole_spec(one_b),
            weight,
            weight,
            pl.BlockSpec((1, 3 * HD), lambda h: (0, h)),
            whole_spec(cos),
            whole_spec(sin),
        ],
        out_specs=[pl.BlockSpec((rows, HD), lambda h: (0, h)), pl.BlockSpec((rows, 2 * HD), lambda h: (0, h))],
        out_shape=[
            jax.ShapeDtypeStruct((rows, heads * HD), bf16),
            jax.ShapeDtypeStruct((rows, heads * 2 * HD), bf16),
        ],
        compiler_params=params(),
        cost_estimate=cost(4 * rows * half * w_a.shape[1], 14_000_000),
        name="project",
    )(one_a, one_b, w_a, w_b, bias, cos, sin)


def lay(parts, joined):
    at = 0
    for part in parts:
        joined[at : at + part.shape[0], :] = part[...]
        at += part.shape[0]


def expand_kernel(two_a, two_b, bias, *refs):
    *parts, active, slope, weight = refs
    lay(parts, weight)
    rows, half = two_a.shape
    for start in range(0, rows, 512):
        at = slice(start, start + 512)
        hidden = mul(two_a[at], weight[:half]) + mul(two_b[at], weight[half:]) + bias[...]
        below = 0.5 + 0.5 * lax.erf(hidden * (0.5**0.5))
        density = jnp.exp(hidden * hidden * -0.5) * (1.0 / math.sqrt(2.0 * math.pi))
        active[at] = (hidden * below).astype(bf16)
        slope[at] = (below + hidden * density).astype(bf16)


def expand(two_a, two_b, parts, bias, tile=512):
    rows, half = two_a.shape
    width = parts[0].shape[1]
    column = lambda r: pl.BlockSpec((r, tile), lambda n: (0, n))
    return pl.pallas_call(
        expand_kernel,
        grid=(width // tile,),
        in_specs=[whole_spec(two_a), whole_spec(two_b), column(1)] + [column(part.shape[0]) for part in parts],
        out_specs=[column(rows), column(rows)],
        out_shape=[jax.ShapeDtypeStruct((rows, width), bf16)] * 2,
        scratch_shapes=[pltpu.VMEM((2 * half, tile), bf16)],
        compiler_params=params(),
        cost_estimate=cost(0, 0),
        name="expand",
    )(two_a, two_b, bias, *parts)


def branch_kernel(attended, active, mine, theirs, out):
    depth = attended.shape[1]
    slabs = BLOCK // 128
    for number, weight in enumerate((mine, theirs)):
        full = (mul(attended[...], weight[:depth]) + mul(active[...], weight[depth:])).astype(bf16)
        for slab in range(slabs):
            out[number * slabs + slab] = full[:, slab * 128 : (slab + 1) * 128]


def branch_piece(attended, active, mine, theirs, tile=512):
    rows = attended.shape[0]
    depth = mine.shape[0]
    slabs = 2 * BLOCK // 128
    row = lambda a: pl.BlockSpec((tile, a.shape[1]), lambda i: (i, 0))
    return pl.pallas_call(
        branch_kernel,
        grid=(rows // tile,),
        in_specs=[row(attended), row(active), whole_spec(mine), whole_spec(theirs)],
        out_specs=pl.BlockSpec((slabs, tile, 128), lambda i: (0, i, 0)),
        out_shape=jax.ShapeDtypeStruct((slabs, rows, 128), bf16),
        compiler_params=params(),
        cost_estimate=cost(4 * rows * depth * BLOCK, 2 * (rows * depth + 2 * (rows + depth) * BLOCK)),
        name="branch",
    )(attended, active, mine, theirs)


def back_kernel(up_a, up_b, blocks, slope, out, sums, joined):
    for place in range(BLOCKS):
        joined[:, place * BLOCK : (place + 1) * BLOCK] = blocks[place][...]
    half = HALF * BLOCK
    total = jnp.zeros((1, out.shape[1]), f32)
    for start in range(0, out.shape[0], 512):
        at = slice(start, start + 512)
        grad = mul(up_a[at], joined[:, :half], NT) + mul(up_b[at], joined[:, half:], NT)
        if slope is not None:
            grad = grad * slope[at].astype(f32)
        grad = grad.astype(bf16)
        out[at] = grad
        if sums is not None:
            total = total + jnp.sum(grad.astype(f32), axis=0, keepdims=True)
    if sums is not None:
        sums[...] = total


def back(up_a, up_b, blocks, start, width, slope=None, tile=512):
    rows, half = up_a.shape
    weight = pl.BlockSpec((tile, BLOCK), lambda n: (n + start // tile, 0))
    column = lambda r: pl.BlockSpec((r, tile), lambda n: (0, n))
    scaled = slope is not None

    def body(a, b, *rest):
        blocks, rest = rest[:BLOCKS], rest[BLOCKS:]
        if scaled:
            s, out, sums, joined = rest
        else:
            (out, joined), s, sums = rest, None, None
        back_kernel(a, b, blocks, s, out, sums, joined)

    out = jax.ShapeDtypeStruct((rows, width), bf16)
    return pl.pallas_call(
        body,
        grid=(width // tile,),
        in_specs=[whole_spec(up_a), whole_spec(up_b)] + [weight] * BLOCKS + [column(rows)] * scaled,
        out_specs=[column(rows), column(1)] if scaled else column(rows),
        out_shape=[out, jax.ShapeDtypeStruct((1, width), f32)] if scaled else out,
        scratch_shapes=[pltpu.VMEM((tile, 2 * half), bf16)],
        compiler_params=params(),
        cost_estimate=cost(4 * rows * half * width, 4 * rows * half + 4 * half * width + 4 * rows * width),
        name="back",
    )(up_a, up_b, *blocks, *([slope] if scaled else []))


def second_kernel(grad, *refs):
    *parts, out, weight = refs
    tile = weight.shape[0]
    taken, size = [[]], 0
    for part in parts:
        for start in range(0, part.shape[0], tile):
            if size == tile:
                taken.append([])
                size = 0
            rows = min(tile, part.shape[0] - start)
            taken[-1].append(part.at[start : start + rows])
            size += rows
    for number, runs in enumerate(taken):
        pl.when(pl.program_id(0) == number)(functools.partial(lay, runs, weight))
    out[...] = mul(grad[...], weight[...], NT).astype(bf16)


def second_back(grad, parts, tile=512):
    rows, width = grad.shape
    depth = sum(part.shape[0] for part in parts)
    return pl.pallas_call(
        second_kernel,
        grid=(depth // tile,),
        in_specs=[whole_spec(grad)] + [whole_spec(part) for part in parts],
        out_specs=pl.BlockSpec((rows, tile), lambda n: (0, n)),
        out_shape=jax.ShapeDtypeStruct((rows, depth), bf16),
        scratch_shapes=[pltpu.VMEM((tile, width), bf16)],
        compiler_params=params(),
        cost_estimate=cost(2 * rows * depth * width, 2 * (rows + depth) * width + 2 * rows * depth),
        name="second_back",
    )(grad, *parts)


def row_grad_kernel(where, left_a, left_b, right, *rest):
    out = rest[-1]
    for number, left in enumerate((left_a, left_b)):
        full = mul(left[...], right[...], TN)
        for place in range(HALF):
            out[where[number * HALF + place]] = full[place * BLOCK : (place + 1) * BLOCK].astype(bf16)


def row_grad(where, left_a, left_b, right, total, start=0, into=None, tile=512):
    rows, width = right.shape
    blocks = 2 * HALF
    extra = [] if into is None else [into]
    return pl.pallas_call(
        row_grad_kernel,
        grid_spec=pltpu.PrefetchScalarGridSpec(
            num_scalar_prefetch=1,
            grid=(width // tile,),
            in_specs=[whole_spec(left_a), whole_spec(left_b), pl.BlockSpec((rows, tile), lambda n, *_: (0, n))]
            + [pl.BlockSpec(memory_space=pl.ANY)] * len(extra),
            out_specs=pl.BlockSpec((blocks, BLOCK, tile), lambda n, *_: (0, 0, n + start // tile)),
        ),
        out_shape=jax.ShapeDtypeStruct((blocks, BLOCK, total), bf16),
        input_output_aliases={4: 0} if extra else {},
        compiler_params=params(),
        cost_estimate=cost(2 * rows * blocks * BLOCK * width, 2 * blocks * BLOCK * (rows + width) + 2 * rows * width),
        name="row_grad",
    )(where, left_a, left_b, right, *extra)


def column_grad_kernel(where, left, right_a, right_b, *rest):
    out = rest[-1]
    for number, right in enumerate((right_a, right_b)):
        full = mul(left[...], right[...], TN)
        for place in range(HALF):
            out[where[number * HALF + place]] = full[:, place * BLOCK : (place + 1) * BLOCK].astype(bf16)


def column_grad(where, left, right_a, right_b, total, start=0, into=None, tile=512):
    rows, width = left.shape
    blocks = 2 * HALF
    extra = [] if into is None else [into]
    return pl.pallas_call(
        column_grad_kernel,
        grid_spec=pltpu.PrefetchScalarGridSpec(
            num_scalar_prefetch=1,
            grid=(width // tile,),
            in_specs=[pl.BlockSpec((rows, tile), lambda n, *_: (0, n)), whole_spec(right_a), whole_spec(right_b)]
            + [pl.BlockSpec(memory_space=pl.ANY)] * len(extra),
            out_specs=pl.BlockSpec((blocks, tile, BLOCK), lambda n, *_: (0, n + start // tile, 0)),
        ),
        out_shape=jax.ShapeDtypeStruct((blocks, total, BLOCK), bf16),
        input_output_aliases={4: 0} if extra else {},
        compiler_params=params(),
        cost_estimate=cost(0, 0),
        name="column_grad",
    )(where, left, right_a, right_b, *extra)


def fill(refs, heads, place):
    for head in range(heads):
        at = 0
        for ref in refs:
            for start in range(0, ref.shape[0], 512):
                rows = slice(start, start + 512)
                place(head, at, ref[rows, 2 * head * HD : (2 * head + 1) * HD], ref[rows, (2 * head + 1) * HD : (2 * head + 2) * HD])
                at += 512


def attend_kernel(first, last, q, left, own, right, low, high, out, lse, keys, values_turned, *, wide):
    step = pl.program_id(0)
    tall = q.shape[0]
    heads = range(keys.shape[0])

    @pl.when(step == 0)
    def _():
        def place(head, at, k, v):
            keys[head, at : at + 512, :] = k
            values_turned[head, :, at : at + 512] = jnp.transpose(v)

        fill((left, own, right), len(heads), place)

    scaled = [q[:, h * HD : (h + 1) * HD] * jnp.asarray(HD**-0.5, bf16) for h in heads]
    low_row = low[...]
    high_row = high[...]

    def block(j, carry):
        rows = pl.ds(pl.multiple_of(j * wide, wide), wide)
        key = j * wide + lax.broadcasted_iota(jnp.int32, (wide, tall), 0)
        seen = (key >= low_row) & (key <= high_row)
        scores = [mul(keys[h, rows, :], scaled[h], NT) for h in heads]
        after_block = []
        for h in heads:
            top, total, acc = carry[h]
            masked = jnp.where(seen, scores[h], MASKED)
            new = jnp.maximum(top, jnp.max(masked, axis=0, keepdims=True))
            weights = jnp.exp(masked - new)
            fade = jnp.exp(top - new)
            total = total * fade + jnp.sum(weights, axis=0, keepdims=True)
            acc = acc * fade + mul(values_turned[h, :, rows], weights.astype(bf16))
            after_block.append((new, total, acc))
        return tuple(after_block)

    start = (jnp.full((1, tall), MASKED, f32), jnp.zeros((1, tall), f32), jnp.zeros((HD, tall), f32))
    done = lax.fori_loop(first[step], last[step] + 1, block, tuple(start for _ in heads))
    for h in heads:
        top, total, acc = done[h]
        out[:, h * HD : (h + 1) * HD] = jnp.transpose(acc / total).astype(bf16)
        lse[h] = top + jnp.log(total)


def key_blocks(low, high, tall, wide):
    return jnp.min(low.reshape(-1, tall), axis=1) // wide, jnp.max(high.reshape(-1, tall), axis=1) // wide


def attend(q, left, own, right, low, high, tall=256, wide=512):
    rows, width = q.shape
    heads = width // HD
    extent = left.shape[0] + rows + right.shape[0]
    row = pl.BlockSpec((1, tall), lambda i, *_: (0, i))
    mine = pl.BlockSpec((tall, width), lambda i, *_: (i, 0))
    return pl.pallas_call(
        functools.partial(attend_kernel, wide=wide),
        grid_spec=pltpu.PrefetchScalarGridSpec(
            num_scalar_prefetch=2,
            grid=(rows // tall,),
            in_specs=[mine, whole_spec(left), whole_spec(own), whole_spec(right), row, row],
            out_specs=[mine, pl.BlockSpec((heads, 1, tall), lambda i, *_: (0, 0, i))],
            scratch_shapes=[pltpu.VMEM((heads, extent, HD), bf16), pltpu.VMEM((heads, HD, extent), bf16)],
        ),
        out_shape=[jax.ShapeDtypeStruct((rows, width), bf16), jax.ShapeDtypeStruct((heads, 1, rows), f32)],
        compiler_params=params(),
        cost_estimate=cost(8_000_000_000, 10_000_000, 3_000_000),
        name="attend",
    )(*key_blocks(low, high, tall, wide), q, left, own, right, low.reshape(1, rows), high.reshape(1, rows))


def attend_back_kernel(
    first, last, q, left, own, right, low, high, lse, attended, grad, cos, sin,
    dq, dleft, down, dright, keys, values, keys_turned, dk, dv, *, wide,
):
    step = pl.program_id(0)
    tall = q.shape[0]
    heads = range(keys.shape[0])

    @pl.when(step == 0)
    def _():
        def place(head, at, k, v):
            keys[head, at : at + 512, :] = k
            values[head, at : at + 512, :] = v
            keys_turned[head, :, at : at + 512] = jnp.transpose(k)

        fill((left, own, right), len(heads), place)
        dk[...] = jnp.zeros_like(dk)
        dv[...] = jnp.zeros_like(dv)

    cut = lambda ref, h: ref[:, h * HD : (h + 1) * HD]
    scaled = [cut(q, h) * jnp.asarray(HD**-0.5, bf16) for h in heads]
    given = [cut(grad, h) for h in heads]
    low_row = low[...]
    high_row = high[...]
    deltas = [
        jnp.sum(jnp.transpose(given[h].astype(f32) * cut(attended, h).astype(f32)), axis=0, keepdims=True) for h in heads
    ]

    def block(j, accs):
        rows = pl.ds(pl.multiple_of(j * wide, wide), wide)
        key = j * wide + lax.broadcasted_iota(jnp.int32, (wide, tall), 0)
        seen = (key >= low_row) & (key <= high_row)
        scores = [mul(keys[h, rows, :], scaled[h], NT) for h in heads]
        grad_probs = [mul(values[h, rows, :], given[h], NT) for h in heads]
        after_block = []
        for h in heads:
            probs = jnp.exp(jnp.where(seen, scores[h] - lse[h], MASKED))
            grad_scores = (probs * (grad_probs[h] - deltas[h])).astype(bf16)
            dv[h, rows, :] += mul(probs.astype(bf16), given[h])
            dk[h, rows, :] += mul(grad_scores, scaled[h])
            after_block.append(accs[h] + mul(keys_turned[h, :, rows], grad_scores))
        return tuple(after_block)

    accs = lax.fori_loop(first[step], last[step] + 1, block, tuple(jnp.zeros((HD, tall), f32) for _ in heads))
    for h in heads:
        full = jnp.transpose(accs[h]) * (HD**-0.5)
        dq[:, h * HD : h * HD + 128] = turn(full[:, :128], cos[...], sin[...], -1).astype(bf16)
        dq[:, h * HD + 128 : (h + 1) * HD] = full[:, 128:].astype(bf16)

    @pl.when(step == pl.num_programs(0) - 1)
    def _():
        for h in heads:
            at = 0
            for ref in (dleft, down, dright):
                count = ref.shape[0]
                ref[:, 2 * h * HD : (2 * h + 1) * HD] = dk[h, at : at + count, :].astype(ref.dtype)
                ref[:, (2 * h + 1) * HD : (2 * h + 2) * HD] = dv[h, at : at + count, :].astype(ref.dtype)
                at += count


def attend_back(q, left, own, right, low, high, lse, attended, grad, cos, sin, tall=256, wide=512):
    rows, width = q.shape
    heads = width // HD
    extent = left.shape[0] + rows + right.shape[0]
    row = pl.BlockSpec((1, tall), lambda i, *_: (0, i))
    mine = pl.BlockSpec((tall, width), lambda i, *_: (i, 0))
    table = pl.BlockSpec((tall, 128), lambda i, *_: (i, 0))
    return pl.pallas_call(
        functools.partial(attend_back_kernel, wide=wide),
        grid_spec=pltpu.PrefetchScalarGridSpec(
            num_scalar_prefetch=2,
            grid=(rows // tall,),
            in_specs=[
                mine, whole_spec(left), whole_spec(own), whole_spec(right), row, row,
                pl.BlockSpec((heads, 1, tall), lambda i, *_: (0, 0, i)), mine, mine, table, table,
            ],
            out_specs=[mine, whole_spec(left), whole_spec(own), whole_spec(right)],
            scratch_shapes=[
                pltpu.VMEM((heads, extent, HD), bf16),
                pltpu.VMEM((heads, extent, HD), bf16),
                pltpu.VMEM((heads, HD, extent), bf16),
                pltpu.VMEM((heads, extent, HD), f32),
                pltpu.VMEM((heads, extent, HD), f32),
            ],
        ),
        out_shape=[
            jax.ShapeDtypeStruct((rows, width), bf16),
            jax.ShapeDtypeStruct(left.shape, bf16),
            jax.ShapeDtypeStruct(own.shape, f32),
            jax.ShapeDtypeStruct(right.shape, bf16),
        ],
        compiler_params=params(),
        cost_estimate=cost(16_000_000_000, 20_000_000, 3_000_000),
        name="attend_back",
    )(*key_blocks(low, high, tall, wide), q, left, own, right, low.reshape(1, rows), high.reshape(1, rows), lse, attended, grad, cos, sin)


def mixed_kernel(dq, own, later, earlier, cos, sin, out, sums):
    rows = dq.shape[0]
    near = earlier.shape[0]
    out[:, :HD] = dq[...]
    pairs = own[...] + later[...].astype(f32)
    top = pairs[:near] + earlier[...].astype(f32)
    for at, part in ((slice(0, near), top), (slice(near, rows), pairs[near:])):
        out[at, HD : HD + 128] = turn(part[:, :128], cos[at], sin[at], -1).astype(bf16)
        out[at, HD + 128 :] = part[:, 128:].astype(bf16)
    sums[...] = jnp.sum(out[...].astype(f32), axis=0, keepdims=True)


def mix(dq, own, later, earlier, cos, sin):
    rows, width = dq.shape
    heads = width // HD
    pair = lambda a: pl.BlockSpec((a.shape[0], 2 * HD), lambda h: (0, h))
    return pl.pallas_call(
        mixed_kernel,
        grid=(heads,),
        in_specs=[
            pl.BlockSpec((rows, HD), lambda h: (0, h)), pair(own), pair(later), pair(earlier),
            whole_spec(cos), whole_spec(sin),
        ],
        out_specs=[pl.BlockSpec((rows, 3 * HD), lambda h: (0, h)), pl.BlockSpec((1, 3 * HD), lambda h: (0, h))],
        out_shape=[
            jax.ShapeDtypeStruct((rows, 3 * width), bf16),
            jax.ShapeDtypeStruct((1, 3 * width), f32),
        ],
        compiler_params=params(),
        cost_estimate=cost(10_000_000, 14_000_000),
        name="mix",
    )(dq, own, later, earlier, cos, sin)


def input_kernel(mixed, w_a, w_b, second, tok, mean, inverse, gains, out_a, out_b, sums):
    step = pl.program_id(0)
    half = w_a.shape[0]
    grad_a = mul(mixed[...], w_a[...], NT)
    grad_b = mul(mixed[...], w_b[...], NT)
    scale = inverse[...]

    @pl.when(step == 0)
    def _():
        sums[...] = jnp.zeros_like(sums)

    pieces = []
    total = 0.0
    product = 0.0
    for number, grad in enumerate((grad_a, grad_b)):
        at = slice(number * half, (number + 1) * half)
        normed = (tok[:, at].astype(f32) - mean[...]) * scale
        other = second[:, at].astype(f32)
        both = grad * gains[0:1, at] + other * gains[2:3, at]
        sums[0:1, at] += jnp.sum(grad * normed, axis=0, keepdims=True)
        sums[1:2, at] += jnp.sum(grad, axis=0, keepdims=True)
        sums[2:3, at] += jnp.sum(other * normed, axis=0, keepdims=True)
        sums[3:4, at] += jnp.sum(other, axis=0, keepdims=True)
        total = total + jnp.sum(both, axis=1, keepdims=True)
        product = product + jnp.sum(both * normed, axis=1, keepdims=True)
        pieces.append((at, both, normed))
    total = total * (0.5 / half)
    product = product * (0.5 / half)
    for ref, chosen in ((out_a, step == 0), (out_b, step == 1)):

        @pl.when(chosen)
        def _(ref=ref):
            for at, both, normed in pieces:
                grad = (scale * (both - total - normed * product)).astype(bf16)
                for slab in range(half // 128):
                    ref[at.start // 128 + slab] = grad[:, slab * 128 : (slab + 1) * 128]


def input_back(mixed, w_a, w_b, second, tok, mean, inverse, gains, start, tile=256):
    width = tok.shape[1]
    depth = mixed.shape[1]
    row = lambda w: pl.BlockSpec((tile, w), lambda i: (i + start, 0))
    slabs = (width // 128, tile, 128)
    out = pl.BlockSpec(slabs, lambda i: (0, 0, 0))
    return pl.pallas_call(
        input_kernel,
        grid=(2,),
        in_specs=[
            row(depth), whole_spec(w_a), whole_spec(w_b), row(width), row(width), row(1), row(1), whole_spec(gains),
        ],
        out_specs=[out, out, pl.BlockSpec((8, width), lambda i: (0, 0))],
        out_shape=[jax.ShapeDtypeStruct(slabs, bf16)] * 2 + [jax.ShapeDtypeStruct((8, width), f32)],
        compiler_params=params(),
        cost_estimate=cost(4 * tile * depth * width, 14_000_000),
        name="input_back",
    )(mixed, w_a, w_b, second, tok, mean, inverse, gains)


def output_kernel(places, middle, tokens, bias, *refs):
    out = refs[-1]
    inside = middle[0] == 1
    for place in range(BLOCKS):
        settled, passed = refs[place % HALF], refs[HALF + place % HALF]
        for slab in range(BLOCK // 128):
            to = pl.ds(pl.multiple_of(places[place] * BLOCK + slab * 128, 128), 128)
            at = place // HALF * (BLOCK // 128) + slab
            total = jnp.where(inside, settled[at].astype(f32), passed[at].astype(f32))
            here = bias[0:1, place * BLOCK + slab * 128 : place * BLOCK + slab * 128 + 128]
            out[:, to] = (tokens[:, to].astype(f32) + total + here).astype(bf16)


def output_sum(places, middle, bias, settled, passed, tokens, tile=256):
    rows, width = tokens.shape
    row = lambda w: pl.BlockSpec((tile, w), lambda i, *_: (i, 0))
    slabs = pl.BlockSpec((width // 512, tile, 128), lambda i, *_: (0, i, 0))
    view = lambda a: a.reshape(width // 512, rows, 128)
    return pl.pallas_call(
        output_kernel,
        grid_spec=pltpu.PrefetchScalarGridSpec(
            num_scalar_prefetch=2,
            grid=(rows // tile,),
            in_specs=[row(width), whole_spec(bias)] + [slabs] * 8,
            out_specs=row(width),
        ),
        out_shape=jax.ShapeDtypeStruct((rows, width), bf16),
        compiler_params=params(),
        cost_estimate=cost(36_000_000_000, 17_000_000),
        name="output_sum",
    )(places, middle, tokens, bias, *map(view, settled), *map(view, passed))


def tokens_kernel(places, middle, upstream, settled, passed, *rest):
    out = rest[-1]
    inside = middle[0] == 1
    tile = out.shape[0]
    for slab in range(out.shape[1] // 128):
        per = BLOCK // 128
        at = slice(slab * tile, (slab + 1) * tile)
        to = pl.ds(pl.multiple_of(places[slab // per] * BLOCK + slab % per * 128, 128), 128)
        total = jnp.where(inside, settled[at].astype(f32), passed[at].astype(f32))
        out[:, to] = (upstream[:, to].astype(f32) + total).astype(bf16)


def tokens_sum(places, middle, upstream, settled, passed, number, earlier, tile=256):
    rows, width = upstream.shape
    row = pl.BlockSpec((tile, width), lambda i, *_: (number, 0))
    slabs = pl.BlockSpec((width // 128 * tile, 128), lambda i, *_: (0, 0))
    extra = [earlier]
    return pl.pallas_call(
        tokens_kernel,
        grid_spec=pltpu.PrefetchScalarGridSpec(
            num_scalar_prefetch=2,
            grid=(1,),
            in_specs=[row, slabs, slabs] + [pl.BlockSpec(memory_space=pl.ANY)] * len(extra),
            out_specs=row,
        ),
        out_shape=jax.ShapeDtypeStruct((rows, width), bf16),
        input_output_aliases={5: 0} if number else {},
        compiler_params=params(),
        cost_estimate=cost(36_000_000_000, 4_000_000),
        name="tokens_sum",
    )(places, middle, upstream, settled, passed, *extra)


class LineSum:
    def __init__(self, middle):
        self.middle = middle[0] == 1
        self.line = lax.axis_size("tensor") == 4
        self.pieces, self.joined, self.other, self.results = [], {}, {}, []

    def slot(self, piece, seen):
        number = len(self.pieces)
        shape = None if piece is None else piece.shape
        piece = None if piece is None else piece.reshape(-1, 128)
        self.pieces.append(piece)
        if not self.line:
            if piece is not None:
                total = lax.psum(piece, "tensor")
                self.results.append((total, total))
            return seen
        sent = []
        pairs, operand = [], None
        if piece is not None:
            operand = after(piece, seen)
            pairs += [(0, 1), (3, 2)]
        done = self.pieces[number - 2] if number >= 2 else None
        if done is not None:
            other = after(self.other[number - 2], (seen, self.inward))
            settled = (self.joined[number - 2] + other.astype(f32)).astype(bf16)
            if operand is None:
                operand = settled
            else:
                settled = jnp.pad(settled, ((0, operand.shape[0] - settled.shape[0]), (0, 0)))
                operand = jnp.where(self.middle, settled, operand)
            pairs += [(1, 0), (2, 3)]
        if number >= 1 and self.pieces[number - 1] is not None:
            inward = after(self.inward, seen).astype(f32)
            joined = (self.pieces[number - 1].astype(f32) + inward).astype(bf16)
            self.joined[number - 1] = joined.astype(f32)
            self.other[number - 1] = lax.ppermute(joined, "tensor", [(1, 2), (2, 1)])
            sent.append(joined)
        if operand is not None:
            self.inward = lax.ppermute(operand, "tensor", pairs)
            sent.append(operand)
        if done is not None:
            self.results.append((operand, self.inward))
        return tuple(sent)


def scatter_blocks(blocks, by_rows):
    if is_cube():
        return lax.psum_scatter(blocks, "dp", scatter_dimension=0, tiled=True)[0].astype(f32)
    if by_rows:
        full = blocks.reshape(-1, blocks.shape[2])
        return lax.psum_scatter(full, "dp", scatter_dimension=0, tiled=True).astype(f32)
    full = blocks.transpose(1, 0, 2).reshape(blocks.shape[1], -1)
    return lax.psum_scatter(full, "dp", scatter_dimension=1, tiled=True).astype(f32)


def ring(value, step):
    count = lax.axis_size("dp")
    pairs = [(i, i + step) for i in range(count) if 0 <= i + step < count]
    return lax.ppermute(value, "dp", pairs)


def locate(token_index, lengths, prefix):
    ends = jnp.cumsum(lengths)
    starts = ends - lengths
    inside = (token_index[:, None] >= starts[None, :]) & (token_index[:, None] < ends[None, :])
    begin = jnp.sum(jnp.where(inside, starts[None, :], 0), axis=1)
    limit = jnp.sum(jnp.where(inside, jnp.minimum(prefix, lengths)[None, :], 0), axis=1)
    return begin, limit


def rotary_tables(places):
    lane = jnp.arange(128, dtype=jnp.int32)
    exponents = (lane % (ROT // 2)).astype(f32) * (2.0 / ROT)
    angles = places.astype(f32)[:, None] * jnp.exp(exponents * -math.log(10000.0))[None, :]
    turned = (lane < ROT)[None, :]
    sign = jnp.where(lane < ROT // 2, -1.0, 1.0)[None, :]
    return jnp.where(turned, jnp.cos(angles), 1.0), jnp.where(turned, jnp.sin(angles) * sign, 0.0)


def on_device(
    tokens,
    project_weight,
    project_bias,
    dense_weight,
    dense_bias,
    expand_weight,
    expand_bias,
    shrink_weight,
    shrink_bias,
    first_gain,
    first_shift,
    second_gain,
    second_shift,
    lengths,
    prefix,
    upstream,
):
    rows, width = tokens.shape
    count = lax.axis_size("dp")
    me = lax.axis_index("dp")
    heads = project_bias.shape[0]
    places = natural_places()
    cube = is_cube()
    line = lax.axis_index("tensor")
    middle = ((line == 1) | (line == 2)).astype(jnp.int32).reshape(1)

    turned_width, hidden_width = dense_weight.shape[0], shrink_weight.shape[0]
    vectors = [first_gain, first_shift, second_gain, second_shift, dense_bias, shrink_bias]
    if cube:
        own = jnp.concatenate([v.reshape(-1).astype(bf16) for v in (*vectors, expand_bias, project_bias)])
        own = jnp.pad(own, (0, -own.size % 2048)).reshape(-1, 128)
        gathered = lax.all_gather(own, "dp", axis=0).reshape(count, -1)
        small = jnp.take(gathered, places, axis=0).astype(f32)
        wide = vectors[0].shape[0]
        rows_of = jnp.stack([small[:, k * wide : (k + 1) * wide].reshape(-1) for k in range(len(vectors))])
        at = len(vectors) * wide
        small = gathered.astype(f32)
        split = at + expand_bias.size
        full_expand_bias = small[:, at:split].reshape((count,) + expand_bias.shape).transpose(1, 0, 2).reshape(1, -1)
        full_project_bias = small[:, split : split + project_bias.size].reshape((count,) + project_bias.shape).transpose(1, 0, 2).reshape(1, -1)
    else:
        gathered = lax.all_gather(jnp.stack(vectors).astype(bf16), "dp", axis=1, tiled=True)
        rows_of = gathered.astype(f32)
        full_expand_bias = lax.all_gather(expand_bias.astype(bf16), "dp", axis=1, tiled=True).astype(f32).reshape(1, -1)
        full_project_bias = lax.all_gather(project_bias.astype(bf16), "dp", axis=1, tiled=True).astype(f32).reshape(1, -1)
    gains = jnp.concatenate([rows_of[:4], jnp.zeros((4, width), f32)], axis=0)
    bias_total = rows_of[4:5] + rows_of[5:6]

    def halved(vector, bit):
        keep = vector.shape[0] // 2
        return vector[:keep] + swap(vector[keep:], bit)

    def vector_parts(sums, grad_bias, expand_bias_sums, project_bias_sums):
        norms = sums[:4].reshape(4, BLOCKS, BLOCK).transpose(1, 0, 2).reshape(BLOCKS, -1)
        bias = grad_bias[0].reshape(BLOCKS, BLOCK)
        per_head = lambda v, like: v.reshape(heads, BLOCKS, like.shape[1]).transpose(1, 0, 2).reshape(BLOCKS, -1)
        heads_part = jnp.concatenate(
            [per_head(expand_bias_sums, expand_bias), per_head(project_bias_sums, project_bias)], axis=1
        )
        heads_part = jnp.take(heads_part, places, axis=0)
        return jnp.concatenate([norms, bias, heads_part], axis=1)

    token_index = me * rows + jnp.arange(rows, dtype=jnp.int32)
    begin, limit = locate(token_index, lengths, prefix)
    base = me * rows - SEQ_MAX
    low = begin - base
    high = jnp.maximum(token_index, begin + limit - 1) - base
    cos, sin = rotary_tables(token_index - begin)

    spread_project = Spread(project_weight.astype(bf16), True)
    seen_project = spread_project.first()
    seen_project_too = spread_project.second(seen_project, gathered)
    spread_expand = Spread(after(expand_weight.astype(bf16), (gathered, seen_project)), True)
    seen_expand = spread_expand.first()
    project_a, project_b = spread_project.join(seen_project_too)
    tok, one_a, one_b, two_a, two_b, up_a, up_b, mean, inverse, grad_bias = norm(
        places, tokens, upstream, after(gains, project_a)
    )
    seen_expand_too = spread_expand.second(seen_expand, project_a)
    queries, pairs = project(after(one_a, seen_expand), one_b, project_a, project_b, full_project_bias, cos, sin)
    sent = after(pairs, seen_expand_too)
    left = ring(sent, 1)
    right = ring(sent[:PREFIX_MAX], -1)
    spread_expand.begin_parts(seen_expand_too)
    expand_mine, expand_theirs = spread_expand.parts(pairs)
    down_weight = jnp.concatenate([dense_weight.astype(bf16), shrink_weight.astype(bf16)], axis=0)
    spread_down = Spread(after(down_weight, (mean, seen_project)), False)
    active, slope = expand(after(two_a, sent), two_b, expand_mine + expand_theirs, full_expand_bias)
    depth = turned_width + hidden_width
    column_blocks = column_grad(places, active, up_a, up_b, depth, turned_width)
    blocks = [spread_down.pair(0, active)] if cube else []
    spread_down.weight = after(spread_down.weight, (left, active))
    seen_down = spread_down.first()
    if not cube:
        blocks = [spread_down.pair(0)]
    attended, lse = attend(after(queries, column_blocks), left, pairs, right, low, high)

    line = LineSum(middle)
    seen_down_too = spread_down.second(seen_down, attended)
    blocks += [spread_down.pair(place, (attended, seen_down)) for place in range(len(blocks), HALF - 1)]
    pieces = [branch_piece(attended, active, *blocks[0])]
    seen = line.slot(pieces[0], ())
    column_blocks = column_grad(places, after(attended, (pieces[0], seen)), up_a, up_b, depth, 0, column_blocks)
    blocks.append(spread_down.pair(3, (column_blocks, seen_down_too)))
    down_blocks = [b for b, _ in blocks] + [b for _, b in blocks]
    grad_attended = back(after(up_a, column_blocks), up_b, down_blocks, 0, turned_width)
    dq, dleft, down, dright = attend_back(
        queries, left, pairs, right, low, high, lse, attended, grad_attended, cos, sin
    )
    later = ring(dleft, -1)
    earlier = ring(dright, 1)
    last = dq
    for place in (1, 2, 3):
        pieces.append(branch_piece(after(attended, last), active, *blocks[place]))
        last = pieces[-1]
        if place == 1:
            seen = line.slot(pieces[1], last)
            last = (last, seen)
    grad_hidden, expand_bias_sums = back(
        after(up_a, pieces[-1]), up_b, down_blocks, turned_width, hidden_width, slope
    )
    column_blocks, later, earlier, grad_hidden = lax.optimization_barrier((column_blocks, later, earlier, grad_hidden))
    grad_down = scatter_blocks(column_blocks, False)
    seen = line.slot(pieces[2], grad_hidden)
    grad_second = second_back(after(grad_hidden, seen), expand_mine + expand_theirs)
    grad_mixed, project_bias_sums = mix(after(dq, grad_second), down, later, earlier, cos, sin)
    seen = line.slot(pieces[3], grad_mixed)
    *tails, sums = input_back(
        after(grad_mixed, seen), project_a, project_b, grad_second, tok, mean, inverse, gains, 0
    )
    seen = line.slot(tails[0], sums)
    *more, part = input_back(
        after(grad_mixed, (sums, seen)), project_a, project_b, grad_second, tok, mean, inverse, gains, 2
    )
    tails += more
    sums = sums + part
    seen = line.slot(tails[1], part)
    widths = grad_hidden.shape[1], grad_mixed.shape[1]
    row_blocks = row_grad(places, two_a, two_b, after(grad_hidden, seen), sum(widths))
    vector = part
    if cube:
        vector = after(vector_parts(sums, grad_bias, expand_bias_sums, project_bias_sums), seen)
        vector = halved(halved(vector, CORE), ALONG_Y)
        vector = halved(after(vector, row_blocks), ALONG_X)[0]
    seen = line.slot(tails[2], row_blocks)
    row_blocks = row_grad(places, one_a, one_b, after(grad_mixed, seen), sum(widths), widths[0], row_blocks)
    row_blocks, grad_down, vector = lax.optimization_barrier((row_blocks, grad_down, vector))
    if cube:
        grad_rows = scatter_blocks(row_blocks, True)
        grad_expand, grad_project = grad_rows[:, : widths[0]], grad_rows[:, widths[0] :]
    else:
        grad_expand = scatter_blocks(row_blocks[:, :, : widths[0]], True)
        grad_project = scatter_blocks(row_blocks[:, :, widths[0] :], True)
    settled, passed = zip(*line.results[:4])
    output = output_sum(places, middle, after(bias_total, (row_blocks, seen)), settled, passed, tokens)
    tail = tails[3]
    if cube:
        norms = vector[: 4 * BLOCK].astype(bf16).reshape(-1, 128)
        tail = jnp.concatenate([tail.reshape(-1, 128), norms, jnp.zeros_like(norms)], axis=0)
    seen = line.slot(tail, output)
    tokens_grad = tokens_sum(places, middle, upstream, *line.results[4], 0, after(up_a, (output, seen)))
    seen = line.slot(None, tokens_grad)
    tokens_grad = tokens_sum(places, middle, upstream, *line.results[5], 1, after(tokens_grad, seen))
    line.slot(None, tokens_grad)
    for number in range(2, 4):
        tokens_grad = tokens_sum(places, middle, upstream, *line.results[4 + number], number, tokens_grad)
    grad_dense, grad_shrink = grad_down[:turned_width], grad_down[turned_width:]

    if cube:
        settled, passed = line.results[7]
        norms = jnp.where(middle[0] == 1, settled[-16:-8], passed[-16:-8]).astype(f32).reshape(4, BLOCK)
        at = 5 * BLOCK
        bias = vector[4 * BLOCK : at]
        expand_bias_grad = vector[at : at + expand_bias.size].reshape(expand_bias.shape)
        project_bias_grad = vector[at + expand_bias.size :].reshape(project_bias.shape)
    else:
        norms = lax.psum(lax.psum_scatter(sums[:4], "dp", scatter_dimension=1, tiled=True), "tensor")
        bias = lax.psum_scatter(grad_bias[0], "dp", scatter_dimension=0, tiled=True)
        split = lambda v: lax.psum_scatter(v.reshape(heads, -1), "dp", scatter_dimension=1, tiled=True)
        expand_bias_grad, project_bias_grad = split(expand_bias_sums), split(project_bias_sums)
    return (
        output,
        tokens_grad,
        grad_project,
        project_bias_grad,
        grad_dense,
        bias,
        grad_expand,
        expand_bias_grad,
        grad_shrink,
        bias,
        norms[0],
        norms[1],
        norms[2],
        norms[3],
    )


def solution(mesh):
    placed = (
        P("dp", None),
        P("dp", "tensor"),
        P("tensor", "dp"),
        P("tensor", "dp"),
        P("dp"),
        P("dp", "tensor"),
        P("tensor", "dp"),
        P("tensor", "dp"),
        P("dp"),
        P("dp"),
        P("dp"),
        P("dp"),
        P("dp"),
        P(),
        P(),
        P("dp", None),
    )
    return jax.shard_map(
        on_device,
        mesh=mesh,
        in_specs=placed,
        out_specs=(
            P("dp", None),
            P("dp", None),
            P("dp", "tensor"),
            P("tensor", "dp"),
            P("tensor", "dp"),
            P("dp"),
            P("dp", "tensor"),
            P("tensor", "dp"),
            P("tensor", "dp"),
            P("dp"),
            P("dp"),
            P("dp"),
            P("dp"),
            P("dp"),
        ),
        check_vma=False,
    )
```

```python
import functools
import math

import jax
import jax.numpy as jnp
from jax import lax
from jax.experimental import pallas as pl
from jax.experimental.pallas import tpu as pltpu
from jax.sharding import PartitionSpec as P

HD = 256
ROT = 64
SEQ_MAX = 1024
PREFIX_MAX = 512
BLOCK = 256
BLOCKS = 8
HALF = 4
EPSILON = 1e-05
MASKED = -1e30
bf16 = jnp.bfloat16
f32 = jnp.float32
NN = (((1,), (0,)), ((), ()))
NT = (((1,), (1,)), ((), ()))
TN = (((0,), (0,)), ((), ()))
VMEM_BYTES = 56 * 2**20


def mul(a, b, dims=NN):
    return lax.dot_general(a, b, dims, preferred_element_type=f32)


def params(**more):
    return pltpu.CompilerParams(vmem_limit_bytes=VMEM_BYTES, **more)


def cost(flops, moved, transcendentals=0):
    return pl.CostEstimate(flops=flops, bytes_accessed=moved, transcendentals=transcendentals)


def whole_spec(array):
    zeros = (0,) * array.ndim
    return pl.BlockSpec(array.shape, lambda *_: zeros)


def swap(value, bit):
    count = lax.axis_size("dp")
    return lax.ppermute(value, "dp", [(i, i ^ bit) for i in range(count)])


CORE, ALONG_X, ALONG_Y = 1, 2, 4


def is_cube():
    return lax.axis_size("dp") == BLOCKS


def natural_places():
    place = jnp.arange(BLOCKS, dtype=jnp.int32)
    if not is_cube():
        return place
    owner = ((place >> 2) & 1) * CORE + ((place >> 1) & 1) * ALONG_Y + (place & 1) * ALONG_X
    return owner ^ lax.axis_index("dp")


class Spread:
    def __init__(self, weight, by_rows):
        self.weight, self.by_rows = weight, by_rows

    def first(self):
        if is_cube():
            self.from_x = swap(self.weight, ALONG_X)
            self.from_y = swap(self.weight, ALONG_Y)
            return self.from_x, self.from_y
        self.full = lax.all_gather(self.weight, "dp", axis=0 if self.by_rows else 1, tiled=True)
        return (self.full,)

    def second(self, *seen):
        if is_cube():
            half = self.weight.shape[0] // 2
            self.over_x = swap(after(self.from_x[:half], seen), ALONG_Y)
            self.over_y = swap(after(self.from_y[half:], seen), ALONG_X)
            return self.over_x, self.over_y
        return (self.full,)

    def join(self, *seen):
        if is_cube():
            parts = [self.weight, self.from_x, self.from_y, self.over_x, self.over_y]
            mine = jnp.concatenate(after(parts, seen), axis=0)
            return mine, swap(mine, CORE)
        half = self.full.shape[0] // 2
        return self.full[:half], self.full[half:]

    def begin_parts(self, *seen):
        if is_cube():
            self.near = [swap(after(part, seen), CORE) for part in (self.weight, self.from_x, self.from_y)]

    def parts(self, *seen):
        if is_cube():
            far = [swap(after(part, seen), CORE) for part in (self.over_x, self.over_y)]
            return [self.weight, self.from_x, self.from_y, self.over_x, self.over_y], self.near + far
        half = self.full.shape[0] // 2
        return [self.full[:half]], [self.full[half:]]

    def pair(self, place, seen=()):
        if is_cube():
            if place == 3:
                mine = jnp.concatenate([self.over_x, self.over_y], axis=0)
            else:
                mine = self.weight if place == 0 else (self.from_x, self.from_y)[place - 1]
            return mine, swap(after(mine, seen), CORE)
        blocks = self.full.reshape(self.full.shape[0], BLOCKS, -1)
        return blocks[:, place], blocks[:, place + HALF]


def after(value, seen):
    return lax.optimization_barrier((value, seen))[0]


def norm_kernel(places, tokens, upstream, gains, tok, one_a, one_b, two_a, two_b, up_a, up_b, mean, inverse, grad_bias):
    values = tokens[...].astype(f32)
    average = jnp.mean(values, axis=1, keepdims=True)
    center = values - average
    scale = lax.rsqrt(jnp.mean(center * center, axis=1, keepdims=True) + EPSILON)
    mean[...] = average
    inverse[...] = scale

    @pl.when(pl.program_id(0) == 0)
    def _():
        grad_bias[...] = jnp.zeros_like(grad_bias)

    for place in range(BLOCKS):
        from_ = pl.ds(pl.multiple_of(places[place] * BLOCK, BLOCK), BLOCK)
        to = pl.ds(place * BLOCK, BLOCK)
        inner = pl.ds(place % HALF * BLOCK, BLOCK)
        first, second, up = (one_a, two_a, up_a) if place < HALF else (one_b, two_b, up_b)
        low = tokens[:, from_]
        tok[:, to] = low
        normed = (low.astype(f32) - average) * scale
        first[:, inner] = (normed * gains[0:1, to] + gains[1:2, to]).astype(bf16)
        second[:, inner] = (normed * gains[2:3, to] + gains[3:4, to]).astype(bf16)
        grad = upstream[:, from_]
        up[:, inner] = grad
        grad_bias[0:1, to] += jnp.sum(grad.astype(f32), axis=0, keepdims=True)


def norm(places, tokens, upstream, gains, tile=256):
    rows, width = tokens.shape
    row = lambda w: pl.BlockSpec((tile, w), lambda i, *_: (i, 0))
    shape = lambda w, kind: jax.ShapeDtypeStruct((rows, w), kind)
    half = width // 2
    return pl.pallas_call(
        norm_kernel,
        grid_spec=pltpu.PrefetchScalarGridSpec(
            num_scalar_prefetch=1,
            grid=(rows // tile,),
            in_specs=[row(width), row(width), whole_spec(gains)],
            out_specs=[row(width)] + [row(half)] * 6 + [row(1), row(1), pl.BlockSpec((8, width), lambda *_: (0, 0))],
        ),
        out_shape=[shape(width, bf16)]
        + [shape(half, bf16)] * 6
        + [shape(1, f32), shape(1, f32), jax.ShapeDtypeStruct((8, width), f32)],
        compiler_params=params(),
        cost_estimate=cost(20 * rows * width, 20 * rows * width),
        name="norm",
    )(places, tokens, upstream, gains)


def turn(part, cos, sin, sign):
    lane = lax.broadcasted_iota(jnp.int32, part.shape, 1)
    partner = jnp.where(lane < ROT // 2, pltpu.roll(part, 128 - ROT // 2, 1), pltpu.roll(part, ROT // 2, 1))
    if sign > 0:
        return part * cos + partner * sin
    return part * cos - partner * sin


def project_kernel(one_a, one_b, w_a, w_b, bias, cos, sin, queries, pairs):
    for part in range(3):
        at = slice(part * HD, (part + 1) * HD)
        mixed = mul(one_a[...], w_a[:, at]) + mul(one_b[...], w_b[:, at]) + bias[:, at]
        if part < 2:
            ref, to = (queries, 0) if part == 0 else (pairs, 0)
            ref[:, to : to + 128] = turn(mixed[:, :128], cos[...], sin[...], 1).astype(bf16)
            ref[:, to + 128 : to + HD] = mixed[:, 128:].astype(bf16)
        else:
            pairs[:, HD:] = mixed.astype(bf16)


def project(one_a, one_b, w_a, w_b, bias, cos, sin):
    rows, half = one_a.shape
    heads = w_a.shape[1] // (3 * HD)
    weight = pl.BlockSpec((half, 3 * HD), lambda h: (0, h))
    return pl.pallas_call(
        project_kernel,
        grid=(heads,),
        in_specs=[
            whole_spec(one_a),
            whole_spec(one_b),
            weight,
            weight,
            pl.BlockSpec((1, 3 * HD), lambda h: (0, h)),
            whole_spec(cos),
            whole_spec(sin),
        ],
        out_specs=[pl.BlockSpec((rows, HD), lambda h: (0, h)), pl.BlockSpec((rows, 2 * HD), lambda h: (0, h))],
        out_shape=[
            jax.ShapeDtypeStruct((rows, heads * HD), bf16),
            jax.ShapeDtypeStruct((rows, heads * 2 * HD), bf16),
        ],
        compiler_params=params(),
        cost_estimate=cost(4 * rows * half * w_a.shape[1], 14_000_000),
        name="project",
    )(one_a, one_b, w_a, w_b, bias, cos, sin)


def lay(parts, joined):
    at = 0
    for part in parts:
        joined[at : at + part.shape[0], :] = part[...]
        at += part.shape[0]


def expand_kernel(two_a, two_b, bias, *refs):
    *parts, active, slope, weight = refs
    lay(parts, weight)
    rows, half = two_a.shape
    for start in range(0, rows, 512):
        at = slice(start, start + 512)
        hidden = mul(two_a[at], weight[:half]) + mul(two_b[at], weight[half:]) + bias[...]
        below = 0.5 + 0.5 * lax.erf(hidden * (0.5**0.5))
        density = jnp.exp(hidden * hidden * -0.5) * (1.0 / math.sqrt(2.0 * math.pi))
        active[at] = (hidden * below).astype(bf16)
        slope[at] = (below + hidden * density).astype(bf16)


def expand(two_a, two_b, parts, bias, tile=512):
    rows, half = two_a.shape
    width = parts[0].shape[1]
    column = lambda r: pl.BlockSpec((r, tile), lambda n: (0, n))
    return pl.pallas_call(
        expand_kernel,
        grid=(width // tile,),
        in_specs=[whole_spec(two_a), whole_spec(two_b), column(1)] + [column(part.shape[0]) for part in parts],
        out_specs=[column(rows), column(rows)],
        out_shape=[jax.ShapeDtypeStruct((rows, width), bf16)] * 2,
        scratch_shapes=[pltpu.VMEM((2 * half, tile), bf16)],
        compiler_params=params(),
        cost_estimate=cost(0, 0),
        name="expand",
    )(two_a, two_b, bias, *parts)


def branch_kernel(attended, active, dense_a, dense_b, mine, theirs, out):
    slabs = BLOCK // 128
    for number, (dense, weight) in enumerate(((dense_a, mine), (dense_b, theirs))):
        full = mul(active[...], weight[...])
        for at in range(0, attended.shape[1], BLOCK):
            full = full + mul(attended[:, at : at + BLOCK], dense[:, at : at + BLOCK])
        full = full.astype(bf16)
        for slab in range(slabs):
            out[number * slabs + slab] = full[:, slab * 128 : (slab + 1) * 128]


def branch_piece(attended, active, w_a, w_b, pair, place, tile=512):
    rows, turned = attended.shape
    slabs = 2 * BLOCK // 128
    row = lambda a: pl.BlockSpec((tile, a.shape[1]), lambda i: (i, 0))
    dense = pl.BlockSpec((BLOCK, turned), lambda i: (place, w_a.shape[1] // turned - 1))
    return pl.pallas_call(
        branch_kernel,
        grid=(rows // tile,),
        in_specs=[row(attended), row(active), dense, dense, whole_spec(pair[0]), whole_spec(pair[1])],
        out_specs=pl.BlockSpec((slabs, tile, 128), lambda i: (0, i, 0)),
        out_shape=jax.ShapeDtypeStruct((slabs, rows, 128), bf16),
        compiler_params=params(),
        cost_estimate=cost(0, 0),
        name="branch",
    )(attended, active, w_a, w_b, *pair)


def dense_kernel(up_a, up_b, w_a, w_b, out, joined):
    for place in range(BLOCKS):
        ref = w_a if place < HALF else w_b
        rows = slice(place % HALF * BLOCK, (place % HALF + 1) * BLOCK)
        for at in range(0, out.shape[1], BLOCK):
            joined[at : at + BLOCK, place * BLOCK : (place + 1) * BLOCK] = ref[rows, at : at + BLOCK]
    half = up_a.shape[1]
    for start in range(0, out.shape[0], 512):
        at = slice(start, start + 512)
        out[at] = (mul(up_a[at], joined[:, :half], NT) + mul(up_b[at], joined[:, half:], NT)).astype(bf16)


def dense_back(up_a, up_b, w_a, w_b, turned):
    rows, half = up_a.shape
    dense = pl.BlockSpec((half, turned), lambda i: (0, w_a.shape[1] // turned - 1))
    return pl.pallas_call(
        dense_kernel,
        grid=(1,),
        in_specs=[whole_spec(up_a), whole_spec(up_b), dense, dense],
        out_specs=pl.BlockSpec((rows, turned), lambda i: (0, 0)),
        out_shape=jax.ShapeDtypeStruct((rows, turned), bf16),
        scratch_shapes=[pltpu.VMEM((turned, 2 * half), bf16)],
        compiler_params=params(),
        cost_estimate=cost(0, 0),
        name="dense_back",
    )(up_a, up_b, w_a, w_b)


def back_kernel(up_a, up_b, blocks, slope, out, sums, joined):
    for place in range(BLOCKS):
        joined[:, place * BLOCK : (place + 1) * BLOCK] = blocks[place][...]
    half = HALF * BLOCK
    total = jnp.zeros((1, out.shape[1]), f32)
    for start in range(0, out.shape[0], 512):
        at = slice(start, start + 512)
        grad = mul(up_a[at], joined[:, :half], NT) + mul(up_b[at], joined[:, half:], NT)
        if slope is not None:
            grad = grad * slope[at].astype(f32)
        grad = grad.astype(bf16)
        out[at] = grad
        if sums is not None:
            total = total + jnp.sum(grad.astype(f32), axis=0, keepdims=True)
    if sums is not None:
        sums[...] = total


def back(up_a, up_b, blocks, start, width, slope=None, tile=512):
    rows, half = up_a.shape
    weight = pl.BlockSpec((tile, BLOCK), lambda n: (n + start // tile, 0))
    column = lambda r: pl.BlockSpec((r, tile), lambda n: (0, n))
    scaled = slope is not None

    def body(a, b, *rest):
        blocks, rest = rest[:BLOCKS], rest[BLOCKS:]
        if scaled:
            s, out, sums, joined = rest
        else:
            (out, joined), s, sums = rest, None, None
        back_kernel(a, b, blocks, s, out, sums, joined)

    out = jax.ShapeDtypeStruct((rows, width), bf16)
    return pl.pallas_call(
        body,
        grid=(width // tile,),
        in_specs=[whole_spec(up_a), whole_spec(up_b)] + [weight] * BLOCKS + [column(rows)] * scaled,
        out_specs=[column(rows), column(1)] if scaled else column(rows),
        out_shape=[out, jax.ShapeDtypeStruct((1, width), f32)] if scaled else out,
        scratch_shapes=[pltpu.VMEM((tile, 2 * half), bf16)],
        compiler_params=params(),
        cost_estimate=cost(4 * rows * half * width, 4 * rows * half + 4 * half * width + 4 * rows * width),
        name="back",
    )(up_a, up_b, *blocks, *([slope] if scaled else []))


def second_kernel(grad, *refs):
    count = len(refs) - 3
    parts, out, weight, arrived = refs[:count], *refs[count:]
    tile = out.shape[1]
    step = pl.program_id(0)
    copies, ends, at = [], [], 0
    for number, part in enumerate(parts):
        to = weight.at[at : at + part.shape[0]]
        copies.append(pltpu.make_async_copy(part, to, arrived.at[number]))
        at += part.shape[0]
        ends.append(at)

    @pl.when(step == 0)
    def _():
        for copy in copies:
            copy.start()

    for number in range(weight.shape[0] // tile):

        @pl.when(step == number)
        def _(number=number):
            before = 0
            for copy, end in zip(copies, ends):
                last_needed_at = before // tile
                if last_needed_at == number:
                    copy.wait()
                before = end

    rows = pl.ds(pl.multiple_of(step * tile, tile), tile)
    out[...] = mul(grad[...], weight[rows], NT).astype(bf16)


def second_back(grad, parts, tile=512):
    rows, width = grad.shape
    depth = sum(part.shape[0] for part in parts)
    return pl.pallas_call(
        second_kernel,
        grid=(depth // tile,),
        in_specs=[whole_spec(grad)] + [pl.BlockSpec(memory_space=pl.ANY)] * len(parts),
        out_specs=pl.BlockSpec((rows, tile), lambda n: (0, n)),
        out_shape=jax.ShapeDtypeStruct((rows, depth), bf16),
        scratch_shapes=[pltpu.VMEM((depth, width), bf16), pltpu.SemaphoreType.DMA((len(parts),))],
        compiler_params=params(),
        cost_estimate=cost(2 * rows * depth * width, 2 * (rows + depth) * width + 2 * rows * depth),
        name="second_back",
    )(grad, *parts)


def row_grad_kernel(where, left_a, left_b, right, *rest):
    out = rest[-1]
    for number, left in enumerate((left_a, left_b)):
        full = mul(left[...], right[...], TN)
        for place in range(HALF):
            out[where[number * HALF + place]] = full[place * BLOCK : (place + 1) * BLOCK].astype(bf16)


def row_grad(where, left_a, left_b, right, total, start=0, into=None, tile=512):
    rows, width = right.shape
    blocks = 2 * HALF
    extra = [] if into is None else [into]
    return pl.pallas_call(
        row_grad_kernel,
        grid_spec=pltpu.PrefetchScalarGridSpec(
            num_scalar_prefetch=1,
            grid=(width // tile,),
            in_specs=[whole_spec(left_a), whole_spec(left_b), pl.BlockSpec((rows, tile), lambda n, *_: (0, n))]
            + [pl.BlockSpec(memory_space=pl.ANY)] * len(extra),
            out_specs=pl.BlockSpec((blocks, BLOCK, tile), lambda n, *_: (0, 0, n + start // tile)),
        ),
        out_shape=jax.ShapeDtypeStruct((blocks, BLOCK, total), bf16),
        input_output_aliases={4: 0} if extra else {},
        compiler_params=params(),
        cost_estimate=cost(2 * rows * blocks * BLOCK * width, 2 * blocks * BLOCK * (rows + width) + 2 * rows * width),
        name="row_grad",
    )(where, left_a, left_b, right, *extra)


def column_grad_kernel(where, left, right_a, right_b, *rest):
    out = rest[-1]
    for number, right in enumerate((right_a, right_b)):
        full = mul(left[...], right[...], TN)
        for place in range(HALF):
            out[where[number * HALF + place]] = full[:, place * BLOCK : (place + 1) * BLOCK].astype(bf16)


def column_grad(where, left, right_a, right_b, total, start=0, into=None, tile=512):
    rows, width = left.shape
    blocks = 2 * HALF
    extra = [] if into is None else [into]
    return pl.pallas_call(
        column_grad_kernel,
        grid_spec=pltpu.PrefetchScalarGridSpec(
            num_scalar_prefetch=1,
            grid=(width // tile,),
            in_specs=[pl.BlockSpec((rows, tile), lambda n, *_: (0, n)), whole_spec(right_a), whole_spec(right_b)]
            + [pl.BlockSpec(memory_space=pl.ANY)] * len(extra),
            out_specs=pl.BlockSpec((blocks, tile, BLOCK), lambda n, *_: (0, n + start // tile, 0)),
        ),
        out_shape=jax.ShapeDtypeStruct((blocks, total, BLOCK), bf16),
        input_output_aliases={4: 0} if extra else {},
        compiler_params=params(),
        cost_estimate=cost(0, 0),
        name="column_grad",
    )(where, left, right_a, right_b, *extra)


def fill(refs, heads, place):
    for head in range(heads):
        at = 0
        for ref in refs:
            for start in range(0, ref.shape[0], 512):
                rows = slice(start, start + 512)
                place(head, at, ref[rows, 2 * head * HD : (2 * head + 1) * HD], ref[rows, (2 * head + 1) * HD : (2 * head + 2) * HD])
                at += 512


def attend_kernel(first, last, q, left, own, right, low, high, out, lse, keys, values_turned, *, wide):
    step = pl.program_id(0)
    tall = q.shape[0]
    heads = range(keys.shape[0])

    @pl.when(step == 0)
    def _():
        def place(head, at, k, v):
            keys[head, at : at + 512, :] = k
            values_turned[head, :, at : at + 512] = jnp.transpose(v)

        fill((left, own, right), len(heads), place)

    scaled = [q[:, h * HD : (h + 1) * HD] * jnp.asarray(HD**-0.5, bf16) for h in heads]
    low_row = low[...]
    high_row = high[...]

    def block(j, carry):
        rows = pl.ds(pl.multiple_of(j * wide, wide), wide)
        key = j * wide + lax.broadcasted_iota(jnp.int32, (wide, tall), 0)
        seen = (key >= low_row) & (key <= high_row)
        scores = [mul(keys[h, rows, :], scaled[h], NT) for h in heads]
        after_block = []
        for h in heads:
            top, total, acc = carry[h]
            masked = jnp.where(seen, scores[h], MASKED)
            new = jnp.maximum(top, jnp.max(masked, axis=0, keepdims=True))
            weights = jnp.exp(masked - new)
            fade = jnp.exp(top - new)
            total = total * fade + jnp.sum(weights, axis=0, keepdims=True)
            acc = acc * fade + mul(values_turned[h, :, rows], weights.astype(bf16))
            after_block.append((new, total, acc))
        return tuple(after_block)

    start = (jnp.full((1, tall), MASKED, f32), jnp.zeros((1, tall), f32), jnp.zeros((HD, tall), f32))
    done = lax.fori_loop(first[step], last[step] + 1, block, tuple(start for _ in heads))
    for h in heads:
        top, total, acc = done[h]
        out[:, h * HD : (h + 1) * HD] = jnp.transpose(acc / total).astype(bf16)
        lse[h] = top + jnp.log(total)


def key_blocks(low, high, tall, wide):
    return jnp.min(low.reshape(-1, tall), axis=1) // wide, jnp.max(high.reshape(-1, tall), axis=1) // wide


def attend(q, left, own, right, low, high, tall=256, wide=512):
    rows, width = q.shape
    heads = width // HD
    extent = left.shape[0] + rows + right.shape[0]
    row = pl.BlockSpec((1, tall), lambda i, *_: (0, i))
    mine = pl.BlockSpec((tall, width), lambda i, *_: (i, 0))
    return pl.pallas_call(
        functools.partial(attend_kernel, wide=wide),
        grid_spec=pltpu.PrefetchScalarGridSpec(
            num_scalar_prefetch=2,
            grid=(rows // tall,),
            in_specs=[mine, whole_spec(left), whole_spec(own), whole_spec(right), row, row],
            out_specs=[mine, pl.BlockSpec((heads, 1, tall), lambda i, *_: (0, 0, i))],
            scratch_shapes=[pltpu.VMEM((heads, extent, HD), bf16), pltpu.VMEM((heads, HD, extent), bf16)],
        ),
        out_shape=[jax.ShapeDtypeStruct((rows, width), bf16), jax.ShapeDtypeStruct((heads, 1, rows), f32)],
        compiler_params=params(),
        cost_estimate=cost(8_000_000_000, 10_000_000, 3_000_000),
        name="attend",
    )(*key_blocks(low, high, tall, wide), q, left, own, right, low.reshape(1, rows), high.reshape(1, rows))


def attend_back_kernel(
    first, last, q, left, own, right, low, high, lse, attended, grad, cos, sin,
    dq, dleft, down, dright, keys, values, keys_turned, dk, dv, *, wide,
):
    step = pl.program_id(0)
    tall = q.shape[0]
    heads = range(keys.shape[0])

    @pl.when(step == 0)
    def _():
        def place(head, at, k, v):
            keys[head, at : at + 512, :] = k
            values[head, at : at + 512, :] = v
            keys_turned[head, :, at : at + 512] = jnp.transpose(k)

        fill((left, own, right), len(heads), place)
        dk[...] = jnp.zeros_like(dk)
        dv[...] = jnp.zeros_like(dv)

    cut = lambda ref, h: ref[:, h * HD : (h + 1) * HD]
    scaled = [cut(q, h) * jnp.asarray(HD**-0.5, bf16) for h in heads]
    given = [cut(grad, h) for h in heads]
    low_row = low[...]
    high_row = high[...]
    deltas = [
        jnp.sum(jnp.transpose(given[h].astype(f32) * cut(attended, h).astype(f32)), axis=0, keepdims=True) for h in heads
    ]

    def block(j, accs):
        rows = pl.ds(pl.multiple_of(j * wide, wide), wide)
        key = j * wide + lax.broadcasted_iota(jnp.int32, (wide, tall), 0)
        seen = (key >= low_row) & (key <= high_row)
        scores = [mul(keys[h, rows, :], scaled[h], NT) for h in heads]
        grad_probs = [mul(values[h, rows, :], given[h], NT) for h in heads]
        after_block = []
        for h in heads:
            probs = jnp.exp(jnp.where(seen, scores[h] - lse[h], MASKED))
            grad_scores = (probs * (grad_probs[h] - deltas[h])).astype(bf16)
            dv[h, rows, :] += mul(probs.astype(bf16), given[h])
            dk[h, rows, :] += mul(grad_scores, scaled[h])
            after_block.append(accs[h] + mul(keys_turned[h, :, rows], grad_scores))
        return tuple(after_block)

    accs = lax.fori_loop(first[step], last[step] + 1, block, tuple(jnp.zeros((HD, tall), f32) for _ in heads))
    for h in heads:
        full = jnp.transpose(accs[h]) * (HD**-0.5)
        dq[:, h * HD : h * HD + 128] = turn(full[:, :128], cos[...], sin[...], -1).astype(bf16)
        dq[:, h * HD + 128 : (h + 1) * HD] = full[:, 128:].astype(bf16)

    @pl.when(step == pl.num_programs(0) - 1)
    def _():
        for h in heads:
            at = 0
            for ref in (dleft, down, dright):
                count = ref.shape[0]
                ref[:, 2 * h * HD : (2 * h + 1) * HD] = dk[h, at : at + count, :].astype(ref.dtype)
                ref[:, (2 * h + 1) * HD : (2 * h + 2) * HD] = dv[h, at : at + count, :].astype(ref.dtype)
                at += count


def attend_back(q, left, own, right, low, high, lse, attended, grad, cos, sin, tall=256, wide=512):
    rows, width = q.shape
    heads = width // HD
    extent = left.shape[0] + rows + right.shape[0]
    row = pl.BlockSpec((1, tall), lambda i, *_: (0, i))
    mine = pl.BlockSpec((tall, width), lambda i, *_: (i, 0))
    table = pl.BlockSpec((tall, 128), lambda i, *_: (i, 0))
    return pl.pallas_call(
        functools.partial(attend_back_kernel, wide=wide),
        grid_spec=pltpu.PrefetchScalarGridSpec(
            num_scalar_prefetch=2,
            grid=(rows // tall,),
            in_specs=[
                mine, whole_spec(left), whole_spec(own), whole_spec(right), row, row,
                pl.BlockSpec((heads, 1, tall), lambda i, *_: (0, 0, i)), mine, mine, table, table,
            ],
            out_specs=[mine, whole_spec(left), whole_spec(own), whole_spec(right)],
            scratch_shapes=[
                pltpu.VMEM((heads, extent, HD), bf16),
                pltpu.VMEM((heads, extent, HD), bf16),
                pltpu.VMEM((heads, HD, extent), bf16),
                pltpu.VMEM((heads, extent, HD), f32),
                pltpu.VMEM((heads, extent, HD), f32),
            ],
        ),
        out_shape=[
            jax.ShapeDtypeStruct((rows, width), bf16),
            jax.ShapeDtypeStruct(left.shape, bf16),
            jax.ShapeDtypeStruct(own.shape, bf16),
            jax.ShapeDtypeStruct(right.shape, bf16),
        ],
        compiler_params=params(),
        cost_estimate=cost(16_000_000_000, 20_000_000, 3_000_000),
        name="attend_back",
    )(*key_blocks(low, high, tall, wide), q, left, own, right, low.reshape(1, rows), high.reshape(1, rows), lse, attended, grad, cos, sin)


def mixed_kernel(dq, own, later, earlier, cos, sin, out, sums):
    rows = dq.shape[0]
    near = earlier.shape[0]
    out[:, :HD] = dq[...]
    pairs = own[...].astype(f32) + later[...].astype(f32)
    top = pairs[:near] + earlier[...].astype(f32)
    for at, part in ((slice(0, near), top), (slice(near, rows), pairs[near:])):
        out[at, HD : HD + 128] = turn(part[:, :128], cos[at], sin[at], -1).astype(bf16)
        out[at, HD + 128 :] = part[:, 128:].astype(bf16)
    sums[...] = jnp.sum(out[...].astype(f32), axis=0, keepdims=True)


def mix(dq, own, later, earlier, cos, sin):
    rows, width = dq.shape
    heads = width // HD
    pair = lambda a: pl.BlockSpec((a.shape[0], 2 * HD), lambda h: (0, h))
    return pl.pallas_call(
        mixed_kernel,
        grid=(heads,),
        in_specs=[
            pl.BlockSpec((rows, HD), lambda h: (0, h)), pair(own), pair(later), pair(earlier),
            whole_spec(cos), whole_spec(sin),
        ],
        out_specs=[pl.BlockSpec((rows, 3 * HD), lambda h: (0, h)), pl.BlockSpec((1, 3 * HD), lambda h: (0, h))],
        out_shape=[
            jax.ShapeDtypeStruct((rows, 3 * width), bf16),
            jax.ShapeDtypeStruct((1, 3 * width), f32),
        ],
        compiler_params=params(),
        cost_estimate=cost(10_000_000, 14_000_000),
        name="mix",
    )(dq, own, later, earlier, cos, sin)


def input_kernel(mixed, w_a, w_b, second, tok, mean, inverse, gains, *outs):
    *outs, sums = outs
    step = pl.program_id(0)
    half = w_a.shape[0]
    grad_a = mul(mixed[...], w_a[...], NT)
    grad_b = mul(mixed[...], w_b[...], NT)
    scale = inverse[...]

    @pl.when(step == 0)
    def _():
        sums[...] = jnp.zeros_like(sums)

    pieces = []
    total = 0.0
    product = 0.0
    for number, grad in enumerate((grad_a, grad_b)):
        at = slice(number * half, (number + 1) * half)
        normed = (tok[:, at].astype(f32) - mean[...]) * scale
        other = second[:, at].astype(f32)
        both = grad * gains[0:1, at] + other * gains[2:3, at]
        sums[0:1, at] += jnp.sum(grad * normed, axis=0, keepdims=True)
        sums[1:2, at] += jnp.sum(grad, axis=0, keepdims=True)
        sums[2:3, at] += jnp.sum(other * normed, axis=0, keepdims=True)
        sums[3:4, at] += jnp.sum(other, axis=0, keepdims=True)
        total = total + jnp.sum(both, axis=1, keepdims=True)
        product = product + jnp.sum(both * normed, axis=1, keepdims=True)
        pieces.append((at, both, normed))
    total = total * (0.5 / half)
    product = product * (0.5 / half)

    def store(ref):
        for at, both, normed in pieces:
            grad = (scale * (both - total - normed * product)).astype(bf16)
            for slab in range(half // 128):
                ref[at.start // 128 + slab] = grad[:, slab * 128 : (slab + 1) * 128]

    if len(outs) == 1:
        store(outs[0])
    else:
        for number, ref in enumerate(outs):
            pl.when(step == number)(functools.partial(store, ref))


def input_back(mixed, w_a, w_b, second, tok, mean, inverse, gains, start, count, tile=256):
    width = tok.shape[1]
    depth = mixed.shape[1]
    row = lambda w: pl.BlockSpec((tile, w), lambda i: (i + start, 0))
    weight = pl.BlockSpec((w_a.shape[0], depth), lambda i: (0, 0))
    slabs = (width // 128, tile, 128)
    out = pl.BlockSpec(slabs, lambda i: (0, 0, 0))
    return pl.pallas_call(
        input_kernel,
        grid=(count,),
        in_specs=[
            row(depth), weight, weight, row(width), row(width), row(1), row(1), whole_spec(gains),
        ],
        out_specs=[out] * count + [pl.BlockSpec((8, width), lambda i: (0, 0))],
        out_shape=[jax.ShapeDtypeStruct(slabs, bf16)] * count + [jax.ShapeDtypeStruct((8, width), f32)],
        compiler_params=params(),
        cost_estimate=cost(2 * count * tile * depth * width, 14_000_000),
        name="input_back",
    )(mixed, w_a, w_b, second, tok, mean, inverse, gains)


def output_kernel(places, middle, tokens, bias, *refs):
    out = refs[-1]
    inside = middle[0] == 1
    for place in range(BLOCKS):
        settled, passed = refs[place % HALF], refs[HALF + place % HALF]
        for slab in range(BLOCK // 128):
            to = pl.ds(pl.multiple_of(places[place] * BLOCK + slab * 128, 128), 128)
            at = place // HALF * (BLOCK // 128) + slab
            total = jnp.where(inside, settled[at].astype(f32), passed[at].astype(f32))
            here = bias[0:1, place * BLOCK + slab * 128 : place * BLOCK + slab * 128 + 128]
            out[:, to] = (tokens[:, to].astype(f32) + total + here).astype(bf16)


def output_sum(places, middle, bias, settled, passed, tokens, tile=256):
    rows, width = tokens.shape
    row = lambda w: pl.BlockSpec((tile, w), lambda i, *_: (i, 0))
    slabs = pl.BlockSpec((width // 512, tile, 128), lambda i, *_: (0, i, 0))
    view = lambda a: a.reshape(width // 512, rows, 128)
    return pl.pallas_call(
        output_kernel,
        grid_spec=pltpu.PrefetchScalarGridSpec(
            num_scalar_prefetch=2,
            grid=(rows // tile,),
            in_specs=[row(width), whole_spec(bias)] + [slabs] * 8,
            out_specs=row(width),
        ),
        out_shape=jax.ShapeDtypeStruct((rows, width), bf16),
        compiler_params=params(),
        cost_estimate=cost(36_000_000_000, 17_000_000),
        name="output_sum",
    )(places, middle, tokens, bias, *map(view, settled), *map(view, passed))


def tokens_kernel(places, middle, upstream, settled, passed, *rest):
    out = rest[-1]
    inside = middle[0] == 1
    tile = out.shape[0]
    for slab in range(out.shape[1] // 128):
        per = BLOCK // 128
        at = slice(slab * tile, (slab + 1) * tile)
        to = pl.ds(pl.multiple_of(places[slab // per] * BLOCK + slab % per * 128, 128), 128)
        total = jnp.where(inside, settled[at].astype(f32), passed[at].astype(f32))
        out[:, to] = (upstream[:, to].astype(f32) + total).astype(bf16)


def tokens_sum(places, middle, upstream, settled, passed, number, earlier, tile=256):
    rows, width = upstream.shape
    row = pl.BlockSpec((tile, width), lambda i, *_: (number, 0))
    slabs = pl.BlockSpec((width // 128 * tile, 128), lambda i, *_: (0, 0))
    extra = [earlier]
    return pl.pallas_call(
        tokens_kernel,
        grid_spec=pltpu.PrefetchScalarGridSpec(
            num_scalar_prefetch=2,
            grid=(1,),
            in_specs=[row, slabs, slabs] + [pl.BlockSpec(memory_space=pl.ANY)] * len(extra),
            out_specs=row,
        ),
        out_shape=jax.ShapeDtypeStruct((rows, width), bf16),
        input_output_aliases={5: 0} if number else {},
        compiler_params=params(),
        cost_estimate=cost(36_000_000_000, 4_000_000),
        name="tokens_sum",
    )(places, middle, upstream, settled, passed, *extra)


class LineSum:
    def __init__(self, middle):
        self.middle = middle[0] == 1
        self.line = lax.axis_size("tensor") == 4
        self.pieces, self.joined, self.other, self.results = [], {}, {}, []

    def slot(self, piece, seen):
        number = len(self.pieces)
        shape = None if piece is None else piece.shape
        piece = None if piece is None else piece.reshape(-1, 128)
        self.pieces.append(piece)
        if not self.line:
            if piece is not None:
                total = lax.psum(piece, "tensor")
                self.results.append((total, total))
            return seen
        sent = []
        pairs, operand = [], None
        if piece is not None:
            operand = after(piece, seen)
            pairs += [(0, 1), (3, 2)]
        done = self.pieces[number - 2] if number >= 2 else None
        if done is not None:
            other = after(self.other[number - 2], (seen, self.inward))
            settled = (self.joined[number - 2] + other.astype(f32)).astype(bf16)
            if operand is None:
                operand = settled
            else:
                settled = jnp.pad(settled, ((0, operand.shape[0] - settled.shape[0]), (0, 0)))
                operand = jnp.where(self.middle, settled, operand)
            pairs += [(1, 0), (2, 3)]
        if number >= 1 and self.pieces[number - 1] is not None:
            inward = after(self.inward, seen).astype(f32)
            joined = (self.pieces[number - 1].astype(f32) + inward).astype(bf16)
            self.joined[number - 1] = joined.astype(f32)
            self.other[number - 1] = lax.ppermute(joined, "tensor", [(1, 2), (2, 1)])
            sent.append(joined)
        if operand is not None:
            self.inward = lax.ppermute(operand, "tensor", pairs)
            sent.append(operand)
        if done is not None:
            self.results.append((operand, self.inward))
        return tuple(sent)


def scatter_blocks(blocks, by_rows):
    if is_cube():
        return lax.psum_scatter(blocks, "dp", scatter_dimension=0, tiled=True)[0]
    if by_rows:
        full = blocks.reshape(-1, blocks.shape[2])
        return lax.psum_scatter(full, "dp", scatter_dimension=0, tiled=True)
    full = blocks.transpose(1, 0, 2).reshape(blocks.shape[1], -1)
    return lax.psum_scatter(full, "dp", scatter_dimension=1, tiled=True)


def ring(value, step):
    count = lax.axis_size("dp")
    pairs = [(i, i + step) for i in range(count) if 0 <= i + step < count]
    return lax.ppermute(value, "dp", pairs)


def locate(token_index, lengths, prefix):
    ends = jnp.cumsum(lengths)
    starts = ends - lengths
    inside = (token_index[:, None] >= starts[None, :]) & (token_index[:, None] < ends[None, :])
    begin = jnp.sum(jnp.where(inside, starts[None, :], 0), axis=1)
    limit = jnp.sum(jnp.where(inside, jnp.minimum(prefix, lengths)[None, :], 0), axis=1)
    return begin, limit


def rotary_tables(places):
    lane = jnp.arange(128, dtype=jnp.int32)
    exponents = (lane % (ROT // 2)).astype(f32) * (2.0 / ROT)
    angles = places.astype(f32)[:, None] * jnp.exp(exponents * -math.log(10000.0))[None, :]
    turned = (lane < ROT)[None, :]
    sign = jnp.where(lane < ROT // 2, -1.0, 1.0)[None, :]
    return jnp.where(turned, jnp.cos(angles), 1.0), jnp.where(turned, jnp.sin(angles) * sign, 0.0)


def on_device(
    tokens,
    project_weight,
    project_bias,
    dense_weight,
    dense_bias,
    expand_weight,
    expand_bias,
    shrink_weight,
    shrink_bias,
    first_gain,
    first_shift,
    second_gain,
    second_shift,
    lengths,
    prefix,
    upstream,
):
    rows, width = tokens.shape
    count = lax.axis_size("dp")
    me = lax.axis_index("dp")
    heads = project_bias.shape[0]
    places = natural_places()
    cube = is_cube()
    line = lax.axis_index("tensor")
    middle = ((line == 1) | (line == 2)).astype(jnp.int32).reshape(1)

    vectors = [first_gain, first_shift, second_gain, second_shift, dense_bias, shrink_bias]
    if cube:
        own = jnp.concatenate([v.reshape(-1).astype(bf16) for v in (*vectors, expand_bias, project_bias)])
        own = jnp.pad(own, (0, -own.size % 2048)).reshape(-1, 128)
        gathered = lax.all_gather(own, "dp", axis=0).reshape(count, -1)
        small = jnp.take(gathered, places, axis=0).astype(f32)
        wide = vectors[0].shape[0]
        rows_of = jnp.stack([small[:, k * wide : (k + 1) * wide].reshape(-1) for k in range(len(vectors))])
        at = len(vectors) * wide
        small = gathered.astype(f32)
        split = at + expand_bias.size
        full_expand_bias = small[:, at:split].reshape((count,) + expand_bias.shape).transpose(1, 0, 2).reshape(1, -1)
        full_project_bias = small[:, split : split + project_bias.size].reshape((count,) + project_bias.shape).transpose(1, 0, 2).reshape(1, -1)
    else:
        gathered = lax.all_gather(jnp.stack(vectors).astype(bf16), "dp", axis=1, tiled=True)
        rows_of = gathered.astype(f32)
        full_expand_bias = lax.all_gather(expand_bias.astype(bf16), "dp", axis=1, tiled=True).astype(f32).reshape(1, -1)
        full_project_bias = lax.all_gather(project_bias.astype(bf16), "dp", axis=1, tiled=True).astype(f32).reshape(1, -1)
    gains = jnp.concatenate([rows_of[:4], jnp.zeros((4, width), f32)], axis=0)
    bias_total = rows_of[4:5] + rows_of[5:6]

    def halved(vector, bit):
        keep = vector.shape[0] // 2
        return vector[:keep] + swap(vector[keep:], bit)

    def vector_parts(sums, grad_bias, expand_bias_sums, project_bias_sums):
        norms = sums[:4].reshape(4, BLOCKS, BLOCK).transpose(1, 0, 2).reshape(BLOCKS, -1)
        bias = grad_bias[0].reshape(BLOCKS, BLOCK)
        per_head = lambda v, like: v.reshape(heads, BLOCKS, like.shape[1]).transpose(1, 0, 2).reshape(BLOCKS, -1)
        heads_part = jnp.concatenate(
            [per_head(expand_bias_sums, expand_bias), per_head(project_bias_sums, project_bias)], axis=1
        )
        heads_part = jnp.take(heads_part, places, axis=0)
        return jnp.concatenate([norms, bias, heads_part], axis=1)

    token_index = me * rows + jnp.arange(rows, dtype=jnp.int32)
    begin, limit = locate(token_index, lengths, prefix)
    base = me * rows - SEQ_MAX
    low = begin - base
    high = jnp.maximum(token_index, begin + limit - 1) - base
    cos, sin = rotary_tables(token_index - begin)

    turned_width, hidden_width = dense_weight.shape[0], shrink_weight.shape[0]
    project_low, dense_low = project_weight.astype(bf16), dense_weight.astype(bf16)
    if cube:
        dense_low = dense_low.reshape(-1, BLOCK, BLOCK).transpose(1, 0, 2).reshape(BLOCK, -1)
        spread_project = Spread(jnp.concatenate([project_low, dense_low], axis=1), True)
        seen_project = spread_project.first()
        seen_project_too = spread_project.second(seen_project, gathered)
    else:
        seen_project = seen_project_too = ()
    spread_expand = Spread(after(expand_weight.astype(bf16), (gathered, seen_project)), True)
    seen_expand = spread_expand.first()
    if cube:
        project_a, project_b = spread_project.join(seen_project_too, spread_expand.weight)
    else:
        dense_full = lax.all_gather(dense_low, "dp", axis=1, tiled=True)
        dense_full = dense_full.reshape(-1, BLOCK, BLOCKS, BLOCK).transpose(2, 1, 0, 3).reshape(width, -1)
        both = jnp.concatenate([lax.all_gather(project_low, "dp", axis=0, tiled=True), dense_full], axis=1)
        project_a, project_b = both[: width // 2], both[width // 2 :]
    tok, one_a, one_b, two_a, two_b, up_a, up_b, mean, inverse, grad_bias = norm(
        places, tokens, upstream, after(gains, project_a)
    )
    seen_expand_too = spread_expand.second(seen_expand, project_a)
    queries, pairs = project(after(one_a, seen_expand), one_b, project_a, project_b, full_project_bias, cos, sin)
    sent = after(pairs, seen_expand_too)
    left = ring(sent, 1)
    right = ring(sent[:PREFIX_MAX], -1)
    spread_expand.begin_parts(seen_expand_too)
    expand_mine, expand_theirs = spread_expand.parts(pairs)
    spread_down = Spread(after(shrink_weight.astype(bf16), (mean, seen_project)), False)
    active, slope = expand(after(two_a, sent), two_b, expand_mine + expand_theirs, full_expand_bias)
    grad_attended = dense_back(after(up_a, active), up_b, project_a, project_b, turned_width)
    blocks = [spread_down.pair(0, active)] if cube else []
    spread_down.weight = after(spread_down.weight, (left, active))
    seen_down = spread_down.first()
    if not cube:
        blocks = [spread_down.pair(0)]
    attended, lse = attend(after(queries, grad_attended), left, pairs, right, low, high)
    seen_down_too = spread_down.second(seen_down, attended)
    blocks += [spread_down.pair(place, (attended, seen_down)) for place in range(len(blocks), HALF - 1)]
    dq, dleft, down, dright = attend_back(
        queries, left, pairs, right, low, high, lse, attended, grad_attended, cos, sin
    )
    later = ring(dleft, -1)
    earlier = ring(dright, 1)
    blocks.append(spread_down.pair(3, (dq, seen_down_too)))

    line = LineSum(middle)
    branch = lambda place, *seen: branch_piece(after(attended, seen), active, project_a, project_b, blocks[place], place)
    pieces = [branch(0, dq, seen_down_too)]
    seen = line.slot(pieces[0], ())
    depth = turned_width + hidden_width
    pieces.append(branch(1, pieces[0], seen))
    column_blocks = column_grad(places, after(attended, pieces[1]), up_a, up_b, depth)
    seen = line.slot(pieces[1], column_blocks)
    column_blocks = column_grad(places, after(active, seen), up_a, up_b, depth, turned_width, column_blocks)
    pieces.append(branch(2, column_blocks))
    seen = line.slot(pieces[2], pieces[2])
    column_blocks, later, earlier, last = lax.optimization_barrier((column_blocks, later, earlier, pieces[2]))
    grad_down = scatter_blocks(column_blocks, False)
    down_blocks = [b for b, _ in blocks] + [b for _, b in blocks]
    grad_hidden, expand_bias_sums = back(after(up_a, (last, seen)), up_b, down_blocks, 0, hidden_width, slope)
    pieces.append(branch(3, grad_hidden))
    seen = line.slot(pieces[3], pieces[3])
    grad_second = second_back(after(grad_hidden, (pieces[3], seen)), expand_mine + expand_theirs)
    grad_mixed, project_bias_sums = mix(after(dq, grad_second), down, later, earlier, cos, sin)
    *tails, sums = input_back(
        grad_mixed, project_a, project_b, grad_second, tok, mean, inverse, gains, 0, 1
    )
    seen = line.slot(tails[0], sums)
    *more, part = input_back(
        after(grad_mixed, (sums, seen)), project_a, project_b, grad_second, tok, mean, inverse, gains, 1, 3
    )
    tails += more
    sums = sums + part
    seen = line.slot(tails[1], part)
    widths = grad_hidden.shape[1], grad_mixed.shape[1]
    row_blocks = row_grad(places, two_a, two_b, after(grad_hidden, seen), sum(widths))
    vector = part
    if cube:
        vector = after(vector_parts(sums, grad_bias, expand_bias_sums, project_bias_sums), seen)
        vector = halved(halved(vector, CORE), ALONG_Y)
        vector = halved(after(vector, row_blocks), ALONG_X)[0]
    seen = line.slot(tails[2], row_blocks)
    row_blocks = row_grad(places, one_a, one_b, after(grad_mixed, seen), sum(widths), widths[0], row_blocks)
    row_blocks, grad_down, vector = lax.optimization_barrier((row_blocks, grad_down, vector))
    if cube:
        grad_rows = scatter_blocks(row_blocks, True)
        grad_expand, grad_project = grad_rows[:, : widths[0]].astype(f32), grad_rows[:, widths[0] :].astype(f32)
    else:
        grad_expand = scatter_blocks(row_blocks[:, :, : widths[0]], True).astype(f32)
        grad_project = scatter_blocks(row_blocks[:, :, widths[0] :], True).astype(f32)
    settled, passed = zip(*line.results[:4])
    output = output_sum(places, middle, after(bias_total, (row_blocks, seen)), settled, passed, tokens)
    tail = tails[3]
    if cube:
        norms = vector[: 4 * BLOCK].astype(bf16).reshape(-1, 128)
        tail = jnp.concatenate([tail.reshape(-1, 128), norms, jnp.zeros_like(norms)], axis=0)
    seen = line.slot(tail, output)
    tokens_grad = tokens_sum(places, middle, upstream, *line.results[4], 0, after(up_a, (output, seen)))
    seen = line.slot(None, tokens_grad)
    tokens_grad = tokens_sum(places, middle, upstream, *line.results[5], 1, after(tokens_grad, seen))
    line.slot(None, tokens_grad)
    for number in range(2, 4):
        tokens_grad = tokens_sum(places, middle, upstream, *line.results[4 + number], number, tokens_grad)
    grad_dense, grad_shrink = grad_down[:turned_width].astype(f32), grad_down[turned_width:].astype(f32)

    if cube:
        settled, passed = line.results[7]
        norms = jnp.where(middle[0] == 1, settled[-16:-8], passed[-16:-8]).astype(f32).reshape(4, BLOCK)
        at = 5 * BLOCK
        bias = vector[4 * BLOCK : at]
        expand_bias_grad = vector[at : at + expand_bias.size].reshape(expand_bias.shape)
        project_bias_grad = vector[at + expand_bias.size :].reshape(project_bias.shape)
    else:
        norms = lax.psum(lax.psum_scatter(sums[:4], "dp", scatter_dimension=1, tiled=True), "tensor")
        bias = lax.psum_scatter(grad_bias[0], "dp", scatter_dimension=0, tiled=True)
        split = lambda v: lax.psum_scatter(v.reshape(heads, -1), "dp", scatter_dimension=1, tiled=True)
        expand_bias_grad, project_bias_grad = split(expand_bias_sums), split(project_bias_sums)
    return (
        output,
        tokens_grad,
        grad_project,
        project_bias_grad,
        grad_dense,
        bias,
        grad_expand,
        expand_bias_grad,
        grad_shrink,
        bias,
        norms[0],
        norms[1],
        norms[2],
        norms[3],
    )


def solution(mesh):
    placed = (
        P("dp", None),
        P("dp", "tensor"),
        P("tensor", "dp"),
        P("tensor", "dp"),
        P("dp"),
        P("dp", "tensor"),
        P("tensor", "dp"),
        P("tensor", "dp"),
        P("dp"),
        P("dp"),
        P("dp"),
        P("dp"),
        P("dp"),
        P(),
        P(),
        P("dp", None),
    )
    return jax.shard_map(
        on_device,
        mesh=mesh,
        in_specs=placed,
        out_specs=(
            P("dp", None),
            P("dp", None),
            P("dp", "tensor"),
            P("tensor", "dp"),
            P("tensor", "dp"),
            P("dp"),
            P("dp", "tensor"),
            P("tensor", "dp"),
            P("tensor", "dp"),
            P("dp"),
            P("dp"),
            P("dp"),
            P("dp"),
            P("dp"),
        ),
        check_vma=False,
    )
```

```python
import functools
import math

import jax
import jax.numpy as jnp
from jax import lax
from jax.experimental import pallas as pl
from jax.experimental.pallas import tpu as pltpu
from jax.sharding import PartitionSpec as P

HD = 256
ROT = 64
SEQ_MAX = 1024
PREFIX_MAX = 512
BLOCK = 256
BLOCKS = 8
HALF = 4
EPSILON = 1e-05
MASKED = -1e30
bf16 = jnp.bfloat16
f32 = jnp.float32
NN = (((1,), (0,)), ((), ()))
NT = (((1,), (1,)), ((), ()))
TN = (((0,), (0,)), ((), ()))
VMEM_BYTES = 56 * 2**20


def mul(a, b, dims=NN):
    return lax.dot_general(a, b, dims, preferred_element_type=f32)


def params(**more):
    return pltpu.CompilerParams(vmem_limit_bytes=VMEM_BYTES, **more)


def cost(flops, moved, transcendentals=0):
    return pl.CostEstimate(flops=flops, bytes_accessed=moved, transcendentals=transcendentals)


def whole_spec(array):
    zeros = (0,) * array.ndim
    return pl.BlockSpec(array.shape, lambda *_: zeros)


def swap(value, bit):
    count = lax.axis_size("dp")
    return lax.ppermute(value, "dp", [(i, i ^ bit) for i in range(count)])


CORE, ALONG_X, ALONG_Y = 1, 2, 4


def is_cube():
    return lax.axis_size("dp") == BLOCKS


def natural_places():
    place = jnp.arange(BLOCKS, dtype=jnp.int32)
    if not is_cube():
        return place
    owner = ((place >> 2) & 1) * CORE + ((place >> 1) & 1) * ALONG_Y + (place & 1) * ALONG_X
    return owner ^ lax.axis_index("dp")


class Spread:
    def __init__(self, weight, by_rows):
        self.weight, self.by_rows = weight, by_rows

    def first(self):
        if is_cube():
            self.from_x = swap(self.weight, ALONG_X)
            self.from_y = swap(self.weight, ALONG_Y)
            return self.from_x, self.from_y
        self.full = lax.all_gather(self.weight, "dp", axis=0 if self.by_rows else 1, tiled=True)
        return (self.full,)

    def second(self, *seen):
        if is_cube():
            half = self.weight.shape[0] // 2
            self.over_x = swap(after(self.from_x[:half], seen), ALONG_Y)
            self.over_y = swap(after(self.from_y[half:], seen), ALONG_X)
            return self.over_x, self.over_y
        return (self.full,)

    def join(self, *seen):
        if is_cube():
            parts = [self.weight, self.from_x, self.from_y, self.over_x, self.over_y]
            mine = jnp.concatenate(after(parts, seen), axis=0)
            return mine, swap(mine, CORE)
        half = self.full.shape[0] // 2
        return self.full[:half], self.full[half:]

    def begin_parts(self, *seen):
        if is_cube():
            self.near = [swap(after(part, seen), CORE) for part in (self.weight, self.from_x, self.from_y)]

    def parts(self, *seen):
        if is_cube():
            far = [swap(after(part, seen), CORE) for part in (self.over_x, self.over_y)]
            return [self.weight, self.from_x, self.from_y, self.over_x, self.over_y], self.near + far
        half = self.full.shape[0] // 2
        return [self.full[:half]], [self.full[half:]]

    def pair(self, place, seen=()):
        if is_cube():
            if place == 3:
                mine = jnp.concatenate([self.over_x, self.over_y], axis=0)
            else:
                mine = self.weight if place == 0 else (self.from_x, self.from_y)[place - 1]
            return mine, swap(after(mine, seen), CORE)
        blocks = self.full.reshape(self.full.shape[0], BLOCKS, -1)
        return blocks[:, place], blocks[:, place + HALF]


def after(value, seen):
    return lax.optimization_barrier((value, seen))[0]


def norm_kernel(places, tokens, upstream, gains, tok, one_a, one_b, two_a, two_b, up_a, up_b, mean, inverse, grad_bias):
    values = tokens[...].astype(f32)
    average = jnp.mean(values, axis=1, keepdims=True)
    center = values - average
    scale = lax.rsqrt(jnp.mean(center * center, axis=1, keepdims=True) + EPSILON)
    mean[...] = average
    inverse[...] = scale

    @pl.when(pl.program_id(0) == 0)
    def _():
        grad_bias[...] = jnp.zeros_like(grad_bias)

    for place in range(BLOCKS):
        from_ = pl.ds(pl.multiple_of(places[place] * BLOCK, BLOCK), BLOCK)
        to = pl.ds(place * BLOCK, BLOCK)
        inner = pl.ds(place % HALF * BLOCK, BLOCK)
        first, second, up = (one_a, two_a, up_a) if place < HALF else (one_b, two_b, up_b)
        low = tokens[:, from_]
        tok[:, to] = low
        normed = (low.astype(f32) - average) * scale
        first[:, inner] = (normed * gains[0:1, to] + gains[1:2, to]).astype(bf16)
        second[:, inner] = (normed * gains[2:3, to] + gains[3:4, to]).astype(bf16)
        grad = upstream[:, from_]
        up[:, inner] = grad
        grad_bias[0:1, to] += jnp.sum(grad.astype(f32), axis=0, keepdims=True)


def norm(places, tokens, upstream, gains, tile=256):
    rows, width = tokens.shape
    row = lambda w: pl.BlockSpec((tile, w), lambda i, *_: (i, 0))
    shape = lambda w, kind: jax.ShapeDtypeStruct((rows, w), kind)
    half = width // 2
    return pl.pallas_call(
        norm_kernel,
        grid_spec=pltpu.PrefetchScalarGridSpec(
            num_scalar_prefetch=1,
            grid=(rows // tile,),
            in_specs=[row(width), row(width), whole_spec(gains)],
            out_specs=[row(width)] + [row(half)] * 6 + [row(1), row(1), pl.BlockSpec((8, width), lambda *_: (0, 0))],
        ),
        out_shape=[shape(width, bf16)]
        + [shape(half, bf16)] * 6
        + [shape(1, f32), shape(1, f32), jax.ShapeDtypeStruct((8, width), f32)],
        compiler_params=params(),
        cost_estimate=cost(20 * rows * width, 20 * rows * width),
        name="norm",
    )(places, tokens, upstream, gains)


def turn(part, cos, sin, sign):
    lane = lax.broadcasted_iota(jnp.int32, part.shape, 1)
    partner = jnp.where(lane < ROT // 2, pltpu.roll(part, 128 - ROT // 2, 1), pltpu.roll(part, ROT // 2, 1))
    if sign > 0:
        return part * cos + partner * sin
    return part * cos - partner * sin


def project_kernel(one_a, one_b, w_a, w_b, bias, cos, sin, queries, pairs):
    for part in range(3):
        at = slice(part * HD, (part + 1) * HD)
        mixed = mul(one_a[...], w_a[:, at]) + mul(one_b[...], w_b[:, at]) + bias[:, at]
        if part < 2:
            ref, to = (queries, 0) if part == 0 else (pairs, 0)
            ref[:, to : to + 128] = turn(mixed[:, :128], cos[...], sin[...], 1).astype(bf16)
            ref[:, to + 128 : to + HD] = mixed[:, 128:].astype(bf16)
        else:
            pairs[:, HD:] = mixed.astype(bf16)


def project(one_a, one_b, w_a, w_b, bias, cos, sin):
    rows, half = one_a.shape
    heads = w_a.shape[1] // (3 * HD)
    weight = pl.BlockSpec((half, 3 * HD), lambda h: (0, h))
    return pl.pallas_call(
        project_kernel,
        grid=(heads,),
        in_specs=[
            whole_spec(one_a),
            whole_spec(one_b),
            weight,
            weight,
            pl.BlockSpec((1, 3 * HD), lambda h: (0, h)),
            whole_spec(cos),
            whole_spec(sin),
        ],
        out_specs=[pl.BlockSpec((rows, HD), lambda h: (0, h)), pl.BlockSpec((rows, 2 * HD), lambda h: (0, h))],
        out_shape=[
            jax.ShapeDtypeStruct((rows, heads * HD), bf16),
            jax.ShapeDtypeStruct((rows, heads * 2 * HD), bf16),
        ],
        compiler_params=params(),
        cost_estimate=cost(4 * rows * half * w_a.shape[1], 14_000_000),
        name="project",
    )(one_a, one_b, w_a, w_b, bias, cos, sin)


def lay(parts, joined):
    at = 0
    for part in parts:
        joined[at : at + part.shape[0], :] = part[...]
        at += part.shape[0]


def expand_kernel(two_a, two_b, bias, *refs):
    *parts, active, slope, weight = refs
    lay(parts, weight)
    rows, half = two_a.shape
    for start in range(0, rows, 512):
        at = slice(start, start + 512)
        hidden = mul(two_a[at], weight[:half]) + mul(two_b[at], weight[half:]) + bias[...]
        below = 0.5 + 0.5 * lax.erf(hidden * (0.5**0.5))
        density = jnp.exp(hidden * hidden * -0.5) * (1.0 / math.sqrt(2.0 * math.pi))
        active[at] = (hidden * below).astype(bf16)
        slope[at] = (below + hidden * density).astype(bf16)


def expand(two_a, two_b, parts, bias, tile=512):
    rows, half = two_a.shape
    width = parts[0].shape[1]
    column = lambda r: pl.BlockSpec((r, tile), lambda n: (0, n))
    return pl.pallas_call(
        expand_kernel,
        grid=(width // tile,),
        in_specs=[whole_spec(two_a), whole_spec(two_b), column(1)] + [column(part.shape[0]) for part in parts],
        out_specs=[column(rows), column(rows)],
        out_shape=[jax.ShapeDtypeStruct((rows, width), bf16)] * 2,
        scratch_shapes=[pltpu.VMEM((2 * half, tile), bf16)],
        compiler_params=params(),
        cost_estimate=cost(0, 0),
        name="expand",
    )(two_a, two_b, bias, *parts)


def branch_kernel(attended, active, dense_a, dense_b, mine, theirs, out):
    slabs = BLOCK // 128
    for number, (dense, weight) in enumerate(((dense_a, mine), (dense_b, theirs))):
        full = mul(active[...], weight[...])
        for at in range(0, attended.shape[1], BLOCK):
            full = full + mul(attended[:, at : at + BLOCK], dense[:, at : at + BLOCK])
        full = full.astype(bf16)
        for slab in range(slabs):
            out[number * slabs + slab] = full[:, slab * 128 : (slab + 1) * 128]


def branch_piece(attended, active, w_a, w_b, pair, place, tile=512):
    rows, turned = attended.shape
    slabs = 2 * BLOCK // 128
    row = lambda a: pl.BlockSpec((tile, a.shape[1]), lambda i: (i, 0))
    dense = pl.BlockSpec((BLOCK, turned), lambda i: (place, w_a.shape[1] // turned - 1))
    return pl.pallas_call(
        branch_kernel,
        grid=(rows // tile,),
        in_specs=[row(attended), row(active), dense, dense, whole_spec(pair[0]), whole_spec(pair[1])],
        out_specs=pl.BlockSpec((slabs, tile, 128), lambda i: (0, i, 0)),
        out_shape=jax.ShapeDtypeStruct((slabs, rows, 128), bf16),
        compiler_params=params(),
        cost_estimate=cost(0, 0),
        name="branch",
    )(attended, active, w_a, w_b, *pair)


def dense_kernel(up_a, up_b, w_a, w_b, out, joined):
    for place in range(BLOCKS):
        ref = w_a if place < HALF else w_b
        rows = slice(place % HALF * BLOCK, (place % HALF + 1) * BLOCK)
        for at in range(0, out.shape[1], BLOCK):
            joined[at : at + BLOCK, place * BLOCK : (place + 1) * BLOCK] = ref[rows, at : at + BLOCK]
    half = up_a.shape[1]
    for start in range(0, out.shape[0], 512):
        at = slice(start, start + 512)
        out[at] = (mul(up_a[at], joined[:, :half], NT) + mul(up_b[at], joined[:, half:], NT)).astype(bf16)


def dense_back(up_a, up_b, w_a, w_b, turned):
    rows, half = up_a.shape
    dense = pl.BlockSpec((half, turned), lambda i: (0, w_a.shape[1] // turned - 1))
    return pl.pallas_call(
        dense_kernel,
        grid=(1,),
        in_specs=[whole_spec(up_a), whole_spec(up_b), dense, dense],
        out_specs=pl.BlockSpec((rows, turned), lambda i: (0, 0)),
        out_shape=jax.ShapeDtypeStruct((rows, turned), bf16),
        scratch_shapes=[pltpu.VMEM((turned, 2 * half), bf16)],
        compiler_params=params(),
        cost_estimate=cost(0, 0),
        name="dense_back",
    )(up_a, up_b, w_a, w_b)


def back_kernel(up_a, up_b, blocks, slope, out, sums, joined):
    for place in range(BLOCKS):
        joined[:, place * BLOCK : (place + 1) * BLOCK] = blocks[place][...]
    half = HALF * BLOCK
    total = jnp.zeros((1, out.shape[1]), f32)
    for start in range(0, out.shape[0], 512):
        at = slice(start, start + 512)
        grad = mul(up_a[at], joined[:, :half], NT) + mul(up_b[at], joined[:, half:], NT)
        if slope is not None:
            grad = grad * slope[at].astype(f32)
        grad = grad.astype(bf16)
        out[at] = grad
        if sums is not None:
            total = total + jnp.sum(grad.astype(f32), axis=0, keepdims=True)
    if sums is not None:
        sums[...] = total


def back(up_a, up_b, blocks, start, width, slope=None, tile=512):
    rows, half = up_a.shape
    weight = pl.BlockSpec((tile, BLOCK), lambda n: (n + start // tile, 0))
    column = lambda r: pl.BlockSpec((r, tile), lambda n: (0, n))
    scaled = slope is not None

    def body(a, b, *rest):
        blocks, rest = rest[:BLOCKS], rest[BLOCKS:]
        if scaled:
            s, out, sums, joined = rest
        else:
            (out, joined), s, sums = rest, None, None
        back_kernel(a, b, blocks, s, out, sums, joined)

    out = jax.ShapeDtypeStruct((rows, width), bf16)
    return pl.pallas_call(
        body,
        grid=(width // tile,),
        in_specs=[whole_spec(up_a), whole_spec(up_b)] + [weight] * BLOCKS + [column(rows)] * scaled,
        out_specs=[column(rows), column(1)] if scaled else column(rows),
        out_shape=[out, jax.ShapeDtypeStruct((1, width), f32)] if scaled else out,
        scratch_shapes=[pltpu.VMEM((tile, 2 * half), bf16)],
        compiler_params=params(),
        cost_estimate=cost(4 * rows * half * width, 4 * rows * half + 4 * half * width + 4 * rows * width),
        name="back",
    )(up_a, up_b, *blocks, *([slope] if scaled else []))


def second_kernel(grad, *refs):
    count = len(refs) - 3
    parts, out, weight, arrived = refs[:count], *refs[count:]
    tile = out.shape[1]
    step = pl.program_id(0)
    copies, ends, at = [], [], 0
    for number, part in enumerate(parts):
        to = weight.at[at : at + part.shape[0]]
        copies.append(pltpu.make_async_copy(part, to, arrived.at[number]))
        at += part.shape[0]
        ends.append(at)

    @pl.when(step == 0)
    def _():
        for copy in copies:
            copy.start()

    for number in range(weight.shape[0] // tile):

        @pl.when(step == number)
        def _(number=number):
            before = 0
            for copy, end in zip(copies, ends):
                last_needed_at = before // tile
                if last_needed_at == number:
                    copy.wait()
                before = end

    rows = pl.ds(pl.multiple_of(step * tile, tile), tile)
    out[...] = mul(grad[...], weight[rows], NT).astype(bf16)


def second_back(grad, parts, tile=512):
    rows, width = grad.shape
    depth = sum(part.shape[0] for part in parts)
    return pl.pallas_call(
        second_kernel,
        grid=(depth // tile,),
        in_specs=[whole_spec(grad)] + [pl.BlockSpec(memory_space=pl.ANY)] * len(parts),
        out_specs=pl.BlockSpec((rows, tile), lambda n: (0, n)),
        out_shape=jax.ShapeDtypeStruct((rows, depth), bf16),
        scratch_shapes=[pltpu.VMEM((depth, width), bf16), pltpu.SemaphoreType.DMA((len(parts),))],
        compiler_params=params(),
        cost_estimate=cost(2 * rows * depth * width, 2 * (rows + depth) * width + 2 * rows * depth),
        name="second_back",
    )(grad, *parts)


def row_grad_kernel(where, left_a, left_b, right, *rest):
    out = rest[-1]
    for number, left in enumerate((left_a, left_b)):
        full = mul(left[...], right[...], TN)
        for place in range(HALF):
            out[where[number * HALF + place]] = full[place * BLOCK : (place + 1) * BLOCK].astype(bf16)


def row_grad(where, left_a, left_b, right, total, start=0, into=None, tile=512):
    rows, width = right.shape
    blocks = 2 * HALF
    extra = [] if into is None else [into]
    return pl.pallas_call(
        row_grad_kernel,
        grid_spec=pltpu.PrefetchScalarGridSpec(
            num_scalar_prefetch=1,
            grid=(width // tile,),
            in_specs=[whole_spec(left_a), whole_spec(left_b), pl.BlockSpec((rows, tile), lambda n, *_: (0, n))]
            + [pl.BlockSpec(memory_space=pl.ANY)] * len(extra),
            out_specs=pl.BlockSpec((blocks, BLOCK, tile), lambda n, *_: (0, 0, n + start // tile)),
        ),
        out_shape=jax.ShapeDtypeStruct((blocks, BLOCK, total), bf16),
        input_output_aliases={4: 0} if extra else {},
        compiler_params=params(),
        cost_estimate=cost(2 * rows * blocks * BLOCK * width, 2 * blocks * BLOCK * (rows + width) + 2 * rows * width),
        name="row_grad",
    )(where, left_a, left_b, right, *extra)


def column_grad_kernel(where, left, right_a, right_b, *rest):
    out = rest[-1]
    for number, right in enumerate((right_a, right_b)):
        full = mul(left[...], right[...], TN)
        for place in range(HALF):
            out[where[number * HALF + place]] = full[:, place * BLOCK : (place + 1) * BLOCK].astype(bf16)


def column_grad(where, left, right_a, right_b, total, start=0, into=None, tile=512):
    rows, width = left.shape
    blocks = 2 * HALF
    extra = [] if into is None else [into]
    return pl.pallas_call(
        column_grad_kernel,
        grid_spec=pltpu.PrefetchScalarGridSpec(
            num_scalar_prefetch=1,
            grid=(width // tile,),
            in_specs=[pl.BlockSpec((rows, tile), lambda n, *_: (0, n)), whole_spec(right_a), whole_spec(right_b)]
            + [pl.BlockSpec(memory_space=pl.ANY)] * len(extra),
            out_specs=pl.BlockSpec((blocks, tile, BLOCK), lambda n, *_: (0, n + start // tile, 0)),
        ),
        out_shape=jax.ShapeDtypeStruct((blocks, total, BLOCK), bf16),
        input_output_aliases={4: 0} if extra else {},
        compiler_params=params(),
        cost_estimate=cost(0, 0),
        name="column_grad",
    )(where, left, right_a, right_b, *extra)


def fill(refs, heads, place):
    for head in range(heads):
        at = 0
        for ref in refs:
            for start in range(0, ref.shape[0], 512):
                rows = slice(start, start + 512)
                place(head, at, ref[rows, 2 * head * HD : (2 * head + 1) * HD], ref[rows, (2 * head + 1) * HD : (2 * head + 2) * HD])
                at += 512


def attend_kernel(first, last, q, left, own, right, low, high, out, lse, keys, values_turned, *, wide):
    step = pl.program_id(0)
    tall = q.shape[0]
    heads = range(keys.shape[0])

    @pl.when(step == 0)
    def _():
        def place(head, at, k, v):
            keys[head, at : at + 512, :] = k
            values_turned[head, :, at : at + 512] = jnp.transpose(v)

        fill((left, own, right), len(heads), place)

    scaled = [q[:, h * HD : (h + 1) * HD] * jnp.asarray(HD**-0.5, bf16) for h in heads]
    low_row = low[...]
    high_row = high[...]

    def block(j, carry):
        rows = pl.ds(pl.multiple_of(j * wide, wide), wide)
        key = j * wide + lax.broadcasted_iota(jnp.int32, (wide, tall), 0)
        seen = (key >= low_row) & (key <= high_row)
        scores = [mul(keys[h, rows, :], scaled[h], NT) for h in heads]
        after_block = []
        for h in heads:
            top, total, acc = carry[h]
            masked = jnp.where(seen, scores[h], MASKED)
            new = jnp.maximum(top, jnp.max(masked, axis=0, keepdims=True))
            weights = jnp.exp(masked - new)
            fade = jnp.exp(top - new)
            total = total * fade + jnp.sum(weights, axis=0, keepdims=True)
            acc = acc * fade + mul(values_turned[h, :, rows], weights.astype(bf16))
            after_block.append((new, total, acc))
        return tuple(after_block)

    start = (jnp.full((1, tall), MASKED, f32), jnp.zeros((1, tall), f32), jnp.zeros((HD, tall), f32))
    done = lax.fori_loop(first[step], last[step] + 1, block, tuple(start for _ in heads))
    for h in heads:
        top, total, acc = done[h]
        out[:, h * HD : (h + 1) * HD] = jnp.transpose(acc / total).astype(bf16)
        lse[h] = top + jnp.log(total)


def key_blocks(low, high, tall, wide):
    return jnp.min(low.reshape(-1, tall), axis=1) // wide, jnp.max(high.reshape(-1, tall), axis=1) // wide


def attend(q, left, own, right, low, high, tall=256, wide=512):
    rows, width = q.shape
    heads = width // HD
    extent = left.shape[0] + rows + right.shape[0]
    row = pl.BlockSpec((1, tall), lambda i, *_: (0, i))
    mine = pl.BlockSpec((tall, width), lambda i, *_: (i, 0))
    return pl.pallas_call(
        functools.partial(attend_kernel, wide=wide),
        grid_spec=pltpu.PrefetchScalarGridSpec(
            num_scalar_prefetch=2,
            grid=(rows // tall,),
            in_specs=[mine, whole_spec(left), whole_spec(own), whole_spec(right), row, row],
            out_specs=[mine, pl.BlockSpec((heads, 1, tall), lambda i, *_: (0, 0, i))],
            scratch_shapes=[pltpu.VMEM((heads, extent, HD), bf16), pltpu.VMEM((heads, HD, extent), bf16)],
        ),
        out_shape=[jax.ShapeDtypeStruct((rows, width), bf16), jax.ShapeDtypeStruct((heads, 1, rows), f32)],
        compiler_params=params(),
        cost_estimate=cost(8_000_000_000, 10_000_000, 3_000_000),
        name="attend",
    )(*key_blocks(low, high, tall, wide), q, left, own, right, low.reshape(1, rows), high.reshape(1, rows))


def attend_back_kernel(
    first, last, q, left, own, right, low, high, lse, attended, grad, cos, sin,
    dq, dleft, down, dright, keys, values, keys_turned, dk, dv, *, wide,
):
    step = pl.program_id(0)
    tall = q.shape[0]
    heads = range(keys.shape[0])

    @pl.when(step == 0)
    def _():
        def place(head, at, k, v):
            keys[head, at : at + 512, :] = k
            values[head, at : at + 512, :] = v
            keys_turned[head, :, at : at + 512] = jnp.transpose(k)

        fill((left, own, right), len(heads), place)
        dk[...] = jnp.zeros_like(dk)
        dv[...] = jnp.zeros_like(dv)

    cut = lambda ref, h: ref[:, h * HD : (h + 1) * HD]
    scaled = [cut(q, h) * jnp.asarray(HD**-0.5, bf16) for h in heads]
    given = [cut(grad, h) for h in heads]
    low_row = low[...]
    high_row = high[...]
    deltas = [
        jnp.sum(jnp.transpose(given[h].astype(f32) * cut(attended, h).astype(f32)), axis=0, keepdims=True) for h in heads
    ]

    def block(j, accs):
        rows = pl.ds(pl.multiple_of(j * wide, wide), wide)
        key = j * wide + lax.broadcasted_iota(jnp.int32, (wide, tall), 0)
        seen = (key >= low_row) & (key <= high_row)
        scores = [mul(keys[h, rows, :], scaled[h], NT) for h in heads]
        grad_probs = [mul(values[h, rows, :], given[h], NT) for h in heads]
        after_block = []
        for h in heads:
            probs = jnp.exp(jnp.where(seen, scores[h] - lse[h], MASKED))
            grad_scores = (probs * (grad_probs[h] - deltas[h])).astype(bf16)
            dv[h, rows, :] += mul(probs.astype(bf16), given[h])
            dk[h, rows, :] += mul(grad_scores, scaled[h])
            after_block.append(accs[h] + mul(keys_turned[h, :, rows], grad_scores))
        return tuple(after_block)

    accs = lax.fori_loop(first[step], last[step] + 1, block, tuple(jnp.zeros((HD, tall), f32) for _ in heads))
    for h in heads:
        full = jnp.transpose(accs[h]) * (HD**-0.5)
        dq[:, h * HD : h * HD + 128] = turn(full[:, :128], cos[...], sin[...], -1).astype(bf16)
        dq[:, h * HD + 128 : (h + 1) * HD] = full[:, 128:].astype(bf16)

    @pl.when(step == pl.num_programs(0) - 1)
    def _():
        for h in heads:
            at = 0
            for ref in (dleft, down, dright):
                count = ref.shape[0]
                ref[:, 2 * h * HD : (2 * h + 1) * HD] = dk[h, at : at + count, :].astype(ref.dtype)
                ref[:, (2 * h + 1) * HD : (2 * h + 2) * HD] = dv[h, at : at + count, :].astype(ref.dtype)
                at += count


def attend_back(q, left, own, right, low, high, lse, attended, grad, cos, sin, tall=256, wide=512):
    rows, width = q.shape
    heads = width // HD
    extent = left.shape[0] + rows + right.shape[0]
    row = pl.BlockSpec((1, tall), lambda i, *_: (0, i))
    mine = pl.BlockSpec((tall, width), lambda i, *_: (i, 0))
    table = pl.BlockSpec((tall, 128), lambda i, *_: (i, 0))
    return pl.pallas_call(
        functools.partial(attend_back_kernel, wide=wide),
        grid_spec=pltpu.PrefetchScalarGridSpec(
            num_scalar_prefetch=2,
            grid=(rows // tall,),
            in_specs=[
                mine, whole_spec(left), whole_spec(own), whole_spec(right), row, row,
                pl.BlockSpec((heads, 1, tall), lambda i, *_: (0, 0, i)), mine, mine, table, table,
            ],
            out_specs=[mine, whole_spec(left), whole_spec(own), whole_spec(right)],
            scratch_shapes=[
                pltpu.VMEM((heads, extent, HD), bf16),
                pltpu.VMEM((heads, extent, HD), bf16),
                pltpu.VMEM((heads, HD, extent), bf16),
                pltpu.VMEM((heads, extent, HD), f32),
                pltpu.VMEM((heads, extent, HD), f32),
            ],
        ),
        out_shape=[
            jax.ShapeDtypeStruct((rows, width), bf16),
            jax.ShapeDtypeStruct(left.shape, bf16),
            jax.ShapeDtypeStruct(own.shape, bf16),
            jax.ShapeDtypeStruct(right.shape, bf16),
        ],
        compiler_params=params(),
        cost_estimate=cost(16_000_000_000, 20_000_000, 3_000_000),
        name="attend_back",
    )(*key_blocks(low, high, tall, wide), q, left, own, right, low.reshape(1, rows), high.reshape(1, rows), lse, attended, grad, cos, sin)


def mixed_kernel(dq, own, later, earlier, cos, sin, out, sums):
    rows = dq.shape[0]
    near = earlier.shape[0]
    out[:, :HD] = dq[...]
    pairs = own[...].astype(f32) + later[...].astype(f32)
    top = pairs[:near] + earlier[...].astype(f32)
    for at, part in ((slice(0, near), top), (slice(near, rows), pairs[near:])):
        out[at, HD : HD + 128] = turn(part[:, :128], cos[at], sin[at], -1).astype(bf16)
        out[at, HD + 128 :] = part[:, 128:].astype(bf16)
    sums[...] = jnp.sum(out[...].astype(f32), axis=0, keepdims=True)


def mix(dq, own, later, earlier, cos, sin):
    rows, width = dq.shape
    heads = width // HD
    pair = lambda a: pl.BlockSpec((a.shape[0], 2 * HD), lambda h: (0, h))
    return pl.pallas_call(
        mixed_kernel,
        grid=(heads,),
        in_specs=[
            pl.BlockSpec((rows, HD), lambda h: (0, h)), pair(own), pair(later), pair(earlier),
            whole_spec(cos), whole_spec(sin),
        ],
        out_specs=[pl.BlockSpec((rows, 3 * HD), lambda h: (0, h)), pl.BlockSpec((1, 3 * HD), lambda h: (0, h))],
        out_shape=[
            jax.ShapeDtypeStruct((rows, 3 * width), bf16),
            jax.ShapeDtypeStruct((1, 3 * width), f32),
        ],
        compiler_params=params(),
        cost_estimate=cost(10_000_000, 14_000_000),
        name="mix",
    )(dq, own, later, earlier, cos, sin)


def input_kernel(mixed, w_a, w_b, second, tok, mean, inverse, gains, *outs):
    *outs, sums = outs
    step = pl.program_id(0)
    half = w_a.shape[0]
    grad_a = mul(mixed[...], w_a[...], NT)
    grad_b = mul(mixed[...], w_b[...], NT)
    scale = inverse[...]

    @pl.when(step == 0)
    def _():
        sums[...] = jnp.zeros_like(sums)

    pieces = []
    total = 0.0
    product = 0.0
    for number, grad in enumerate((grad_a, grad_b)):
        at = slice(number * half, (number + 1) * half)
        normed = (tok[:, at].astype(f32) - mean[...]) * scale
        other = second[:, at].astype(f32)
        both = grad * gains[0:1, at] + other * gains[2:3, at]
        sums[0:1, at] += jnp.sum(grad * normed, axis=0, keepdims=True)
        sums[1:2, at] += jnp.sum(grad, axis=0, keepdims=True)
        sums[2:3, at] += jnp.sum(other * normed, axis=0, keepdims=True)
        sums[3:4, at] += jnp.sum(other, axis=0, keepdims=True)
        total = total + jnp.sum(both, axis=1, keepdims=True)
        product = product + jnp.sum(both * normed, axis=1, keepdims=True)
        pieces.append((at, both, normed))
    total = total * (0.5 / half)
    product = product * (0.5 / half)

    def store(ref):
        for at, both, normed in pieces:
            grad = (scale * (both - total - normed * product)).astype(bf16)
            for slab in range(half // 128):
                ref[at.start // 128 + slab] = grad[:, slab * 128 : (slab + 1) * 128]

    if len(outs) == 1:
        store(outs[0])
    else:
        for number, ref in enumerate(outs):
            pl.when(step == number)(functools.partial(store, ref))


def input_back(mixed, w_a, w_b, second, tok, mean, inverse, gains, start, count, tile=256):
    width = tok.shape[1]
    depth = mixed.shape[1]
    row = lambda w: pl.BlockSpec((tile, w), lambda i: (i + start, 0))
    weight = pl.BlockSpec((w_a.shape[0], depth), lambda i: (0, 0))
    slabs = (width // 128, tile, 128)
    out = pl.BlockSpec(slabs, lambda i: (0, 0, 0))
    return pl.pallas_call(
        input_kernel,
        grid=(count,),
        in_specs=[
            row(depth), weight, weight, row(width), row(width), row(1), row(1), whole_spec(gains),
        ],
        out_specs=[out] * count + [pl.BlockSpec((8, width), lambda i: (0, 0))],
        out_shape=[jax.ShapeDtypeStruct(slabs, bf16)] * count + [jax.ShapeDtypeStruct((8, width), f32)],
        compiler_params=params(),
        cost_estimate=cost(2 * count * tile * depth * width, 14_000_000),
        name="input_back",
    )(mixed, w_a, w_b, second, tok, mean, inverse, gains)


def output_kernel(places, middle, tokens, bias, *refs):
    out = refs[-1]
    inside = middle[0] == 1
    for place in range(BLOCKS):
        settled, passed = refs[place % HALF], refs[HALF + place % HALF]
        for slab in range(BLOCK // 128):
            to = pl.ds(pl.multiple_of(places[place] * BLOCK + slab * 128, 128), 128)
            at = place // HALF * (BLOCK // 128) + slab
            total = jnp.where(inside, settled[at].astype(f32), passed[at].astype(f32))
            here = bias[0:1, place * BLOCK + slab * 128 : place * BLOCK + slab * 128 + 128]
            out[:, to] = (tokens[:, to].astype(f32) + total + here).astype(bf16)


def output_sum(places, middle, bias, settled, passed, tokens, tile=256):
    rows, width = tokens.shape
    row = lambda w: pl.BlockSpec((tile, w), lambda i, *_: (i, 0))
    slabs = pl.BlockSpec((width // 512, tile, 128), lambda i, *_: (0, i, 0))
    view = lambda a: a.reshape(width // 512, rows, 128)
    return pl.pallas_call(
        output_kernel,
        grid_spec=pltpu.PrefetchScalarGridSpec(
            num_scalar_prefetch=2,
            grid=(rows // tile,),
            in_specs=[row(width), whole_spec(bias)] + [slabs] * 8,
            out_specs=row(width),
        ),
        out_shape=jax.ShapeDtypeStruct((rows, width), bf16),
        compiler_params=params(),
        cost_estimate=cost(36_000_000_000, 17_000_000),
        name="output_sum",
    )(places, middle, tokens, bias, *map(view, settled), *map(view, passed))


def tokens_kernel(places, middle, upstream, settled, passed, *rest):
    out = rest[-1]
    inside = middle[0] == 1
    tile = out.shape[0]
    for slab in range(out.shape[1] // 128):
        per = BLOCK // 128
        at = slice(slab * tile, (slab + 1) * tile)
        to = pl.ds(pl.multiple_of(places[slab // per] * BLOCK + slab % per * 128, 128), 128)
        total = jnp.where(inside, settled[at].astype(f32), passed[at].astype(f32))
        out[:, to] = (upstream[:, to].astype(f32) + total).astype(bf16)


def tokens_sum(places, middle, upstream, settled, passed, number, earlier, tile=256):
    rows, width = upstream.shape
    row = pl.BlockSpec((tile, width), lambda i, *_: (number, 0))
    slabs = pl.BlockSpec((width // 128 * tile, 128), lambda i, *_: (0, 0))
    extra = [earlier]
    return pl.pallas_call(
        tokens_kernel,
        grid_spec=pltpu.PrefetchScalarGridSpec(
            num_scalar_prefetch=2,
            grid=(1,),
            in_specs=[row, slabs, slabs] + [pl.BlockSpec(memory_space=pl.ANY)] * len(extra),
            out_specs=row,
        ),
        out_shape=jax.ShapeDtypeStruct((rows, width), bf16),
        input_output_aliases={5: 0} if number else {},
        compiler_params=params(),
        cost_estimate=cost(36_000_000_000, 4_000_000),
        name="tokens_sum",
    )(places, middle, upstream, settled, passed, *extra)


class LineSum:
    def __init__(self, middle):
        self.middle = middle[0] == 1
        self.line = lax.axis_size("tensor") == 4
        self.pieces, self.joined, self.other, self.results = [], {}, {}, []

    def slot(self, piece, seen):
        number = len(self.pieces)
        shape = None if piece is None else piece.shape
        piece = None if piece is None else piece.reshape(-1, 128)
        self.pieces.append(piece)
        if not self.line:
            if piece is not None:
                total = lax.psum(piece, "tensor")
                self.results.append((total, total))
            return seen
        sent = []
        pairs, operand = [], None
        if piece is not None:
            operand = after(piece, seen)
            pairs += [(0, 1), (3, 2)]
        done = self.pieces[number - 2] if number >= 2 else None
        if done is not None:
            other = after(self.other[number - 2], (seen, self.inward))
            settled = (self.joined[number - 2] + other.astype(f32)).astype(bf16)
            if operand is None:
                operand = settled
            else:
                settled = jnp.pad(settled, ((0, operand.shape[0] - settled.shape[0]), (0, 0)))
                operand = jnp.where(self.middle, settled, operand)
            pairs += [(1, 0), (2, 3)]
        if number >= 1 and self.pieces[number - 1] is not None:
            inward = after(self.inward, seen).astype(f32)
            joined = (self.pieces[number - 1].astype(f32) + inward).astype(bf16)
            self.joined[number - 1] = joined.astype(f32)
            self.other[number - 1] = lax.ppermute(joined, "tensor", [(1, 2), (2, 1)])
            sent.append(joined)
        if operand is not None:
            self.inward = lax.ppermute(operand, "tensor", pairs)
            sent.append(operand)
        if done is not None:
            self.results.append((operand, self.inward))
        return tuple(sent)


def scatter_blocks(blocks, by_rows):
    if is_cube():
        return lax.psum_scatter(blocks, "dp", scatter_dimension=0, tiled=True)[0]
    if by_rows:
        full = blocks.reshape(-1, blocks.shape[2])
        return lax.psum_scatter(full, "dp", scatter_dimension=0, tiled=True)
    full = blocks.transpose(1, 0, 2).reshape(blocks.shape[1], -1)
    return lax.psum_scatter(full, "dp", scatter_dimension=1, tiled=True)


def ring(value, step):
    count = lax.axis_size("dp")
    pairs = [(i, i + step) for i in range(count) if 0 <= i + step < count]
    return lax.ppermute(value, "dp", pairs)


def locate(token_index, lengths, prefix):
    ends = jnp.cumsum(lengths)
    starts = ends - lengths
    inside = (token_index[:, None] >= starts[None, :]) & (token_index[:, None] < ends[None, :])
    begin = jnp.sum(jnp.where(inside, starts[None, :], 0), axis=1)
    limit = jnp.sum(jnp.where(inside, jnp.minimum(prefix, lengths)[None, :], 0), axis=1)
    return begin, limit


def rotary_tables(places):
    lane = jnp.arange(128, dtype=jnp.int32)
    exponents = (lane % (ROT // 2)).astype(f32) * (2.0 / ROT)
    angles = places.astype(f32)[:, None] * jnp.exp(exponents * -math.log(10000.0))[None, :]
    turned = (lane < ROT)[None, :]
    sign = jnp.where(lane < ROT // 2, -1.0, 1.0)[None, :]
    return jnp.where(turned, jnp.cos(angles), 1.0), jnp.where(turned, jnp.sin(angles) * sign, 0.0)


def on_device(
    tokens,
    project_weight,
    project_bias,
    dense_weight,
    dense_bias,
    expand_weight,
    expand_bias,
    shrink_weight,
    shrink_bias,
    first_gain,
    first_shift,
    second_gain,
    second_shift,
    lengths,
    prefix,
    upstream,
):
    rows, width = tokens.shape
    count = lax.axis_size("dp")
    me = lax.axis_index("dp")
    heads = project_bias.shape[0]
    places = natural_places()
    cube = is_cube()
    line = lax.axis_index("tensor")
    middle = ((line == 1) | (line == 2)).astype(jnp.int32).reshape(1)

    vectors = [first_gain, first_shift, second_gain, second_shift, dense_bias, shrink_bias]
    if cube:
        own = jnp.concatenate([v.reshape(-1).astype(bf16) for v in (*vectors, expand_bias, project_bias)])
        own = jnp.pad(own, (0, -own.size % 2048)).reshape(-1, 128)
        gathered = lax.all_gather(own, "dp", axis=0).reshape(count, -1)
        small = jnp.take(gathered, places, axis=0).astype(f32)
        wide = vectors[0].shape[0]
        rows_of = jnp.stack([small[:, k * wide : (k + 1) * wide].reshape(-1) for k in range(len(vectors))])
        at = len(vectors) * wide
        small = gathered.astype(f32)
        split = at + expand_bias.size
        full_expand_bias = small[:, at:split].reshape((count,) + expand_bias.shape).transpose(1, 0, 2).reshape(1, -1)
        full_project_bias = small[:, split : split + project_bias.size].reshape((count,) + project_bias.shape).transpose(1, 0, 2).reshape(1, -1)
    else:
        gathered = lax.all_gather(jnp.stack(vectors).astype(bf16), "dp", axis=1, tiled=True)
        rows_of = gathered.astype(f32)
        full_expand_bias = lax.all_gather(expand_bias.astype(bf16), "dp", axis=1, tiled=True).astype(f32).reshape(1, -1)
        full_project_bias = lax.all_gather(project_bias.astype(bf16), "dp", axis=1, tiled=True).astype(f32).reshape(1, -1)
    gains = jnp.concatenate([rows_of[:4], jnp.zeros((4, width), f32)], axis=0)
    bias_total = rows_of[4:5] + rows_of[5:6]

    def halved(vector, bit):
        keep = vector.shape[0] // 2
        return vector[:keep] + swap(vector[keep:], bit)

    def vector_parts(sums, grad_bias, expand_bias_sums, project_bias_sums):
        norms = sums[:4].reshape(4, BLOCKS, BLOCK).transpose(1, 0, 2).reshape(BLOCKS, -1)
        bias = grad_bias[0].reshape(BLOCKS, BLOCK)
        per_head = lambda v, like: v.reshape(heads, BLOCKS, like.shape[1]).transpose(1, 0, 2).reshape(BLOCKS, -1)
        heads_part = jnp.concatenate(
            [per_head(expand_bias_sums, expand_bias), per_head(project_bias_sums, project_bias)], axis=1
        )
        heads_part = jnp.take(heads_part, places, axis=0)
        return jnp.concatenate([norms, bias, heads_part], axis=1)

    token_index = me * rows + jnp.arange(rows, dtype=jnp.int32)
    begin, limit = locate(token_index, lengths, prefix)
    base = me * rows - SEQ_MAX
    low = begin - base
    high = jnp.maximum(token_index, begin + limit - 1) - base
    cos, sin = rotary_tables(token_index - begin)

    turned_width, hidden_width = dense_weight.shape[0], shrink_weight.shape[0]
    project_low, dense_low = project_weight.astype(bf16), dense_weight.astype(bf16)
    if cube:
        dense_low = dense_low.reshape(-1, BLOCK, BLOCK).transpose(1, 0, 2).reshape(BLOCK, -1)
        spread_project = Spread(jnp.concatenate([project_low, dense_low], axis=1), True)
        seen_project = spread_project.first()
        seen_project_too = spread_project.second(seen_project, gathered)
    else:
        seen_project = seen_project_too = ()
    spread_expand = Spread(after(expand_weight.astype(bf16), (gathered, seen_project)), True)
    seen_expand = spread_expand.first()
    if cube:
        project_a, project_b = spread_project.join(seen_project_too, spread_expand.weight)
    else:
        dense_full = lax.all_gather(dense_low, "dp", axis=1, tiled=True)
        dense_full = dense_full.reshape(-1, BLOCK, BLOCKS, BLOCK).transpose(2, 1, 0, 3).reshape(width, -1)
        both = jnp.concatenate([lax.all_gather(project_low, "dp", axis=0, tiled=True), dense_full], axis=1)
        project_a, project_b = both[: width // 2], both[width // 2 :]
    tok, one_a, one_b, two_a, two_b, up_a, up_b, mean, inverse, grad_bias = norm(
        places, tokens, upstream, after(gains, project_a)
    )
    seen_expand_too = spread_expand.second(seen_expand, project_a)
    queries, pairs = project(after(one_a, seen_expand), one_b, project_a, project_b, full_project_bias, cos, sin)
    sent = after(pairs, seen_expand_too)
    left = ring(sent, 1)
    right = ring(sent[:PREFIX_MAX], -1)
    spread_expand.begin_parts(seen_expand_too)
    expand_mine, expand_theirs = spread_expand.parts(pairs)
    spread_down = Spread(after(shrink_weight.astype(bf16), (mean, seen_project)), False)
    active, slope = expand(after(two_a, sent), two_b, expand_mine + expand_theirs, full_expand_bias)
    grad_attended = dense_back(after(up_a, active), up_b, project_a, project_b, turned_width)
    blocks = [spread_down.pair(0, active)] if cube else []
    spread_down.weight = after(spread_down.weight, (left, grad_attended))
    seen_down = spread_down.first()
    if not cube:
        blocks = [spread_down.pair(0)]
    attended, lse = attend(after(queries, grad_attended), left, pairs, right, low, high)
    seen_down_too = spread_down.second(seen_down, attended)
    blocks += [spread_down.pair(place, (attended, seen_down)) for place in range(len(blocks), HALF - 1)]
    dq, dleft, down, dright = attend_back(
        queries, left, pairs, right, low, high, lse, attended, grad_attended, cos, sin
    )
    later = ring(dleft, -1)
    earlier = ring(dright, 1)
    blocks.append(spread_down.pair(3, (dq, seen_down_too)))

    line = LineSum(middle)
    branch = lambda place, *seen: branch_piece(after(attended, seen), active, project_a, project_b, blocks[place], place)
    pieces = [branch(0, dq, seen_down_too)]
    seen = line.slot(pieces[0], ())
    depth = turned_width + hidden_width
    pieces.append(branch(1, pieces[0], seen))
    column_blocks = column_grad(places, after(attended, pieces[1]), up_a, up_b, depth)
    seen = line.slot(pieces[1], column_blocks)
    column_blocks = column_grad(places, after(active, seen), up_a, up_b, depth, turned_width, column_blocks)
    pieces.append(branch(2, column_blocks))
    seen = line.slot(pieces[2], pieces[2])
    column_blocks, later, earlier, last = lax.optimization_barrier((column_blocks, later, earlier, pieces[2]))
    grad_down = scatter_blocks(column_blocks, False)
    down_blocks = [b for b, _ in blocks] + [b for _, b in blocks]
    grad_hidden, expand_bias_sums = back(after(up_a, (last, seen)), up_b, down_blocks, 0, hidden_width, slope)
    pieces.append(branch(3, grad_hidden))
    seen = line.slot(pieces[3], pieces[3])
    grad_second = second_back(after(grad_hidden, (pieces[3], seen)), expand_mine + expand_theirs)
    grad_mixed, project_bias_sums = mix(after(dq, grad_second), down, later, earlier, cos, sin)
    *tails, sums = input_back(
        grad_mixed, project_a, project_b, grad_second, tok, mean, inverse, gains, 0, 1
    )
    seen = line.slot(tails[0], sums)
    second, more_sums = input_back(
        after(grad_mixed, (sums, seen)), project_a, project_b, grad_second, tok, mean, inverse, gains, 1, 1
    )
    widths = grad_hidden.shape[1], grad_mixed.shape[1]
    expanded = row_grad(places, two_a, two_b, after(grad_hidden, second), sum(widths))
    seen = line.slot(second, expanded)
    *more, part = input_back(
        after(grad_mixed, (expanded, seen)), project_a, project_b, grad_second, tok, mean, inverse, gains, 2, 2
    )
    tails += [second, *more]
    sums = sums + more_sums + part
    row_blocks = row_grad(places, one_a, one_b, after(grad_mixed, part), sum(widths), widths[0], expanded)
    seen = line.slot(tails[2], row_blocks)
    vector = part
    if cube:
        vector = after(vector_parts(sums, grad_bias, expand_bias_sums, project_bias_sums), seen)
        vector = halved(halved(halved(vector, CORE), ALONG_Y), ALONG_X)[0]
    row_blocks, grad_down, vector = lax.optimization_barrier((row_blocks, grad_down, vector))
    if cube:
        grad_rows = scatter_blocks(row_blocks, True)
        grad_expand, grad_project = grad_rows[:, : widths[0]].astype(f32), grad_rows[:, widths[0] :].astype(f32)
    else:
        grad_expand = scatter_blocks(row_blocks[:, :, : widths[0]], True).astype(f32)
        grad_project = scatter_blocks(row_blocks[:, :, widths[0] :], True).astype(f32)
    settled, passed = zip(*line.results[:4])
    output = output_sum(places, middle, after(bias_total, (row_blocks, seen)), settled, passed, tokens)
    tail = tails[3]
    if cube:
        norms = vector[: 4 * BLOCK].astype(bf16).reshape(-1, 128)
        tail = jnp.concatenate([tail.reshape(-1, 128), norms, jnp.zeros_like(norms)], axis=0)
    seen = line.slot(tail, output)
    tokens_grad = tokens_sum(places, middle, upstream, *line.results[4], 0, after(up_a, (output, seen)))
    seen = line.slot(None, tokens_grad)
    tokens_grad = tokens_sum(places, middle, upstream, *line.results[5], 1, after(tokens_grad, seen))
    line.slot(None, tokens_grad)
    for number in range(2, 4):
        tokens_grad = tokens_sum(places, middle, upstream, *line.results[4 + number], number, tokens_grad)
    grad_dense, grad_shrink = grad_down[:turned_width].astype(f32), grad_down[turned_width:].astype(f32)

    if cube:
        settled, passed = line.results[7]
        norms = jnp.where(middle[0] == 1, settled[-16:-8], passed[-16:-8]).astype(f32).reshape(4, BLOCK)
        at = 5 * BLOCK
        bias = vector[4 * BLOCK : at]
        expand_bias_grad = vector[at : at + expand_bias.size].reshape(expand_bias.shape)
        project_bias_grad = vector[at + expand_bias.size :].reshape(project_bias.shape)
    else:
        norms = lax.psum(lax.psum_scatter(sums[:4], "dp", scatter_dimension=1, tiled=True), "tensor")
        bias = lax.psum_scatter(grad_bias[0], "dp", scatter_dimension=0, tiled=True)
        split = lambda v: lax.psum_scatter(v.reshape(heads, -1), "dp", scatter_dimension=1, tiled=True)
        expand_bias_grad, project_bias_grad = split(expand_bias_sums), split(project_bias_sums)
    return (
        output,
        tokens_grad,
        grad_project,
        project_bias_grad,
        grad_dense,
        bias,
        grad_expand,
        expand_bias_grad,
        grad_shrink,
        bias,
        norms[0],
        norms[1],
        norms[2],
        norms[3],
    )


def solution(mesh):
    placed = (
        P("dp", None),
        P("dp", "tensor"),
        P("tensor", "dp"),
        P("tensor", "dp"),
        P("dp"),
        P("dp", "tensor"),
        P("tensor", "dp"),
        P("tensor", "dp"),
        P("dp"),
        P("dp"),
        P("dp"),
        P("dp"),
        P("dp"),
        P(),
        P(),
        P("dp", None),
    )
    return jax.shard_map(
        on_device,
        mesh=mesh,
        in_specs=placed,
        out_specs=(
            P("dp", None),
            P("dp", None),
            P("dp", "tensor"),
            P("tensor", "dp"),
            P("tensor", "dp"),
            P("dp"),
            P("dp", "tensor"),
            P("tensor", "dp"),
            P("tensor", "dp"),
            P("dp"),
            P("dp"),
            P("dp"),
            P("dp"),
            P("dp"),
        ),
        check_vma=False,
    )
```

```python
import functools
import math

import jax
import jax.numpy as jnp
from jax import lax
from jax.experimental import pallas as pl
from jax.experimental.pallas import tpu as pltpu
from jax.sharding import PartitionSpec as P

HD = 256
ROT = 64
SEQ_MAX = 1024
PREFIX_MAX = 512
BLOCK = 256
BLOCKS = 8
HALF = 4
EPSILON = 1e-05
MASKED = -1e30
bf16 = jnp.bfloat16
f32 = jnp.float32
NN = (((1,), (0,)), ((), ()))
NT = (((1,), (1,)), ((), ()))
TN = (((0,), (0,)), ((), ()))
VMEM_BYTES = 56 * 2**20


def mul(a, b, dims=NN):
    return lax.dot_general(a, b, dims, preferred_element_type=f32)


def params(**more):
    return pltpu.CompilerParams(vmem_limit_bytes=VMEM_BYTES, **more)


def cost(flops, moved, transcendentals=0):
    return pl.CostEstimate(flops=flops, bytes_accessed=moved, transcendentals=transcendentals)


def whole_spec(array):
    zeros = (0,) * array.ndim
    return pl.BlockSpec(array.shape, lambda *_: zeros)


def swap(value, bit):
    count = lax.axis_size("dp")
    return lax.ppermute(value, "dp", [(i, i ^ bit) for i in range(count)])


CORE, ALONG_X, ALONG_Y = 1, 2, 4


def is_cube():
    return lax.axis_size("dp") == BLOCKS


def natural_places():
    place = jnp.arange(BLOCKS, dtype=jnp.int32)
    if not is_cube():
        return place
    owner = ((place >> 2) & 1) * CORE + ((place >> 1) & 1) * ALONG_Y + (place & 1) * ALONG_X
    return owner ^ lax.axis_index("dp")


class Spread:
    def __init__(self, weight, by_rows):
        self.weight, self.by_rows = weight, by_rows

    def first(self):
        if is_cube():
            self.from_x = swap(self.weight, ALONG_X)
            self.from_y = swap(self.weight, ALONG_Y)
            return self.from_x, self.from_y
        self.full = lax.all_gather(self.weight, "dp", axis=0 if self.by_rows else 1, tiled=True)
        return (self.full,)

    def second(self, *seen):
        if is_cube():
            half = self.weight.shape[0] // 2
            self.over_x = swap(after(self.from_x[:half], seen), ALONG_Y)
            self.over_y = swap(after(self.from_y[half:], seen), ALONG_X)
            return self.over_x, self.over_y
        return (self.full,)

    def join(self, *seen):
        if is_cube():
            parts = [self.weight, self.from_x, self.from_y, self.over_x, self.over_y]
            mine = jnp.concatenate(after(parts, seen), axis=0)
            return mine, swap(mine, CORE)
        half = self.full.shape[0] // 2
        return self.full[:half], self.full[half:]

    def begin_parts(self, *seen):
        if is_cube():
            self.near = [swap(after(part, seen), CORE) for part in (self.weight, self.from_x, self.from_y)]

    def parts(self, *seen):
        if is_cube():
            far = [swap(after(part, seen), CORE) for part in (self.over_x, self.over_y)]
            return [self.weight, self.from_x, self.from_y, self.over_x, self.over_y], self.near + far
        half = self.full.shape[0] // 2
        return [self.full[:half]], [self.full[half:]]

    def pair(self, place, seen=()):
        if is_cube():
            if place == 3:
                mine = jnp.concatenate([self.over_x, self.over_y], axis=0)
            else:
                mine = self.weight if place == 0 else (self.from_x, self.from_y)[place - 1]
            return mine, swap(after(mine, seen), CORE)
        blocks = self.full.reshape(self.full.shape[0], BLOCKS, -1)
        return blocks[:, place], blocks[:, place + HALF]


def after(value, seen):
    return lax.optimization_barrier((value, seen))[0]


def norm_kernel(places, tokens, upstream, gains, tok, one_a, one_b, two_a, two_b, up_a, up_b, mean, inverse, grad_bias):
    values = tokens[...].astype(f32)
    average = jnp.mean(values, axis=1, keepdims=True)
    center = values - average
    scale = lax.rsqrt(jnp.mean(center * center, axis=1, keepdims=True) + EPSILON)
    mean[...] = average
    inverse[...] = scale

    @pl.when(pl.program_id(0) == 0)
    def _():
        grad_bias[...] = jnp.zeros_like(grad_bias)

    for place in range(BLOCKS):
        from_ = pl.ds(pl.multiple_of(places[place] * BLOCK, BLOCK), BLOCK)
        to = pl.ds(place * BLOCK, BLOCK)
        inner = pl.ds(place % HALF * BLOCK, BLOCK)
        first, second, up = (one_a, two_a, up_a) if place < HALF else (one_b, two_b, up_b)
        low = tokens[:, from_]
        tok[:, to] = low
        normed = (low.astype(f32) - average) * scale
        first[:, inner] = (normed * gains[0:1, to] + gains[1:2, to]).astype(bf16)
        second[:, inner] = (normed * gains[2:3, to] + gains[3:4, to]).astype(bf16)
        grad = upstream[:, from_]
        up[:, inner] = grad
        grad_bias[0:1, to] += jnp.sum(grad.astype(f32), axis=0, keepdims=True)


def norm(places, tokens, upstream, gains, tile=256):
    rows, width = tokens.shape
    row = lambda w: pl.BlockSpec((tile, w), lambda i, *_: (i, 0))
    shape = lambda w, kind: jax.ShapeDtypeStruct((rows, w), kind)
    half = width // 2
    return pl.pallas_call(
        norm_kernel,
        grid_spec=pltpu.PrefetchScalarGridSpec(
            num_scalar_prefetch=1,
            grid=(rows // tile,),
            in_specs=[row(width), row(width), whole_spec(gains)],
            out_specs=[row(width)] + [row(half)] * 6 + [row(1), row(1), pl.BlockSpec((8, width), lambda *_: (0, 0))],
        ),
        out_shape=[shape(width, bf16)]
        + [shape(half, bf16)] * 6
        + [shape(1, f32), shape(1, f32), jax.ShapeDtypeStruct((8, width), f32)],
        compiler_params=params(),
        cost_estimate=cost(20 * rows * width, 20 * rows * width),
        name="norm",
    )(places, tokens, upstream, gains)


def turn(part, cos, sin, sign):
    lane = lax.broadcasted_iota(jnp.int32, part.shape, 1)
    partner = jnp.where(lane < ROT // 2, pltpu.roll(part, 128 - ROT // 2, 1), pltpu.roll(part, ROT // 2, 1))
    if sign > 0:
        return part * cos + partner * sin
    return part * cos - partner * sin


def project_kernel(one_a, one_b, w_a, w_b, bias, cos, sin, queries, pairs):
    for part in range(3):
        at = slice(part * HD, (part + 1) * HD)
        mixed = mul(one_a[...], w_a[:, at]) + mul(one_b[...], w_b[:, at]) + bias[:, at]
        if part < 2:
            ref, to = (queries, 0) if part == 0 else (pairs, 0)
            ref[:, to : to + 128] = turn(mixed[:, :128], cos[...], sin[...], 1).astype(bf16)
            ref[:, to + 128 : to + HD] = mixed[:, 128:].astype(bf16)
        else:
            pairs[:, HD:] = mixed.astype(bf16)


def project(one_a, one_b, w_a, w_b, bias, cos, sin):
    rows, half = one_a.shape
    heads = w_a.shape[1] // (3 * HD)
    weight = pl.BlockSpec((half, 3 * HD), lambda h: (0, h))
    return pl.pallas_call(
        project_kernel,
        grid=(heads,),
        in_specs=[
            whole_spec(one_a),
            whole_spec(one_b),
            weight,
            weight,
            pl.BlockSpec((1, 3 * HD), lambda h: (0, h)),
            whole_spec(cos),
            whole_spec(sin),
        ],
        out_specs=[pl.BlockSpec((rows, HD), lambda h: (0, h)), pl.BlockSpec((rows, 2 * HD), lambda h: (0, h))],
        out_shape=[
            jax.ShapeDtypeStruct((rows, heads * HD), bf16),
            jax.ShapeDtypeStruct((rows, heads * 2 * HD), bf16),
        ],
        compiler_params=params(),
        cost_estimate=cost(4 * rows * half * w_a.shape[1], 14_000_000),
        name="project",
    )(one_a, one_b, w_a, w_b, bias, cos, sin)


def lay(parts, joined):
    at = 0
    for part in parts:
        joined[at : at + part.shape[0], :] = part[...]
        at += part.shape[0]


def expand_kernel(two_a, two_b, bias, *refs):
    *parts, active, slope, weight = refs
    lay(parts, weight)
    rows, half = two_a.shape
    for start in range(0, rows, 512):
        at = slice(start, start + 512)
        hidden = mul(two_a[at], weight[:half]) + mul(two_b[at], weight[half:]) + bias[...]
        below = 0.5 + 0.5 * lax.erf(hidden * (0.5**0.5))
        density = jnp.exp(hidden * hidden * -0.5) * (1.0 / math.sqrt(2.0 * math.pi))
        active[at] = (hidden * below).astype(bf16)
        slope[at] = (below + hidden * density).astype(bf16)


def expand(two_a, two_b, parts, bias, tile=512):
    rows, half = two_a.shape
    width = parts[0].shape[1]
    column = lambda r: pl.BlockSpec((r, tile), lambda n: (0, n))
    return pl.pallas_call(
        expand_kernel,
        grid=(width // tile,),
        in_specs=[whole_spec(two_a), whole_spec(two_b), column(1)] + [column(part.shape[0]) for part in parts],
        out_specs=[column(rows), column(rows)],
        out_shape=[jax.ShapeDtypeStruct((rows, width), bf16)] * 2,
        scratch_shapes=[pltpu.VMEM((2 * half, tile), bf16)],
        compiler_params=params(),
        cost_estimate=cost(0, 0),
        name="expand",
    )(two_a, two_b, bias, *parts)


def branch_kernel(attended, active, dense_a, dense_b, mine, theirs, out):
    slabs = BLOCK // 128
    for number, (dense, weight) in enumerate(((dense_a, mine), (dense_b, theirs))):
        full = mul(active[...], weight[...])
        for at in range(0, attended.shape[1], BLOCK):
            full = full + mul(attended[:, at : at + BLOCK], dense[:, at : at + BLOCK])
        full = full.astype(bf16)
        for slab in range(slabs):
            out[number * slabs + slab] = full[:, slab * 128 : (slab + 1) * 128]


def branch_piece(attended, active, w_a, w_b, pair, place, tile=512):
    rows, turned = attended.shape
    slabs = 2 * BLOCK // 128
    row = lambda a: pl.BlockSpec((tile, a.shape[1]), lambda i: (i, 0))
    dense = pl.BlockSpec((BLOCK, turned), lambda i: (place, w_a.shape[1] // turned - 1))
    return pl.pallas_call(
        branch_kernel,
        grid=(rows // tile,),
        in_specs=[row(attended), row(active), dense, dense, whole_spec(pair[0]), whole_spec(pair[1])],
        out_specs=pl.BlockSpec((slabs, tile, 128), lambda i: (0, i, 0)),
        out_shape=jax.ShapeDtypeStruct((slabs, rows, 128), bf16),
        compiler_params=params(),
        cost_estimate=cost(0, 0),
        name="branch",
    )(attended, active, w_a, w_b, *pair)


def dense_kernel(up_a, up_b, w_a, w_b, out, joined):
    for place in range(BLOCKS):
        ref = w_a if place < HALF else w_b
        rows = slice(place % HALF * BLOCK, (place % HALF + 1) * BLOCK)
        for at in range(0, out.shape[1], BLOCK):
            joined[at : at + BLOCK, place * BLOCK : (place + 1) * BLOCK] = ref[rows, at : at + BLOCK]
    half = up_a.shape[1]
    for start in range(0, out.shape[0], 512):
        at = slice(start, start + 512)
        out[at] = (mul(up_a[at], joined[:, :half], NT) + mul(up_b[at], joined[:, half:], NT)).astype(bf16)


def dense_back(up_a, up_b, w_a, w_b, turned):
    rows, half = up_a.shape
    dense = pl.BlockSpec((half, turned), lambda i: (0, w_a.shape[1] // turned - 1))
    return pl.pallas_call(
        dense_kernel,
        grid=(1,),
        in_specs=[whole_spec(up_a), whole_spec(up_b), dense, dense],
        out_specs=pl.BlockSpec((rows, turned), lambda i: (0, 0)),
        out_shape=jax.ShapeDtypeStruct((rows, turned), bf16),
        scratch_shapes=[pltpu.VMEM((turned, 2 * half), bf16)],
        compiler_params=params(),
        cost_estimate=cost(0, 0),
        name="dense_back",
    )(up_a, up_b, w_a, w_b)


def back_kernel(up_a, up_b, blocks, slope, out, sums, joined):
    for place in range(BLOCKS):
        joined[:, place * BLOCK : (place + 1) * BLOCK] = blocks[place][...]
    half = HALF * BLOCK
    total = jnp.zeros((1, out.shape[1]), f32)
    for start in range(0, out.shape[0], 512):
        at = slice(start, start + 512)
        grad = mul(up_a[at], joined[:, :half], NT) + mul(up_b[at], joined[:, half:], NT)
        if slope is not None:
            grad = grad * slope[at].astype(f32)
        grad = grad.astype(bf16)
        out[at] = grad
        if sums is not None:
            total = total + jnp.sum(grad.astype(f32), axis=0, keepdims=True)
    if sums is not None:
        sums[...] = total


def back(up_a, up_b, blocks, start, width, slope=None, tile=512):
    rows, half = up_a.shape
    weight = pl.BlockSpec((tile, BLOCK), lambda n: (n + start // tile, 0))
    column = lambda r: pl.BlockSpec((r, tile), lambda n: (0, n))
    scaled = slope is not None

    def body(a, b, *rest):
        blocks, rest = rest[:BLOCKS], rest[BLOCKS:]
        if scaled:
            s, out, sums, joined = rest
        else:
            (out, joined), s, sums = rest, None, None
        back_kernel(a, b, blocks, s, out, sums, joined)

    out = jax.ShapeDtypeStruct((rows, width), bf16)
    return pl.pallas_call(
        body,
        grid=(width // tile,),
        in_specs=[whole_spec(up_a), whole_spec(up_b)] + [weight] * BLOCKS + [column(rows)] * scaled,
        out_specs=[column(rows), column(1)] if scaled else column(rows),
        out_shape=[out, jax.ShapeDtypeStruct((1, width), f32)] if scaled else out,
        scratch_shapes=[pltpu.VMEM((tile, 2 * half), bf16)],
        compiler_params=params(),
        cost_estimate=cost(4 * rows * half * width, 4 * rows * half + 4 * half * width + 4 * rows * width),
        name="back",
    )(up_a, up_b, *blocks, *([slope] if scaled else []))


def second_kernel(grad, *refs):
    count = len(refs) - 3
    parts, out, weight, arrived = refs[:count], *refs[count:]
    tile = out.shape[1]
    step = pl.program_id(0)
    copies, ends, at = [], [], 0
    for number, part in enumerate(parts):
        to = weight.at[at : at + part.shape[0]]
        copies.append(pltpu.make_async_copy(part, to, arrived.at[number]))
        at += part.shape[0]
        ends.append(at)

    @pl.when(step == 0)
    def _():
        for copy in copies:
            copy.start()

    for number in range(weight.shape[0] // tile):

        @pl.when(step == number)
        def _(number=number):
            before = 0
            for copy, end in zip(copies, ends):
                last_needed_at = before // tile
                if last_needed_at == number:
                    copy.wait()
                before = end

    rows = pl.ds(pl.multiple_of(step * tile, tile), tile)
    out[...] = mul(grad[...], weight[rows], NT).astype(bf16)


def second_back(grad, parts, tile=512):
    rows, width = grad.shape
    depth = sum(part.shape[0] for part in parts)
    return pl.pallas_call(
        second_kernel,
        grid=(depth // tile,),
        in_specs=[whole_spec(grad)] + [pl.BlockSpec(memory_space=pl.ANY)] * len(parts),
        out_specs=pl.BlockSpec((rows, tile), lambda n: (0, n)),
        out_shape=jax.ShapeDtypeStruct((rows, depth), bf16),
        scratch_shapes=[pltpu.VMEM((depth, width), bf16), pltpu.SemaphoreType.DMA((len(parts),))],
        compiler_params=params(),
        cost_estimate=cost(2 * rows * depth * width, 2 * (rows + depth) * width + 2 * rows * depth),
        name="second_back",
    )(grad, *parts)


def row_grad_kernel(where, left_a, left_b, right, *rest):
    out = rest[-1]
    for number, left in enumerate((left_a, left_b)):
        full = mul(left[...], right[...], TN)
        for place in range(HALF):
            out[where[number * HALF + place]] = full[place * BLOCK : (place + 1) * BLOCK].astype(bf16)


def row_grad(where, left_a, left_b, right, total, start=0, into=None, tile=512):
    rows, width = right.shape
    blocks = 2 * HALF
    extra = [] if into is None else [into]
    return pl.pallas_call(
        row_grad_kernel,
        grid_spec=pltpu.PrefetchScalarGridSpec(
            num_scalar_prefetch=1,
            grid=(width // tile,),
            in_specs=[whole_spec(left_a), whole_spec(left_b), pl.BlockSpec((rows, tile), lambda n, *_: (0, n))]
            + [pl.BlockSpec(memory_space=pl.ANY)] * len(extra),
            out_specs=pl.BlockSpec((blocks, BLOCK, tile), lambda n, *_: (0, 0, n + start // tile)),
        ),
        out_shape=jax.ShapeDtypeStruct((blocks, BLOCK, total), bf16),
        input_output_aliases={4: 0} if extra else {},
        compiler_params=params(),
        cost_estimate=cost(0 if extra else 2 * rows * blocks * BLOCK * width, 0),
        name="row_grad",
    )(where, left_a, left_b, right, *extra)


def column_grad_kernel(where, left, right_a, right_b, *rest):
    out = rest[-1]
    for number, right in enumerate((right_a, right_b)):
        full = mul(left[...], right[...], TN)
        for place in range(HALF):
            out[where[number * HALF + place]] = full[:, place * BLOCK : (place + 1) * BLOCK].astype(bf16)


def column_grad(where, left, right_a, right_b, total, start=0, into=None, tile=512):
    rows, width = left.shape
    blocks = 2 * HALF
    extra = [] if into is None else [into]
    return pl.pallas_call(
        column_grad_kernel,
        grid_spec=pltpu.PrefetchScalarGridSpec(
            num_scalar_prefetch=1,
            grid=(width // tile,),
            in_specs=[pl.BlockSpec((rows, tile), lambda n, *_: (0, n)), whole_spec(right_a), whole_spec(right_b)]
            + [pl.BlockSpec(memory_space=pl.ANY)] * len(extra),
            out_specs=pl.BlockSpec((blocks, tile, BLOCK), lambda n, *_: (0, n + start // tile, 0)),
        ),
        out_shape=jax.ShapeDtypeStruct((blocks, total, BLOCK), bf16),
        input_output_aliases={4: 0} if extra else {},
        compiler_params=params(),
        cost_estimate=cost(0, 0),
        name="column_grad",
    )(where, left, right_a, right_b, *extra)


def fill(refs, heads, place):
    for head in range(heads):
        at = 0
        for ref in refs:
            for start in range(0, ref.shape[0], 512):
                rows = slice(start, start + 512)
                place(head, at, ref[rows, 2 * head * HD : (2 * head + 1) * HD], ref[rows, (2 * head + 1) * HD : (2 * head + 2) * HD])
                at += 512


def attend_kernel(first, last, q, left, own, right, low, high, out, lse, keys, values_turned, *, wide):
    step = pl.program_id(0)
    tall = q.shape[0]
    heads = range(keys.shape[0])

    @pl.when(step == 0)
    def _():
        def place(head, at, k, v):
            keys[head, at : at + 512, :] = k
            values_turned[head, :, at : at + 512] = jnp.transpose(v)

        fill((left, own, right), len(heads), place)

    scaled = [q[:, h * HD : (h + 1) * HD] * jnp.asarray(HD**-0.5, bf16) for h in heads]
    low_row = low[...]
    high_row = high[...]

    def block(j, carry):
        rows = pl.ds(pl.multiple_of(j * wide, wide), wide)
        key = j * wide + lax.broadcasted_iota(jnp.int32, (wide, tall), 0)
        seen = (key >= low_row) & (key <= high_row)
        scores = [mul(keys[h, rows, :], scaled[h], NT) for h in heads]
        after_block = []
        for h in heads:
            top, total, acc = carry[h]
            masked = jnp.where(seen, scores[h], MASKED)
            new = jnp.maximum(top, jnp.max(masked, axis=0, keepdims=True))
            weights = jnp.exp(masked - new)
            fade = jnp.exp(top - new)
            total = total * fade + jnp.sum(weights, axis=0, keepdims=True)
            acc = acc * fade + mul(values_turned[h, :, rows], weights.astype(bf16))
            after_block.append((new, total, acc))
        return tuple(after_block)

    start = (jnp.full((1, tall), MASKED, f32), jnp.zeros((1, tall), f32), jnp.zeros((HD, tall), f32))
    done = lax.fori_loop(first[step], last[step] + 1, block, tuple(start for _ in heads))
    for h in heads:
        top, total, acc = done[h]
        out[:, h * HD : (h + 1) * HD] = jnp.transpose(acc / total).astype(bf16)
        lse[h] = top + jnp.log(total)


def key_blocks(low, high, tall, wide):
    return jnp.min(low.reshape(-1, tall), axis=1) // wide, jnp.max(high.reshape(-1, tall), axis=1) // wide


def attend(q, left, own, right, low, high, tall=256, wide=512):
    rows, width = q.shape
    heads = width // HD
    extent = left.shape[0] + rows + right.shape[0]
    row = pl.BlockSpec((1, tall), lambda i, *_: (0, i))
    mine = pl.BlockSpec((tall, width), lambda i, *_: (i, 0))
    return pl.pallas_call(
        functools.partial(attend_kernel, wide=wide),
        grid_spec=pltpu.PrefetchScalarGridSpec(
            num_scalar_prefetch=2,
            grid=(rows // tall,),
            in_specs=[mine, whole_spec(left), whole_spec(own), whole_spec(right), row, row],
            out_specs=[mine, pl.BlockSpec((heads, 1, tall), lambda i, *_: (0, 0, i))],
            scratch_shapes=[pltpu.VMEM((heads, extent, HD), bf16), pltpu.VMEM((heads, HD, extent), bf16)],
        ),
        out_shape=[jax.ShapeDtypeStruct((rows, width), bf16), jax.ShapeDtypeStruct((heads, 1, rows), f32)],
        compiler_params=params(),
        cost_estimate=cost(8_000_000_000, 10_000_000, 3_000_000),
        name="attend",
    )(*key_blocks(low, high, tall, wide), q, left, own, right, low.reshape(1, rows), high.reshape(1, rows))


def attend_back_kernel(
    first, last, q, left, own, right, low, high, lse, attended, grad, cos, sin,
    dq, dleft, down, dright, keys, values, keys_turned, dk, dv, *, wide,
):
    step = pl.program_id(0)
    tall = q.shape[0]
    heads = range(keys.shape[0])

    @pl.when(step == 0)
    def _():
        def place(head, at, k, v):
            keys[head, at : at + 512, :] = k
            values[head, at : at + 512, :] = v
            keys_turned[head, :, at : at + 512] = jnp.transpose(k)

        fill((left, own, right), len(heads), place)
        dk[...] = jnp.zeros_like(dk)
        dv[...] = jnp.zeros_like(dv)

    cut = lambda ref, h: ref[:, h * HD : (h + 1) * HD]
    scaled = [cut(q, h) * jnp.asarray(HD**-0.5, bf16) for h in heads]
    given = [cut(grad, h) for h in heads]
    low_row = low[...]
    high_row = high[...]
    deltas = [
        jnp.sum(jnp.transpose(given[h].astype(f32) * cut(attended, h).astype(f32)), axis=0, keepdims=True) for h in heads
    ]

    def block(j, accs):
        rows = pl.ds(pl.multiple_of(j * wide, wide), wide)
        key = j * wide + lax.broadcasted_iota(jnp.int32, (wide, tall), 0)
        seen = (key >= low_row) & (key <= high_row)
        scores = [mul(keys[h, rows, :], scaled[h], NT) for h in heads]
        grad_probs = [mul(values[h, rows, :], given[h], NT) for h in heads]
        after_block = []
        for h in heads:
            probs = jnp.exp(jnp.where(seen, scores[h] - lse[h], MASKED))
            grad_scores = (probs * (grad_probs[h] - deltas[h])).astype(bf16)
            dv[h, rows, :] += mul(probs.astype(bf16), given[h])
            dk[h, rows, :] += mul(grad_scores, scaled[h])
            after_block.append(accs[h] + mul(keys_turned[h, :, rows], grad_scores))
        return tuple(after_block)

    accs = lax.fori_loop(first[step], last[step] + 1, block, tuple(jnp.zeros((HD, tall), f32) for _ in heads))
    for h in heads:
        full = jnp.transpose(accs[h]) * (HD**-0.5)
        dq[:, h * HD : h * HD + 128] = turn(full[:, :128], cos[...], sin[...], -1).astype(bf16)
        dq[:, h * HD + 128 : (h + 1) * HD] = full[:, 128:].astype(bf16)

    @pl.when(step == pl.num_programs(0) - 1)
    def _():
        for h in heads:
            at = 0
            for ref in (dleft, down, dright):
                count = ref.shape[0]
                ref[:, 2 * h * HD : (2 * h + 1) * HD] = dk[h, at : at + count, :].astype(ref.dtype)
                ref[:, (2 * h + 1) * HD : (2 * h + 2) * HD] = dv[h, at : at + count, :].astype(ref.dtype)
                at += count


def attend_back(q, left, own, right, low, high, lse, attended, grad, cos, sin, tall=256, wide=512):
    rows, width = q.shape
    heads = width // HD
    extent = left.shape[0] + rows + right.shape[0]
    row = pl.BlockSpec((1, tall), lambda i, *_: (0, i))
    mine = pl.BlockSpec((tall, width), lambda i, *_: (i, 0))
    table = pl.BlockSpec((tall, 128), lambda i, *_: (i, 0))
    return pl.pallas_call(
        functools.partial(attend_back_kernel, wide=wide),
        grid_spec=pltpu.PrefetchScalarGridSpec(
            num_scalar_prefetch=2,
            grid=(rows // tall,),
            in_specs=[
                mine, whole_spec(left), whole_spec(own), whole_spec(right), row, row,
                pl.BlockSpec((heads, 1, tall), lambda i, *_: (0, 0, i)), mine, mine, table, table,
            ],
            out_specs=[mine, whole_spec(left), whole_spec(own), whole_spec(right)],
            scratch_shapes=[
                pltpu.VMEM((heads, extent, HD), bf16),
                pltpu.VMEM((heads, extent, HD), bf16),
                pltpu.VMEM((heads, HD, extent), bf16),
                pltpu.VMEM((heads, extent, HD), f32),
                pltpu.VMEM((heads, extent, HD), f32),
            ],
        ),
        out_shape=[
            jax.ShapeDtypeStruct((rows, width), bf16),
            jax.ShapeDtypeStruct(left.shape, bf16),
            jax.ShapeDtypeStruct(own.shape, bf16),
            jax.ShapeDtypeStruct(right.shape, bf16),
        ],
        compiler_params=params(),
        cost_estimate=cost(16_000_000_000, 20_000_000, 3_000_000),
        name="attend_back",
    )(*key_blocks(low, high, tall, wide), q, left, own, right, low.reshape(1, rows), high.reshape(1, rows), lse, attended, grad, cos, sin)


def mixed_kernel(dq, own, later, earlier, cos, sin, out, sums):
    rows = dq.shape[0]
    near = earlier.shape[0]
    out[:, :HD] = dq[...]
    pairs = own[...].astype(f32) + later[...].astype(f32)
    top = pairs[:near] + earlier[...].astype(f32)
    for at, part in ((slice(0, near), top), (slice(near, rows), pairs[near:])):
        out[at, HD : HD + 128] = turn(part[:, :128], cos[at], sin[at], -1).astype(bf16)
        out[at, HD + 128 :] = part[:, 128:].astype(bf16)
    sums[...] = jnp.sum(out[...].astype(f32), axis=0, keepdims=True)


def mix(dq, own, later, earlier, cos, sin):
    rows, width = dq.shape
    heads = width // HD
    pair = lambda a: pl.BlockSpec((a.shape[0], 2 * HD), lambda h: (0, h))
    return pl.pallas_call(
        mixed_kernel,
        grid=(heads,),
        in_specs=[
            pl.BlockSpec((rows, HD), lambda h: (0, h)), pair(own), pair(later), pair(earlier),
            whole_spec(cos), whole_spec(sin),
        ],
        out_specs=[pl.BlockSpec((rows, 3 * HD), lambda h: (0, h)), pl.BlockSpec((1, 3 * HD), lambda h: (0, h))],
        out_shape=[
            jax.ShapeDtypeStruct((rows, 3 * width), bf16),
            jax.ShapeDtypeStruct((1, 3 * width), f32),
        ],
        compiler_params=params(),
        cost_estimate=cost(10_000_000, 14_000_000),
        name="mix",
    )(dq, own, later, earlier, cos, sin)


def input_kernel(mixed, w_a, w_b, second, tok, mean, inverse, gains, *outs):
    *outs, sums = outs
    step = pl.program_id(0)
    half = w_a.shape[0]
    grad_a = mul(mixed[...], w_a[...], NT)
    grad_b = mul(mixed[...], w_b[...], NT)
    scale = inverse[...]

    @pl.when(step == 0)
    def _():
        sums[...] = jnp.zeros_like(sums)

    pieces = []
    total = 0.0
    product = 0.0
    for number, grad in enumerate((grad_a, grad_b)):
        at = slice(number * half, (number + 1) * half)
        normed = (tok[:, at].astype(f32) - mean[...]) * scale
        other = second[:, at].astype(f32)
        both = grad * gains[0:1, at] + other * gains[2:3, at]
        sums[0:1, at] += jnp.sum(grad * normed, axis=0, keepdims=True)
        sums[1:2, at] += jnp.sum(grad, axis=0, keepdims=True)
        sums[2:3, at] += jnp.sum(other * normed, axis=0, keepdims=True)
        sums[3:4, at] += jnp.sum(other, axis=0, keepdims=True)
        total = total + jnp.sum(both, axis=1, keepdims=True)
        product = product + jnp.sum(both * normed, axis=1, keepdims=True)
        pieces.append((at, both, normed))
    total = total * (0.5 / half)
    product = product * (0.5 / half)

    def store(ref):
        for at, both, normed in pieces:
            grad = (scale * (both - total - normed * product)).astype(bf16)
            for slab in range(half // 128):
                ref[at.start // 128 + slab] = grad[:, slab * 128 : (slab + 1) * 128]

    if len(outs) == 1:
        store(outs[0])
    else:
        for number, ref in enumerate(outs):
            pl.when(step == number)(functools.partial(store, ref))


def input_back(mixed, w_a, w_b, second, tok, mean, inverse, gains, start, count, tile=256):
    width = tok.shape[1]
    depth = mixed.shape[1]
    row = lambda w: pl.BlockSpec((tile, w), lambda i: (i + start, 0))
    weight = pl.BlockSpec((w_a.shape[0], depth), lambda i: (0, 0))
    slabs = (width // 128, tile, 128)
    out = pl.BlockSpec(slabs, lambda i: (0, 0, 0))
    return pl.pallas_call(
        input_kernel,
        grid=(count,),
        in_specs=[
            row(depth), weight, weight, row(width), row(width), row(1), row(1), whole_spec(gains),
        ],
        out_specs=[out] * count + [pl.BlockSpec((8, width), lambda i: (0, 0))],
        out_shape=[jax.ShapeDtypeStruct(slabs, bf16)] * count + [jax.ShapeDtypeStruct((8, width), f32)],
        compiler_params=params(),
        cost_estimate=cost(0, 0) if count == 2 else cost(2 * count * tile * depth * width, 14_000_000),
        name="input_back",
    )(mixed, w_a, w_b, second, tok, mean, inverse, gains)


def output_kernel(places, middle, tokens, bias, *refs):
    out = refs[-1]
    inside = middle[0] == 1
    for place in range(BLOCKS):
        settled, passed = refs[place % HALF], refs[HALF + place % HALF]
        for slab in range(BLOCK // 128):
            to = pl.ds(pl.multiple_of(places[place] * BLOCK + slab * 128, 128), 128)
            at = place // HALF * (BLOCK // 128) + slab
            total = jnp.where(inside, settled[at].astype(f32), passed[at].astype(f32))
            here = bias[0:1, place * BLOCK + slab * 128 : place * BLOCK + slab * 128 + 128]
            out[:, to] = (tokens[:, to].astype(f32) + total + here).astype(bf16)


def output_sum(places, middle, bias, settled, passed, tokens, tile=256):
    rows, width = tokens.shape
    row = lambda w: pl.BlockSpec((tile, w), lambda i, *_: (i, 0))
    slabs = pl.BlockSpec((width // 512, tile, 128), lambda i, *_: (0, i, 0))
    view = lambda a: a.reshape(width // 512, rows, 128)
    return pl.pallas_call(
        output_kernel,
        grid_spec=pltpu.PrefetchScalarGridSpec(
            num_scalar_prefetch=2,
            grid=(rows // tile,),
            in_specs=[row(width), whole_spec(bias)] + [slabs] * 8,
            out_specs=row(width),
        ),
        out_shape=jax.ShapeDtypeStruct((rows, width), bf16),
        compiler_params=params(),
        cost_estimate=cost(36_000_000_000, 17_000_000),
        name="output_sum",
    )(places, middle, tokens, bias, *map(view, settled), *map(view, passed))


def tokens_kernel(places, middle, upstream, settled, passed, *rest):
    out = rest[-1]
    inside = middle[0] == 1
    tile = out.shape[0]
    for slab in range(out.shape[1] // 128):
        per = BLOCK // 128
        at = slice(slab * tile, (slab + 1) * tile)
        to = pl.ds(pl.multiple_of(places[slab // per] * BLOCK + slab % per * 128, 128), 128)
        total = jnp.where(inside, settled[at].astype(f32), passed[at].astype(f32))
        out[:, to] = (upstream[:, to].astype(f32) + total).astype(bf16)


def tokens_sum(places, middle, upstream, settled, passed, number, earlier, tile=256):
    rows, width = upstream.shape
    row = pl.BlockSpec((tile, width), lambda i, *_: (number, 0))
    slabs = pl.BlockSpec((width // 128 * tile, 128), lambda i, *_: (0, 0))
    extra = [earlier]
    return pl.pallas_call(
        tokens_kernel,
        grid_spec=pltpu.PrefetchScalarGridSpec(
            num_scalar_prefetch=2,
            grid=(1,),
            in_specs=[row, slabs, slabs] + [pl.BlockSpec(memory_space=pl.ANY)] * len(extra),
            out_specs=row,
        ),
        out_shape=jax.ShapeDtypeStruct((rows, width), bf16),
        input_output_aliases={5: 0} if number else {},
        compiler_params=params(),
        cost_estimate=cost(36_000_000_000, 4_000_000),
        name="tokens_sum",
    )(places, middle, upstream, settled, passed, *extra)


class LineSum:
    def __init__(self, middle):
        self.middle = middle[0] == 1
        self.line = lax.axis_size("tensor") == 4
        self.pieces, self.joined, self.other, self.results = [], {}, {}, []

    def slot(self, piece, seen):
        number = len(self.pieces)
        shape = None if piece is None else piece.shape
        piece = None if piece is None else piece.reshape(-1, 128)
        self.pieces.append(piece)
        if not self.line:
            if piece is not None:
                total = lax.psum(piece, "tensor")
                self.results.append((total, total))
            return seen
        sent = []
        pairs, operand = [], None
        if piece is not None:
            operand = after(piece, seen)
            pairs += [(0, 1), (3, 2)]
        done = self.pieces[number - 2] if number >= 2 else None
        if done is not None:
            other = after(self.other[number - 2], (seen, self.inward))
            settled = (self.joined[number - 2] + other.astype(f32)).astype(bf16)
            if operand is None:
                operand = settled
            else:
                settled = jnp.pad(settled, ((0, operand.shape[0] - settled.shape[0]), (0, 0)))
                operand = jnp.where(self.middle, settled, operand)
            pairs += [(1, 0), (2, 3)]
        if number >= 1 and self.pieces[number - 1] is not None:
            inward = after(self.inward, seen).astype(f32)
            joined = (self.pieces[number - 1].astype(f32) + inward).astype(bf16)
            self.joined[number - 1] = joined.astype(f32)
            self.other[number - 1] = lax.ppermute(joined, "tensor", [(1, 2), (2, 1)])
            sent.append(joined)
        if operand is not None:
            self.inward = lax.ppermute(operand, "tensor", pairs)
            sent.append(operand)
        if done is not None:
            self.results.append((operand, self.inward))
        return tuple(sent)


def scatter_blocks(blocks, by_rows):
    if is_cube():
        return lax.psum_scatter(blocks, "dp", scatter_dimension=0, tiled=True)[0]
    if by_rows:
        full = blocks.reshape(-1, blocks.shape[2])
        return lax.psum_scatter(full, "dp", scatter_dimension=0, tiled=True)
    full = blocks.transpose(1, 0, 2).reshape(blocks.shape[1], -1)
    return lax.psum_scatter(full, "dp", scatter_dimension=1, tiled=True)


def ring(value, step):
    count = lax.axis_size("dp")
    pairs = [(i, i + step) for i in range(count) if 0 <= i + step < count]
    return lax.ppermute(value, "dp", pairs)


def locate(token_index, lengths, prefix):
    ends = jnp.cumsum(lengths)
    starts = ends - lengths
    inside = (token_index[:, None] >= starts[None, :]) & (token_index[:, None] < ends[None, :])
    begin = jnp.sum(jnp.where(inside, starts[None, :], 0), axis=1)
    limit = jnp.sum(jnp.where(inside, jnp.minimum(prefix, lengths)[None, :], 0), axis=1)
    return begin, limit


def rotary_tables(places):
    lane = jnp.arange(128, dtype=jnp.int32)
    exponents = (lane % (ROT // 2)).astype(f32) * (2.0 / ROT)
    angles = places.astype(f32)[:, None] * jnp.exp(exponents * -math.log(10000.0))[None, :]
    turned = (lane < ROT)[None, :]
    sign = jnp.where(lane < ROT // 2, -1.0, 1.0)[None, :]
    return jnp.where(turned, jnp.cos(angles), 1.0), jnp.where(turned, jnp.sin(angles) * sign, 0.0)


def on_device(
    tokens,
    project_weight,
    project_bias,
    dense_weight,
    dense_bias,
    expand_weight,
    expand_bias,
    shrink_weight,
    shrink_bias,
    first_gain,
    first_shift,
    second_gain,
    second_shift,
    lengths,
    prefix,
    upstream,
):
    rows, width = tokens.shape
    count = lax.axis_size("dp")
    me = lax.axis_index("dp")
    heads = project_bias.shape[0]
    places = natural_places()
    cube = is_cube()
    line = lax.axis_index("tensor")
    middle = ((line == 1) | (line == 2)).astype(jnp.int32).reshape(1)

    vectors = [first_gain, first_shift, second_gain, second_shift, dense_bias, shrink_bias]
    if cube:
        own = jnp.concatenate([v.reshape(-1).astype(bf16) for v in (*vectors, expand_bias, project_bias)])
        own = jnp.pad(own, (0, -own.size % 2048)).reshape(-1, 128)
        gathered = lax.all_gather(own, "dp", axis=0).reshape(count, -1)
        small = jnp.take(gathered, places, axis=0).astype(f32)
        wide = vectors[0].shape[0]
        rows_of = jnp.stack([small[:, k * wide : (k + 1) * wide].reshape(-1) for k in range(len(vectors))])
        at = len(vectors) * wide
        small = gathered.astype(f32)
        split = at + expand_bias.size
        full_expand_bias = small[:, at:split].reshape((count,) + expand_bias.shape).transpose(1, 0, 2).reshape(1, -1)
        full_project_bias = small[:, split : split + project_bias.size].reshape((count,) + project_bias.shape).transpose(1, 0, 2).reshape(1, -1)
    else:
        gathered = lax.all_gather(jnp.stack(vectors).astype(bf16), "dp", axis=1, tiled=True)
        rows_of = gathered.astype(f32)
        full_expand_bias = lax.all_gather(expand_bias.astype(bf16), "dp", axis=1, tiled=True).astype(f32).reshape(1, -1)
        full_project_bias = lax.all_gather(project_bias.astype(bf16), "dp", axis=1, tiled=True).astype(f32).reshape(1, -1)
    gains = jnp.concatenate([rows_of[:4], jnp.zeros((4, width), f32)], axis=0)
    bias_total = rows_of[4:5] + rows_of[5:6]

    def halved(vector, bit):
        keep = vector.shape[0] // 2
        return vector[:keep] + swap(vector[keep:], bit)

    def vector_parts(sums, grad_bias, expand_bias_sums, project_bias_sums):
        norms = sums[:4].reshape(4, BLOCKS, BLOCK).transpose(1, 0, 2).reshape(BLOCKS, -1)
        bias = grad_bias[0].reshape(BLOCKS, BLOCK)
        per_head = lambda v, like: v.reshape(heads, BLOCKS, like.shape[1]).transpose(1, 0, 2).reshape(BLOCKS, -1)
        heads_part = jnp.concatenate(
            [per_head(expand_bias_sums, expand_bias), per_head(project_bias_sums, project_bias)], axis=1
        )
        heads_part = jnp.take(heads_part, places, axis=0)
        return jnp.concatenate([norms, bias, heads_part], axis=1)

    token_index = me * rows + jnp.arange(rows, dtype=jnp.int32)
    begin, limit = locate(token_index, lengths, prefix)
    base = me * rows - SEQ_MAX
    low = begin - base
    high = jnp.maximum(token_index, begin + limit - 1) - base
    cos, sin = rotary_tables(token_index - begin)

    turned_width, hidden_width = dense_weight.shape[0], shrink_weight.shape[0]
    project_low, dense_low = project_weight.astype(bf16), dense_weight.astype(bf16)
    if cube:
        dense_low = dense_low.reshape(-1, BLOCK, BLOCK).transpose(1, 0, 2).reshape(BLOCK, -1)
        spread_project = Spread(jnp.concatenate([project_low, dense_low], axis=1), True)
        seen_project = spread_project.first()
        seen_project_too = spread_project.second(seen_project, gathered)
    else:
        seen_project = seen_project_too = ()
    spread_expand = Spread(after(expand_weight.astype(bf16), (gathered, seen_project)), True)
    seen_expand = spread_expand.first()
    if cube:
        project_a, project_b = spread_project.join(seen_project_too, spread_expand.weight)
    else:
        dense_full = lax.all_gather(dense_low, "dp", axis=1, tiled=True)
        dense_full = dense_full.reshape(-1, BLOCK, BLOCKS, BLOCK).transpose(2, 1, 0, 3).reshape(width, -1)
        both = jnp.concatenate([lax.all_gather(project_low, "dp", axis=0, tiled=True), dense_full], axis=1)
        project_a, project_b = both[: width // 2], both[width // 2 :]
    tok, one_a, one_b, two_a, two_b, up_a, up_b, mean, inverse, grad_bias = norm(
        places, tokens, upstream, after(gains, project_a)
    )
    seen_expand_too = spread_expand.second(seen_expand, project_a)
    queries, pairs = project(after(one_a, seen_expand), one_b, project_a, project_b, full_project_bias, cos, sin)
    sent = after(pairs, seen_expand_too)
    left = ring(sent, 1)
    right = ring(sent[:PREFIX_MAX], -1)
    spread_expand.begin_parts(seen_expand_too)
    expand_mine, expand_theirs = spread_expand.parts(pairs)
    spread_down = Spread(after(shrink_weight.astype(bf16), (mean, seen_project)), False)
    active, slope = expand(after(two_a, sent), two_b, expand_mine + expand_theirs, full_expand_bias)
    grad_attended = dense_back(after(up_a, active), up_b, project_a, project_b, turned_width)
    blocks = [spread_down.pair(0, active)] if cube else []
    spread_down.weight = after(spread_down.weight, (left, grad_attended))
    seen_down = spread_down.first()
    if not cube:
        blocks = [spread_down.pair(0)]
    attended, lse = attend(after(queries, grad_attended), left, pairs, right, low, high)
    seen_down_too = spread_down.second(seen_down, attended)
    blocks += [spread_down.pair(place, (attended, seen_down)) for place in range(len(blocks), HALF - 1)]
    dq, dleft, down, dright = attend_back(
        queries, left, pairs, right, low, high, lse, attended, grad_attended, cos, sin
    )
    later = ring(dleft, -1)
    earlier = ring(dright, 1)
    blocks.append(spread_down.pair(3, (dq, seen_down_too)))

    line = LineSum(middle)
    branch = lambda place, *seen: branch_piece(after(attended, seen), active, project_a, project_b, blocks[place], place)
    pieces = [branch(0, dq, seen_down_too)]
    seen = line.slot(pieces[0], ())
    depth = turned_width + hidden_width
    pieces.append(branch(1, pieces[0], seen))
    column_blocks = column_grad(places, after(attended, pieces[1]), up_a, up_b, depth)
    seen = line.slot(pieces[1], column_blocks)
    column_blocks = column_grad(places, after(active, seen), up_a, up_b, depth, turned_width, column_blocks)
    pieces.append(branch(2, column_blocks))
    seen = line.slot(pieces[2], pieces[2])
    column_blocks, later, earlier, last = lax.optimization_barrier((column_blocks, later, earlier, pieces[2]))
    grad_down = scatter_blocks(column_blocks, False)
    down_blocks = [b for b, _ in blocks] + [b for _, b in blocks]
    grad_hidden, expand_bias_sums = back(after(up_a, (last, seen)), up_b, down_blocks, 0, hidden_width, slope)
    pieces.append(branch(3, grad_hidden))
    seen = line.slot(pieces[3], pieces[3])
    grad_second = second_back(after(grad_hidden, (pieces[3], seen)), expand_mine + expand_theirs)
    grad_mixed, project_bias_sums = mix(after(dq, grad_second), down, later, earlier, cos, sin)
    *tails, sums = input_back(
        grad_mixed, project_a, project_b, grad_second, tok, mean, inverse, gains, 0, 1
    )
    seen = line.slot(tails[0], sums)
    second, more_sums = input_back(
        after(grad_mixed, (sums, seen)), project_a, project_b, grad_second, tok, mean, inverse, gains, 1, 1
    )
    widths = grad_hidden.shape[1], grad_mixed.shape[1]
    expanded = row_grad(places, two_a, two_b, after(grad_hidden, second), sum(widths))
    seen = line.slot(second, expanded)
    *more, part = input_back(
        after(grad_mixed, (expanded, seen)), project_a, project_b, grad_second, tok, mean, inverse, gains, 2, 2
    )
    tails += [second, *more]
    sums = sums + more_sums + part
    row_blocks = row_grad(places, one_a, one_b, after(grad_mixed, part), sum(widths), widths[0], expanded)
    vector = part
    if cube:
        vector = after(vector_parts(sums, grad_bias, expand_bias_sums, project_bias_sums), part)
        vector = halved(halved(vector, CORE), ALONG_Y)
    seen = line.slot(tails[2], row_blocks)
    if cube:
        vector = halved(after(vector, seen), ALONG_X)[0]
    row_blocks, grad_down, vector = lax.optimization_barrier((row_blocks, grad_down, vector))
    if cube:
        grad_rows = scatter_blocks(row_blocks, True)
        grad_expand, grad_project = grad_rows[:, : widths[0]].astype(f32), grad_rows[:, widths[0] :].astype(f32)
    else:
        grad_expand = scatter_blocks(row_blocks[:, :, : widths[0]], True).astype(f32)
        grad_project = scatter_blocks(row_blocks[:, :, widths[0] :], True).astype(f32)
    settled, passed = zip(*line.results[:4])
    output = output_sum(places, middle, after(bias_total, (row_blocks, seen)), settled, passed, tokens)
    tail = tails[3]
    if cube:
        norms = vector[: 4 * BLOCK].astype(bf16).reshape(-1, 128)
        tail = jnp.concatenate([tail.reshape(-1, 128), norms, jnp.zeros_like(norms)], axis=0)
    seen = line.slot(tail, output)
    tokens_grad = tokens_sum(places, middle, upstream, *line.results[4], 0, after(up_a, (output, seen)))
    seen = line.slot(None, tokens_grad)
    tokens_grad = tokens_sum(places, middle, upstream, *line.results[5], 1, after(tokens_grad, seen))
    line.slot(None, tokens_grad)
    for number in range(2, 4):
        tokens_grad = tokens_sum(places, middle, upstream, *line.results[4 + number], number, tokens_grad)
    grad_dense, grad_shrink = grad_down[:turned_width].astype(f32), grad_down[turned_width:].astype(f32)

    if cube:
        settled, passed = line.results[7]
        norms = jnp.where(middle[0] == 1, settled[-16:-8], passed[-16:-8]).astype(f32).reshape(4, BLOCK)
        at = 5 * BLOCK
        bias = vector[4 * BLOCK : at]
        expand_bias_grad = vector[at : at + expand_bias.size].reshape(expand_bias.shape)
        project_bias_grad = vector[at + expand_bias.size :].reshape(project_bias.shape)
    else:
        norms = lax.psum(lax.psum_scatter(sums[:4], "dp", scatter_dimension=1, tiled=True), "tensor")
        bias = lax.psum_scatter(grad_bias[0], "dp", scatter_dimension=0, tiled=True)
        split = lambda v: lax.psum_scatter(v.reshape(heads, -1), "dp", scatter_dimension=1, tiled=True)
        expand_bias_grad, project_bias_grad = split(expand_bias_sums), split(project_bias_sums)
    return (
        output,
        tokens_grad,
        grad_project,
        project_bias_grad,
        grad_dense,
        bias,
        grad_expand,
        expand_bias_grad,
        grad_shrink,
        bias,
        norms[0],
        norms[1],
        norms[2],
        norms[3],
    )


def solution(mesh):
    placed = (
        P("dp", None),
        P("dp", "tensor"),
        P("tensor", "dp"),
        P("tensor", "dp"),
        P("dp"),
        P("dp", "tensor"),
        P("tensor", "dp"),
        P("tensor", "dp"),
        P("dp"),
        P("dp"),
        P("dp"),
        P("dp"),
        P("dp"),
        P(),
        P(),
        P("dp", None),
    )
    return jax.shard_map(
        on_device,
        mesh=mesh,
        in_specs=placed,
        out_specs=(
            P("dp", None),
            P("dp", None),
            P("dp", "tensor"),
            P("tensor", "dp"),
            P("tensor", "dp"),
            P("dp"),
            P("dp", "tensor"),
            P("tensor", "dp"),
            P("tensor", "dp"),
            P("dp"),
            P("dp"),
            P("dp"),
            P("dp"),
            P("dp"),
        ),
        check_vma=False,
    )
```
